256 devices in a mesh: seq: 32 (over x, z_lo, core), dp: 8 (over z_hi, y).
Axes of the slice: x: 4, y: 4, z: 8 (z_hi: 2, z_lo: 4; z = z_hi * 4 + z_lo), core: 2. Of those that a mesh axis runs over, the one named last changes fastest.
Arguments:
- hidden_in: bfloat16 [8, 32, 256, 1152], P('dp', 'seq'), may hold values from -6 to 6
- qkv_spatial: bfloat16 [8, 32, 256, 3456], P('dp', 'seq'), may hold values from -75 to 75
- qkv_temporal: bfloat16 [8, 32, 256, 3456], P('dp', 'seq'), may hold values from -75 to 75
- grad_out: bfloat16 [8, 32, 256, 1152], P('dp', 'seq'), may hold values from -6 to 6
- grad_temporal: bfloat16 [8, 32, 256, 1152], P('dp', 'seq'), may hold values from -6 to 6
- gate_spatial: bfloat16 [8, 1152], P('dp'), may hold values from 0.5 to 2
- modulation: bfloat16 [8, 2, 1152], P('dp'), may hold values from -2.5 to 2.5
- w_out_spatial: bfloat16 [1152, 1152], P('dp'), may hold values from -0.1875 to 0.1875
- w_qkv_temporal: bfloat16 [1152, 3456], P('dp'), may hold values from -0.1875 to 0.1875
Outputs:
- grad_hidden: bfloat16 [8, 32, 256, 1152], P('dp', 'seq')
- grad_qkv_spatial: bfloat16 [8, 32, 256, 3456], P('dp', 'seq')
- grad_w_out: float32 [1152, 1152], P('dp', 'seq')
- grad_w_qkv: float32 [1152, 3456], P('dp', 'seq')
The draws below stay inside these ranges and needn't reach their ends.
All inputs are finite; a program needn't handle non-finite values.
Results may differ from the reference program's by a relative error of at most 0.03.
Values may be sent and summed in bfloat16 or wider, within the bound.
A program may use at most 128 MiB of HBM per device.

```python
import math
import jax
import jax.numpy as jnp
from jax import lax

D = 1152
HEADS = 16
PATCHES = 256
FR_DEV = 1
FRAMES = 32
CLIPS = 8
N_SEQ = 32


def draw_qkv_spatial(key, part):
    key = jax.random.fold_in(key, 11)
    shape = (CLIPS, FRAMES, PATCHES, 3 * D)
    return jax.random.truncated_normal(key, -4.0, 4.0, shape, jnp.float32).astype(jnp.bfloat16)


def draw_qkv_temporal(key, part):
    key = jax.random.fold_in(key, 23)
    shape = (CLIPS, FRAMES, PATCHES, 3 * D)
    return jax.random.truncated_normal(key, -4.0, 4.0, shape, jnp.float32).astype(jnp.bfloat16)


def with_spikes(values, stream_key, source, target, shards_of, factor):
    def block_of(dim):
        return (jnp.arange(values.shape[dim]) // (values.shape[dim] // shards_of)).reshape((-1,) + (1,) * (values.ndim - 1 - dim))

    one_side = jax.random.permutation(stream_key, shards_of)[block_of(target)]
    other_side = (block_of(target) + shards_of // 2) % shards_of
    return jnp.where((block_of(source) == one_side) | (block_of(source) == other_side), factor * values, values)


def block_levels(own_key, shape, split, least, high):
    gain = 1.0
    for axis_at, parts in split:
        steps = jax.random.uniform(jax.random.fold_in(jax.random.fold_in(own_key, 6), axis_at), (parts,), jnp.float32, least / len(split), high / len(split))
        gain = gain * jnp.repeat(jnp.exp(steps), shape[axis_at] // parts).reshape((-1,) + (1,) * (len(shape) - 1 - axis_at))
    return gain


def centred(rng, dims, deviation, bound, cuts=(), dtype=jnp.bfloat16):
    drawn = deviation * jax.random.normal(rng, dims, jnp.float32)
    if cuts:
        drawn = drawn * block_levels(rng, dims, cuts, -0.22, 0.18)
    return jnp.clip(drawn, -bound, bound).astype(dtype)


def noise_with(own_key, extent, deviation, most, shards, heavy, dtype=jnp.bfloat16):
    result = deviation * jax.random.normal(own_key, extent, jnp.float32)
    if shards:
        result = result * block_levels(own_key, extent, shards, -0.22, 0.18)
    return jnp.clip(with_spikes(result, jax.random.fold_in(own_key, 3), *heavy), -most, most).astype(dtype)


def setup_inputs(seed: int = 0) -> dict:
    key_list = jax.random.split(jax.random.key(seed), 10)
    return {
        "hidden_in": centred(key_list[0], (CLIPS, FRAMES, PATCHES, D), 1.0, 6.0, ((0, 8), (1, 32))),
        "qkv_spatial": draw_qkv_spatial(jax.random.fold_in(key_list[9], 71), 0),
        "qkv_temporal": draw_qkv_temporal(jax.random.fold_in(key_list[9], 71), 0),
        "grad_out": noise_with(key_list[3], (CLIPS, FRAMES, PATCHES, D), 1.0, 6.0, ((0, 8), (1, 32)), (1, 3, 32, 2.75)),
        "grad_temporal": centred(key_list[4], (CLIPS, FRAMES, PATCHES, D), 1.0, 6.0, ((0, 8), (1, 32))),
        "gate_spatial": jnp.clip(jnp.exp(math.log(2.0) - 1.3862944 * jax.random.uniform(key_list[5], (CLIPS, D), jnp.float32) ** block_levels(key_list[5], (CLIPS, D), ((0, 8),), -0.2, 0.2)), 0.5, 2.0).astype(jnp.bfloat16),
        "modulation": centred(key_list[6], (CLIPS, 2, D), 0.5, 2.5, ((0, 8),)),
        "w_out_spatial": centred(key_list[7], (D, D), D ** -0.5, 0.1875, ((0, 8),)),
        "w_qkv_temporal": centred(key_list[8], (D, 3 * D), D ** -0.5, 0.1875, ((0, 8),)),
    }


EPSILON = 1e-06

def head_split(block, head_count):
    return block.reshape(block.shape[:-1] + (head_count, block.shape[-1] // head_count))

def head_merge(block):
    return block.reshape(block.shape[:-2] + (block.shape[-2] * block.shape[-1],))

def subscripts(token_form, letter):
    return token_form.replace('T', letter) + 'hd'

def split_qkv(packed, head_count):
    model_width = packed.shape[-1] // 3
    return (head_split(packed[..., :model_width], head_count), head_split(packed[..., model_width:2 * model_width], head_count), head_split(packed[..., 2 * model_width:], head_count))

def attention_probs(queries, key_heads, token_form, score_scale):
    batch = token_form.replace('T', '')
    spec = subscripts(token_form, 'q') + ',' + subscripts(token_form, 'k') + '->' + batch + 'hqk'
    scores = jnp.einsum(spec, queries.astype(jnp.float32), key_heads.astype(jnp.float32)) * score_scale
    row_top = lax.optimization_barrier(jnp.max(scores, axis=-1, keepdims=True))
    exponent = jnp.exp(scores - row_top)
    return exponent / lax.optimization_barrier(jnp.sum(exponent, axis=-1, keepdims=True))

def attention_forward(packed, token_form, head_count):
    queries, key_heads, values = split_qkv(packed, head_count)
    score_scale = 1.0 / math.sqrt(queries.shape[-1])
    probs_b = attention_probs(queries, key_heads, token_form, score_scale).astype(jnp.bfloat16)
    batch = token_form.replace('T', '')
    spec = batch + 'hqk,' + subscripts(token_form, 'k') + '->' + subscripts(token_form, 'q')
    merged = jnp.einsum(spec, probs_b.astype(jnp.float32), values.astype(jnp.float32))
    return head_merge(merged).astype(jnp.bfloat16)

def attention_backward(packed, grad_in, token_form, head_count):
    queries, key_heads, values = split_qkv(packed, head_count)
    score_scale = 1.0 / math.sqrt(queries.shape[-1])
    probs = attention_probs(queries, key_heads, token_form, score_scale)
    probs_b = probs.astype(jnp.bfloat16).astype(jnp.float32)
    grad_heads = head_split(grad_in, head_count).astype(jnp.float32)
    batch = token_form.replace('T', '')
    q_form = subscripts(token_form, 'q')
    k_form = subscripts(token_form, 'k')
    grad_values = jnp.einsum(batch + 'hqk,' + q_form + '->' + k_form, probs_b, grad_heads).astype(jnp.bfloat16)
    grad_probs = jnp.einsum(q_form + ',' + k_form + '->' + batch + 'hqk', grad_heads, values.astype(jnp.float32))
    row_delta = lax.optimization_barrier(jnp.sum(grad_probs * probs, axis=-1, keepdims=True))
    grad_scores = (probs * (grad_probs - row_delta) * score_scale).astype(jnp.bfloat16).astype(jnp.float32)
    grad_queries = jnp.einsum(batch + 'hqk,' + k_form + '->' + q_form, grad_scores, key_heads.astype(jnp.float32)).astype(jnp.bfloat16)
    grad_keys = jnp.einsum(batch + 'hqk,' + q_form + '->' + k_form, grad_scores, queries.astype(jnp.float32)).astype(jnp.bfloat16)
    return jnp.concatenate([head_merge(grad_queries), head_merge(grad_keys), head_merge(grad_values)], axis=-1)

def reference(hidden_in, qkv_spatial, qkv_temporal, grad_out, grad_temporal, gate_spatial, modulation, w_out_spatial, w_qkv_temporal):
    frame_rows = qkv_spatial.reshape(CLIPS * FRAMES, PATCHES, 3 * D)
    attended = lax.map(lambda block: attention_forward(block, 'T', HEADS), frame_rows)
    attended_flat = attended.reshape(CLIPS * FRAMES * PATCHES, D)
    projected = jnp.dot(attended_flat, w_out_spatial, preferred_element_type=jnp.float32).reshape(CLIPS, FRAMES, PATCHES, D)
    gate_full = gate_spatial.astype(jnp.float32)[:, None, None, :]
    residual = hidden_in.astype(jnp.float32) + gate_full * projected
    centered = residual - lax.optimization_barrier(jnp.mean(residual, axis=-1, keepdims=True))
    inv_std = lax.rsqrt(lax.optimization_barrier(jnp.mean(centered * centered, axis=-1, keepdims=True)) + EPSILON)
    unit = centered * inv_std
    shift_row = modulation[:, 0].astype(jnp.float32)[:, None, None, :]
    scale_row = modulation[:, 1].astype(jnp.float32)[:, None, None, :]
    normed = (unit * (1.0 + scale_row) + shift_row).astype(jnp.bfloat16)
    grad_qkv_t = lax.map(lambda pair: attention_backward(pair[0], pair[1], 'Tp', HEADS), (qkv_temporal, grad_temporal))
    grad_normed = jnp.dot(grad_qkv_t.reshape(-1, 3 * D), w_qkv_temporal.T, preferred_element_type=jnp.float32)
    grad_normed = grad_normed.astype(jnp.bfloat16).reshape(CLIPS, FRAMES, PATCHES, D)
    grad_hat = grad_normed.astype(jnp.float32) * (1.0 + scale_row)
    grad_resid = grad_out.astype(jnp.float32) + inv_std * (grad_hat - lax.optimization_barrier(jnp.mean(grad_hat, axis=-1, keepdims=True)) - unit * lax.optimization_barrier(jnp.mean(grad_hat * unit, axis=-1, keepdims=True)))
    grad_proj = (gate_full * grad_resid).astype(jnp.bfloat16)
    grad_attended = jnp.dot(grad_proj.reshape(-1, D), w_out_spatial.T, preferred_element_type=jnp.float32)
    grad_attended = grad_attended.astype(jnp.bfloat16).reshape(CLIPS * FRAMES, PATCHES, D)
    grad_qkv_s = lax.map(lambda pair: attention_backward(pair[0], pair[1], 'T', HEADS), (frame_rows, grad_attended))
    grad_qkv_s = grad_qkv_s.reshape(CLIPS, FRAMES, PATCHES, 3 * D)
    grad_scale = 1.0 / math.sqrt(CLIPS * FRAMES * PATCHES)
    block_rows = FR_DEV * PATCHES
    pieces = (attended.reshape(CLIPS * N_SEQ, block_rows, D), grad_proj.reshape(CLIPS * N_SEQ, block_rows, D), normed.reshape(CLIPS * N_SEQ, block_rows, D), grad_qkv_t.reshape(CLIPS * N_SEQ, block_rows, 3 * D))
    contract_rows = (((0,), (0,)), ((), ()))

    def accumulate(carry, piece):
        first = lax.dot_general(piece[0], piece[1], contract_rows, preferred_element_type=jnp.float32) * grad_scale
        second = lax.dot_general(piece[2], piece[3], contract_rows, preferred_element_type=jnp.float32) * grad_scale
        first = lax.optimization_barrier(first.astype(jnp.bfloat16)).astype(jnp.float32)
        second = lax.optimization_barrier(second.astype(jnp.bfloat16)).astype(jnp.float32)
        return ((carry[0] + first, carry[1] + second), None)
    start_sums = (jnp.zeros((D, D), jnp.float32), jnp.zeros((D, 3 * D), jnp.float32))
    sums, unused = lax.scan(accumulate, start_sums, pieces)
    return (grad_resid.astype(jnp.bfloat16), grad_qkv_s, sums[0], sums[1])
```

```python
import functools
import math

import jax
import jax.numpy as jnp
from jax import lax
from jax.experimental import pallas as pl
from jax.experimental.pallas import tpu as pltpu
from jax.sharding import PartitionSpec as P

HEADS = 16
D = 1152
SEQ = 32
DP = 8
EPSILON = 1e-06
VMEM_LIMIT = 56 * 1024 * 1024
BF = jnp.bfloat16
F32 = jnp.float32


def head_split(block, head_count):
    return block.reshape(block.shape[:-1] + (head_count, block.shape[-1] // head_count))


def head_merge(block):
    return block.reshape(block.shape[:-2] + (block.shape[-2] * block.shape[-1],))


def subscripts(token_form, letter):
    return token_form.replace("T", letter) + "hd"


def split_qkv(packed, head_count):
    model_width = packed.shape[-1] // 3
    return (
        head_split(packed[..., :model_width], head_count),
        head_split(packed[..., model_width : 2 * model_width], head_count),
        head_split(packed[..., 2 * model_width :], head_count),
    )


def attention_probs(queries, key_heads, token_form, score_scale):
    batch = token_form.replace("T", "")
    spec = subscripts(token_form, "q") + "," + subscripts(token_form, "k") + "->" + batch + "hqk"
    scores = jnp.einsum(spec, queries, key_heads, preferred_element_type=jnp.float32) * score_scale
    row_top = jnp.max(scores, axis=-1, keepdims=True)
    exponent = jnp.exp(scores - row_top)
    return exponent / jnp.sum(exponent, axis=-1, keepdims=True)


def attention_forward(packed, token_form, head_count):
    queries, key_heads, values = split_qkv(packed, head_count)
    score_scale = 1.0 / math.sqrt(queries.shape[-1])
    probs_b = attention_probs(queries, key_heads, token_form, score_scale).astype(jnp.bfloat16)
    batch = token_form.replace("T", "")
    spec = batch + "hqk," + subscripts(token_form, "k") + "->" + subscripts(token_form, "q")
    merged = jnp.einsum(spec, probs_b, values, preferred_element_type=jnp.float32)
    return head_merge(merged).astype(jnp.bfloat16)


def attention_backward(packed, grad_in, token_form, head_count):
    queries, key_heads, values = split_qkv(packed, head_count)
    score_scale = 1.0 / math.sqrt(queries.shape[-1])
    probs = attention_probs(queries, key_heads, token_form, score_scale)
    probs_b = probs.astype(jnp.bfloat16)
    grad_heads = head_split(grad_in, head_count)
    batch = token_form.replace("T", "")
    q_form = subscripts(token_form, "q")
    k_form = subscripts(token_form, "k")
    grad_values = jnp.einsum(
        batch + "hqk," + q_form + "->" + k_form,
        probs_b,
        grad_heads,
        preferred_element_type=jnp.float32,
    ).astype(jnp.bfloat16)
    grad_probs = jnp.einsum(
        q_form + "," + k_form + "->" + batch + "hqk",
        grad_heads,
        values,
        preferred_element_type=jnp.float32,
    )
    row_delta = jnp.sum(grad_probs * probs, axis=-1, keepdims=True)
    grad_scores = (probs * (grad_probs - row_delta) * score_scale).astype(jnp.bfloat16)
    grad_queries = jnp.einsum(
        batch + "hqk," + k_form + "->" + q_form,
        grad_scores,
        key_heads,
        preferred_element_type=jnp.float32,
    ).astype(jnp.bfloat16)
    grad_keys = jnp.einsum(
        batch + "hqk," + q_form + "->" + k_form,
        grad_scores,
        queries,
        preferred_element_type=jnp.float32,
    ).astype(jnp.bfloat16)
    return jnp.concatenate(
        [head_merge(grad_queries), head_merge(grad_keys), head_merge(grad_values)], axis=-1
    )


def position():
    s = lax.axis_index("seq")
    d = lax.axis_index("dp")
    return dict(s=s, d=d, core=s % 2, zlo=(s // 2) % 4, x=s // 8, y=d % 4, zhi=d // 4)


def rcopy(src, dst, ssem, rsem, ps, pd):
    return pltpu.make_async_remote_copy(
        src_ref=src,
        dst_ref=dst,
        send_sem=ssem,
        recv_sem=rsem,
        device_id={"seq": ps, "dp": pd},
        device_id_type=pl.DeviceIdType.MESH,
    )


def greet(ps, pd):
    pl.semaphore_signal(
        pltpu.get_barrier_semaphore(),
        inc=1,
        device_id={"seq": ps, "dp": pd},
        device_id_type=pl.DeviceIdType.MESH,
    )


def a2a_start(p, pairs, ssems, rsems):
    def body(k, carry):
        peer = (p["s"] + k) % SEQ
        for i, (src, dst) in enumerate(pairs):
            rcopy(src.at[peer], dst.at[p["s"]], ssems.at[i], rsems.at[i], peer, p["d"]).start()
        return carry

    lax.fori_loop(1, SEQ, body, 0)


def a2a_wait(p, pairs, ssems, rsems):
    for i, (src, dst) in enumerate(pairs):
        part = pl.ds(0, SEQ - 1)
        rcopy(
            src.at[part], dst.at[part], ssems.at[i], rsems.at[i], (p["s"] + 1) % SEQ, p["d"]
        ).wait()


def greet_seq(p):
    def body(k, carry):
        greet((p["s"] + k) % SEQ, p["d"])
        return carry

    lax.fori_loop(1, SEQ, body, 0)


def gather_kernel(w_ref, qkv_ref, g_ref, wall_ref, qkvm_ref, gm_ref, lsem, asend, arecv, wsend, wrecv):
    p = position()
    s, d, x, y, core, zhi = p["s"], p["d"], p["x"], p["y"], p["core"], p["zhi"]
    own = [
        pltpu.make_async_copy(w_ref, wall_ref.at[d], lsem.at[0]),
        pltpu.make_async_copy(qkv_ref.at[s], qkvm_ref.at[s], lsem.at[1]),
        pltpu.make_async_copy(g_ref.at[s], gm_ref.at[s], lsem.at[2]),
    ]
    for c in own:
        c.start()
    greet_seq(p)
    far = (d + 4) % DP
    greet(s, far)
    y_peers = [zhi * 4 + (y + k) % 4 for k in (1, 2, 3)]
    for peer in y_peers:
        greet(s, peer)
    pl.semaphore_wait(pltpu.get_barrier_semaphore(), SEQ - 1 + 4)
    own[0].wait()

    def piece(dd, xx):
        return wall_ref.at[dd, pl.ds(core * 9, 9), :, pl.ds(pl.multiple_of(xx * D, 128), D)]

    def other_piece(dd, xx):
        return wall_ref.at[dd, pl.ds((1 - core) * 9, 9), :, pl.ds(pl.multiple_of(xx * D, 128), D)]

    sent = []

    def send(dd, xx, sem, ps, pd):
        c = rcopy(piece(dd, xx), piece(dd, xx), wsend.at[sem], wrecv.at[sem], ps, pd)
        c.start()
        sent.append(c)

    def arrived(dd, xx, sem):
        rcopy(piece(dd, xx), piece(dd, xx), wsend.at[sem], wrecv.at[sem], s, far).wait_recv()

    send(d, x, 0, s, far)
    for k in (1, 2, 3):
        send(d, x, k, s, y_peers[k - 1])
    pairs = [(qkv_ref, qkvm_ref), (g_ref, gm_ref)]
    a2a_start(p, pairs, asend, arecv)
    arrived(far, x, 0)
    for k in (1, 2, 3):
        send(far, x, 3 + k, s, y_peers[k - 1])
    sibling = s + 1 - 2 * core
    sources = (
        [far]
        + [zhi * 4 + (y + 4 - k) % 4 for k in (1, 2, 3)]
        + [(1 - zhi) * 4 + (y + 4 - k) % 4 for k in (1, 2, 3)]
    )
    for j, dd in enumerate(sources):
        if j:
            arrived(dd, x, j)
        for k in (1, 2, 3):
            send(dd, x, 7 + j * 3 + k - 1, ((x + k) % 4) * 8 + s % 8, d)
        send(dd, x, 28 + j, sibling, d)
    for j, dd in enumerate(sources):
        for k in (1, 2, 3):
            xx = (x + 4 - k) % 4
            arrived(dd, xx, 7 + j * 3 + k - 1)
            send(dd, xx, 35 + j * 3 + k - 1, sibling, d)
    for j, dd in enumerate(sources):
        for k in (0, 1, 2, 3):
            sem = 28 + j if k == 0 else 35 + j * 3 + k - 1
            ref = other_piece(dd, (x + 4 - k) % 4)
            rcopy(ref, ref, wsend.at[sem], wrecv.at[sem], sibling, d).wait_recv()
    for c in sent:
        c.wait_send()
    a2a_wait(p, pairs, asend, arecv)
    own[1].wait()
    own[2].wait()


def gather_call(w_own, qkv, grad):
    return pl.pallas_call(
        gather_kernel,
        out_shape=(
            jax.ShapeDtypeStruct((DP, 18, 8, 4 * D), BF),
            jax.ShapeDtypeStruct((SEQ, 8, 3 * D), BF),
            jax.ShapeDtypeStruct((SEQ, 8, D), BF),
        ),
        in_specs=[pl.BlockSpec(memory_space=pl.ANY)] * 3,
        out_specs=[pl.BlockSpec(memory_space=pl.ANY)] * 3,
        scratch_shapes=[
            pltpu.SemaphoreType.DMA((3,)),
            pltpu.SemaphoreType.DMA((2,)),
            pltpu.SemaphoreType.DMA((2,)),
            pltpu.SemaphoreType.DMA((56,)),
            pltpu.SemaphoreType.DMA((56,)),
        ],
        compiler_params=pltpu.CompilerParams(collective_id=0, has_side_effects=True),
        name="gather_and_exchange",
    )(w_own, qkv, grad)


def exchange_kernel(a_ref, b_ref, am_ref, bm_ref, lsem, asend, arecv):
    p = position()
    s = p["s"]
    own = [
        pltpu.make_async_copy(a_ref.at[s], am_ref.at[s], lsem.at[0]),
        pltpu.make_async_copy(b_ref.at[s], bm_ref.at[s], lsem.at[1]),
    ]
    for c in own:
        c.start()
    greet_seq(p)
    pl.semaphore_wait(pltpu.get_barrier_semaphore(), SEQ - 1)
    pairs = [(a_ref, am_ref), (b_ref, bm_ref)]
    a2a_start(p, pairs, asend, arecv)
    a2a_wait(p, pairs, asend, arecv)
    for c in own:
        c.wait()


def exchange_call(a, b):
    return pl.pallas_call(
        exchange_kernel,
        out_shape=(jax.ShapeDtypeStruct(a.shape, BF), jax.ShapeDtypeStruct(b.shape, BF)),
        in_specs=[pl.BlockSpec(memory_space=pl.ANY)] * 2,
        out_specs=[pl.BlockSpec(memory_space=pl.ANY)] * 2,
        scratch_shapes=[
            pltpu.SemaphoreType.DMA((2,)),
            pltpu.SemaphoreType.DMA((2,)),
            pltpu.SemaphoreType.DMA((2,)),
        ],
        compiler_params=pltpu.CompilerParams(collective_id=1, has_side_effects=True),
        name="exchange",
    )(a, b)


ROWS = 144
QX, OX = 8 * 128, 3 * 128
CZ = 256


def x_start(xx):
    q = xx * 27 // 4
    return q - xx // 3, xx * 2


def z_start(ss):
    xx = ss // 8
    q0, o0 = x_start(xx)
    q = ss * 27 // 32
    q = q - ss // 31
    o = ss * 9 // 32
    o = jnp.minimum(o, o0 + 1)
    return q - q0, o - o0


def reduce_kernel(
    p_ref,
    out_ref,
    mine,
    from_core,
    from_y,
    xq,
    xo,
    zq,
    zo,
    lsem,
    csend,
    crecv,
    ysend,
    yrecv,
    xsend,
    xrecv,
    zsend,
    zrecv,
):
    p = position()
    s, d, x, y, core, zhi, zlo = p["s"], p["d"], p["x"], p["y"], p["core"], p["zhi"], p["zlo"]
    sibling = s + 1 - 2 * core
    z_me = zhi * 4 + zlo
    order = [(y + k) % 4 for k in (1, 2, 3, 0)]
    loads = []
    for i, r in enumerate(order):
        c = pltpu.make_async_copy(p_ref.at[core * 4 + r], mine.at[r], lsem.at[i])
        c.start()
        loads.append(c)
    for z in range(8):
        for c in range(2):
            ps = x * 8 + (z % 4) * 2 + c
            pd = (z // 4) * 4 + y

            @pl.when(jnp.logical_or(ps != s, pd != d))
            def _():
                greet(ps, pd)

    for k in (1, 2, 3):
        greet(s, zhi * 4 + (y + k) % 4)
        greet(((x + k) % 4) * 8 + s % 8, d)
    pl.semaphore_wait(pltpu.get_barrier_semaphore(), 21)

    sent = []

    def send(src, dst, ssem, rsem, ps, pd):
        c = rcopy(src, dst, ssem, rsem, ps, pd)
        c.start()
        sent.append(c)
        return c

    core_copies = []
    for i, r in enumerate(order):
        core_copies.append(
            send(
                p_ref.at[(1 - core) * 4 + r], from_core.at[r], csend.at[i], crecv.at[i], sibling, d
            )
        )
    for i, r in enumerate(order):
        loads[i].wait()
        core_copies[i].wait_recv()

        @pl.loop(0, 9)
        def _(t):
            cols = pl.ds(pl.multiple_of(t * 512, 512), 512)
            mine[r, :, cols] = (
                mine[r, :, cols].astype(F32) + from_core[r, :, cols].astype(F32)
            ).astype(BF)

        if i < 3:
            send(
                mine.at[r], from_y.at[i], ysend.at[i], yrecv.at[i], s, zhi * 4 + (y + i + 1) % 4
            )
    for i in range(3):
        rcopy(from_y.at[i], from_y.at[i], ysend.at[i], yrecv.at[i], sibling, d).wait_recv()

    @pl.loop(0, 9)
    def _(t):
        cols = pl.ds(pl.multiple_of(t * 512, 512), 512)
        total = mine[y, :, cols].astype(F32)
        for i in range(3):
            total = total + from_y[i, :, cols].astype(F32)
        mine[y, :, cols] = total.astype(BF)

    def share(xx):
        q0, o0 = x_start(xx)
        return (
            pl.ds(pl.multiple_of((q0 + 9) * 128, 128), QX),
            pl.ds(pl.multiple_of(o0 * 128, 128), OX),
        )

    for k in (1, 2, 3):
        xx = (x + k) % 4
        qc, oc = share(xx)
        ps = xx * 8 + s % 8
        send(mine.at[y, :, qc], xq.at[k - 1], xsend.at[k - 1], xrecv.at[k - 1], ps, d)
        send(mine.at[y, :, oc], xo.at[k - 1], xsend.at[k + 2], xrecv.at[k + 2], ps, d)
    for k in range(3):
        rcopy(xq.at[k], xq.at[k], xsend.at[k], xrecv.at[k], sibling, d).wait_recv()
        rcopy(xo.at[k], xo.at[k], xsend.at[k + 3], xrecv.at[k + 3], sibling, d).wait_recv()
    qc, oc = share(x)
    xq[3] = (
        (mine[y, :, qc].astype(F32) + xq[0].astype(F32)) + (xq[1].astype(F32) + xq[2].astype(F32))
    ).astype(BF)
    xo[3] = (
        (mine[y, :, oc].astype(F32) + xo[0].astype(F32)) + (xo[1].astype(F32) + xo[2].astype(F32))
    ).astype(BF)

    def z_copies(z2, c2):
        ss = x * 8 + z2 * 2 + c2
        q, o = z_start(ss)
        i = z2 * 2 + c2
        qs = xq.at[3, :, pl.ds(pl.multiple_of(q * 128, 128), CZ)]
        os = xo.at[3, :, pl.ds(pl.multiple_of(o * 128, 128), CZ)]
        return ss, i, qs, os

    for z2 in range(4):
        for c2 in range(2):
            ss, i, qs, os = z_copies(z2, c2)
            pd = core * 4 + y
            is_me = jnp.logical_and(ss == s, pd == d)

            @pl.when(jnp.logical_not(is_me))
            def _():
                rcopy(qs, zq.at[z_me], zsend.at[i], zrecv.at[z_me], ss, pd).start()
                rcopy(os, zo.at[z_me], zsend.at[i + 8], zrecv.at[z_me + 8], ss, pd).start()

            @pl.when(is_me)
            def _():
                pltpu.make_async_copy(qs, zq.at[z_me], zrecv.at[z_me]).start()
                pltpu.make_async_copy(os, zo.at[z_me], zrecv.at[z_me + 8]).start()

    for z in range(8):
        pltpu.make_async_copy(zq.at[z], zq.at[z], zrecv.at[z]).wait()
        pltpu.make_async_copy(zo.at[z], zo.at[z], zrecv.at[z + 8]).wait()
    total_q = zq[0].astype(F32)
    total_o = zo[0].astype(F32)
    for z in range(1, 8):
        total_q = total_q + zq[z].astype(F32)
        total_o = total_o + zo[z].astype(F32)
    out_ref[:, :CZ] = total_q
    out_ref[:, CZ:] = total_o
    for c in sent:
        c.wait_send()
    for z2 in range(4):
        for c2 in range(2):
            ss, i, qs, os = z_copies(z2, c2)
            pd = core * 4 + y

            @pl.when(jnp.logical_or(ss != s, pd != d))
            def _():
                rcopy(qs, zq.at[z_me], zsend.at[i], zrecv.at[z_me], ss, pd).wait_send()
                rcopy(os, zo.at[z_me], zsend.at[i + 8], zrecv.at[z_me + 8], ss, pd).wait_send()


def reduce_call(partial):
    return pl.pallas_call(
        reduce_kernel,
        out_shape=jax.ShapeDtypeStruct((ROWS, 2 * CZ), F32),
        in_specs=[pl.BlockSpec(memory_space=pl.ANY)],
        out_specs=pl.BlockSpec(memory_space=pltpu.VMEM),
        scratch_shapes=[
            pltpu.VMEM((4, ROWS, 4 * D), BF),
            pltpu.VMEM((4, ROWS, 4 * D), BF),
            pltpu.VMEM((3, ROWS, 4 * D), BF),
            pltpu.VMEM((4, ROWS, QX), BF),
            pltpu.VMEM((4, ROWS, OX), BF),
            pltpu.VMEM((8, ROWS, CZ), BF),
            pltpu.VMEM((8, ROWS, CZ), BF),
            pltpu.SemaphoreType.DMA((4,)),
            pltpu.SemaphoreType.DMA((4,)),
            pltpu.SemaphoreType.DMA((4,)),
            pltpu.SemaphoreType.DMA((3,)),
            pltpu.SemaphoreType.DMA((3,)),
            pltpu.SemaphoreType.DMA((6,)),
            pltpu.SemaphoreType.DMA((6,)),
            pltpu.SemaphoreType.DMA((16,)),
            pltpu.SemaphoreType.DMA((16,)),
        ],
        compiler_params=pltpu.CompilerParams(
            collective_id=2, has_side_effects=True, vmem_limit_bytes=VMEM_LIMIT
        ),
        name="reduce_weight_gradients",
    )(partial)


def per_device(
    hidden_in,
    qkv_spatial,
    qkv_temporal,
    grad_out,
    grad_temporal,
    gate_spatial,
    modulation,
    w_out_spatial,
    w_qkv_temporal,
):
    token_rows = 256
    contract_last = (((1,), (1,)), ((), ()))
    contract_rows = (((0,), (0,)), ((), ()))
    w_own = jnp.concatenate([w_out_spatial, w_qkv_temporal], axis=1).reshape(18, 8, 4 * D)
    w_all, qkv_moved, grad_moved = gather_call(
        w_own, qkv_temporal.reshape(SEQ, 8, 3 * D), grad_temporal.reshape(SEQ, 8, D)
    )
    w_all = w_all.reshape(D, 4 * D)
    w_out_all = w_all[:, :D]
    w_qkv_all = w_all[:, D:]

    frame_rows = qkv_spatial[0]
    attended = attention_forward(frame_rows, "bT", HEADS)
    attended_flat = attended.reshape(token_rows, D)
    projected = jnp.dot(attended_flat, w_out_all, preferred_element_type=F32)
    gate_row = gate_spatial.astype(F32)
    residual = hidden_in.reshape(token_rows, D).astype(F32) + gate_row * projected
    centered = residual - jnp.mean(residual, axis=-1, keepdims=True)
    inv_std = lax.rsqrt(jnp.mean(centered * centered, axis=-1, keepdims=True) + EPSILON)
    unit = centered * inv_std
    shift_row = modulation[:, 0].astype(F32)
    scale_row = modulation[:, 1].astype(F32)
    normed = (unit * (1.0 + scale_row) + shift_row).astype(BF)

    grad_qkv_moved = attention_backward(
        qkv_moved[None], grad_moved[None], "cTp", HEADS
    ).reshape(token_rows, 3 * D)
    grad_normed_moved = lax.dot_general(
        grad_qkv_moved, w_qkv_all, contract_last, preferred_element_type=F32
    ).astype(BF)
    normed_moved, grad_normed = exchange_call(
        normed.reshape(SEQ, 8, D), grad_normed_moved.reshape(SEQ, 8, D)
    )
    grad_normed = grad_normed.reshape(token_rows, D)

    grad_hat = grad_normed.astype(F32) * (1.0 + scale_row)
    grad_resid = grad_out.reshape(token_rows, D).astype(F32) + inv_std * (
        grad_hat
        - jnp.mean(grad_hat, axis=-1, keepdims=True)
        - unit * jnp.mean(grad_hat * unit, axis=-1, keepdims=True)
    )
    grad_proj = (gate_row * grad_resid).astype(BF)
    grad_attended = lax.dot_general(
        grad_proj, w_out_all, contract_last, preferred_element_type=F32
    ).astype(BF)
    grad_qkv_s = attention_backward(
        frame_rows, grad_attended.reshape(1, token_rows, D), "bT", HEADS
    )[None]
    grad_scale = 1.0 / math.sqrt(DP * SEQ * token_rows)
    first = lax.dot_general(attended_flat, grad_proj, contract_rows, preferred_element_type=F32)
    second = lax.dot_general(
        normed_moved.reshape(token_rows, D),
        grad_qkv_moved,
        contract_rows,
        preferred_element_type=F32,
    )
    partial = (jnp.concatenate([first, second], axis=1) * grad_scale).astype(BF)
    sums = reduce_call(partial.reshape(DP, ROWS, 4 * D))
    s = lax.axis_index("seq")
    q_at, o_at = z_start(s)
    q0, o0 = x_start(s // 8)
    grad_w_qkv = lax.dynamic_slice(sums, (0, 108 * s - 128 * (q_at + q0)), (ROWS, 108))
    grad_w_out = lax.dynamic_slice(sums, (0, CZ + 36 * s - 128 * (o_at + o0)), (ROWS, 36))
    return (
        grad_resid.astype(BF).reshape(hidden_in.shape),
        grad_qkv_s,
        grad_w_out,
        grad_w_qkv,
    )


def solution(mesh):
    in_specs = (
        P("dp", "seq", None, None),
        P("dp", "seq", None, None),
        P("dp", "seq", None, None),
        P("dp", "seq", None, None),
        P("dp", "seq", None, None),
        P("dp", None),
        P("dp", None, None),
        P("dp", None),
        P("dp", None),
    )
    out_specs = (
        P("dp", "seq", None, None),
        P("dp", "seq", None, None),
        P("dp", "seq"),
        P("dp", "seq"),
    )
    return jax.shard_map(
        per_device, mesh=mesh, in_specs=in_specs, out_specs=out_specs, check_vma=False
    )
```

```python
import functools
import math

import jax
import jax.numpy as jnp
from jax import lax
from jax.experimental import pallas as pl
from jax.experimental.pallas import tpu as pltpu
from jax.sharding import PartitionSpec as P

HEADS = 16
D = 1152
SEQ = 32
DP = 8
EPSILON = 1e-06
VMEM_LIMIT = 56 * 1024 * 1024
BF = jnp.bfloat16
F32 = jnp.float32


SCALE = 1.0 / math.sqrt(D // HEADS)
LOG2E = math.log2(math.e)


def nt(a, b):
    return lax.dot_general(a, b, (((1,), (1,)), ((), ())), preferred_element_type=F32)


def tn(a, b):
    return lax.dot_general(a, b, (((0,), (0,)), ((), ())), preferred_element_type=F32)


def nn(a, b):
    return jnp.dot(a, b, preferred_element_type=F32)


def window(h):
    chunk = jnp.minimum(h * 9 // 16, 7)
    lane = lax.broadcasted_iota(jnp.int32, (1, 256), 1) + chunk * 128 - h * 72
    keep = jnp.where(jnp.logical_and(lane >= 0, lane < 72), 1.0, 0.0).astype(BF)
    return chunk * 128, keep


def head_probs(q, k, bias):
    s = nt(q, k)
    if bias is not None:
        s = s + bias
    top = jnp.max(s, axis=-1, keepdims=True)
    e = jnp.exp2((s - top) * (SCALE * LOG2E))
    return e * (1.0 / jnp.sum(e, axis=-1, keepdims=True))


def forward_head(load, add, h):
    c, keep = window(h)
    p = head_probs(load(0, c) * keep, load(1, c), None)
    add(0, c, nn(p.astype(BF), load(2, c) * keep))


def backward_head(load, add, h, bias):
    c, keep = window(h)
    q, k, v, g = load(0, c), load(1, c), load(2, c), load(3, c)
    qm, km, gm = q * keep, k * keep, g * keep
    p = head_probs(qm, k, bias)
    pb = p.astype(BF)
    dp = nt(gm, v)
    delta = jnp.sum(dp * p, axis=-1, keepdims=True)
    ds = (p * ((dp - delta) * SCALE)).astype(BF)
    add(2, c, tn(pb, gm))
    add(0, c, nn(ds, km))
    add(1, c, tn(ds, qm))


def columns(j, c):
    return pl.ds(pl.multiple_of(j * D + c, 128), 256)


def adder(ref):
    def add(j, c, value):
        at = columns(j, c)
        ref[:, at] = ref[:, at] + value.astype(BF)

    return add


def flat_loader(qkv_ref, g_ref):
    def load(j, c):
        return qkv_ref[:, columns(j, c)] if j < 3 else g_ref[:, columns(0, c)]

    return load


def block_loader(qkv_ref, g_ref):
    def load(j, c):
        x = qkv_ref[:, :, columns(j, c)] if j < 3 else g_ref[:, :, columns(0, c)]
        return x.reshape(256, 256)

    return load


def spatial_backward_kernel(qkv_ref, g_ref, out_ref):
    out_ref[...] = jnp.zeros_like(out_ref)

    def body(h, carry):
        backward_head(flat_loader(qkv_ref, g_ref), adder(out_ref), h, None)
        return carry

    lax.fori_loop(0, HEADS, body, 0, unroll=4)


def spatial_backward(qkv, grad):
    return pl.pallas_call(
        spatial_backward_kernel,
        out_shape=jax.ShapeDtypeStruct((256, 3 * D), BF),
        in_specs=[pl.BlockSpec(memory_space=pltpu.VMEM)] * 2,
        out_specs=pl.BlockSpec(memory_space=pltpu.VMEM),
        compiler_params=pltpu.CompilerParams(vmem_limit_bytes=VMEM_LIMIT),
        name="spatial_backward",
    )(qkv, grad)


def position():
    s = lax.axis_index("seq")
    d = lax.axis_index("dp")
    return dict(s=s, d=d, core=s % 2, zlo=(s // 2) % 4, x=s // 8, y=d % 4, zhi=d // 4)


def rcopy(src, dst, ssem, rsem, ps, pd):
    return pltpu.make_async_remote_copy(
        src_ref=src,
        dst_ref=dst,
        send_sem=ssem,
        recv_sem=rsem,
        device_id={"seq": ps, "dp": pd},
        device_id_type=pl.DeviceIdType.MESH,
    )


def greet(ps, pd):
    pl.semaphore_signal(
        pltpu.get_barrier_semaphore(),
        inc=1,
        device_id={"seq": ps, "dp": pd},
        device_id_type=pl.DeviceIdType.MESH,
    )


def a2a_start(p, pairs, ssems, rsems):
    def body(k, carry):
        peer = (p["s"] + k) % SEQ
        for i, (src, dst) in enumerate(pairs):
            rcopy(src.at[peer], dst.at[p["s"]], ssems.at[i], rsems.at[i], peer, p["d"]).start()
        return carry

    lax.fori_loop(1, SEQ, body, 0)


def a2a_wait(p, pairs, ssems, rsems):
    for i, (src, dst) in enumerate(pairs):
        part = pl.ds(0, SEQ - 1)
        rcopy(
            src.at[part], dst.at[part], ssems.at[i], rsems.at[i], (p["s"] + 1) % SEQ, p["d"]
        ).wait()


def greet_seq(p):
    def body(k, carry):
        greet((p["s"] + k) % SEQ, p["d"])
        return carry

    lax.fori_loop(1, SEQ, body, 0)


SPLIT = 2048
WA, WB = SPLIT // 4, (4 * D - SPLIT) // 4


def gather_kernel(
    w_ref,
    qkv_ref,
    g_ref,
    spatial_ref,
    wall_ref,
    attended_ref,
    gqkv_ref,
    qkvm_ref,
    gm_ref,
    bias_ref,
    lsem,
    asend,
    arecv,
    wsend,
    wrecv,
):
    p = position()
    s, d, x, y, core, zhi = p["s"], p["d"], p["x"], p["y"], p["core"], p["zhi"]
    own = [
        pltpu.make_async_copy(w_ref, wall_ref.at[d], lsem.at[0]),
        pltpu.make_async_copy(qkv_ref.at[s], qkvm_ref.at[s], lsem.at[1]),
        pltpu.make_async_copy(g_ref.at[s], gm_ref.at[s], lsem.at[2]),
    ]
    for c in own:
        c.start()
    greet_seq(p)
    far = (d + 4) % DP
    greet(s, far)
    y_to = [zhi * 4 + (y + k) % 4 for k in (1, 2, 3)]
    y_from = [zhi * 4 + (y + 4 - k) % 4 for k in (1, 2, 3)]
    y_far = [(1 - zhi) * 4 + (y + 4 - k) % 4 for k in (1, 2, 3)]
    x_to = [((x + k) % 4) * 8 + s % 8 for k in (1, 2, 3)]
    x_from = [(x + 4 - k) % 4 for k in (1, 2, 3)]
    sibling = s + 1 - 2 * core
    for peer in y_to:
        greet(s, peer)
    pl.semaphore_wait(pltpu.get_barrier_semaphore(), SEQ - 1 + 4)

    rows = pl.ds(core * 9, 9)
    other_rows = pl.ds((1 - core) * 9, 9)

    def col_a(xx):
        return pl.ds(pl.multiple_of(xx * WA, 128), WA)

    def col_b(xx):
        return pl.ds(pl.multiple_of(SPLIT + xx * WB, 128), WB)

    all_b = pl.ds(SPLIT, 4 * WB)
    sent = []
    expected = []

    def send(dd, cols, sem, ps, pd, mine=False):
        dst = wall_ref.at[dd, rows, :, cols]
        src = w_ref.at[rows, :, cols] if mine else dst
        c = rcopy(src, dst, wsend.at[sem], wrecv.at[sem], ps, pd)
        c.start()
        sent.append(c)

    def arrived(dd, cols, sem, which=None):
        ref = wall_ref.at[dd, rows if which is None else which, :, cols]
        rcopy(ref, ref, wsend.at[sem], wrecv.at[sem], s, far).wait_recv()

    def hand_on(dd, cols, sem):
        send(dd, cols, sem, sibling, d)
        expected.append((dd, cols, sem))

    send(d, col_b(x), 56, s, far, True)
    send(d, col_a(x), 0, s, far, True)
    for k in range(3):
        send(d, col_a(x), 1 + k, s, y_to[k], True)
    for k in range(3):
        send(d, all_b, 60 + k, s, y_to[k], True)
    pairs = [(qkv_ref, qkvm_ref), (g_ref, gm_ref)]
    a2a_start(p, pairs, asend, arecv)

    arrived(far, col_b(x), 56)
    for k in range(3):
        send(far, col_b(x), 57 + k, x_to[k], d)
    arrived(far, col_a(x), 0)
    for k in range(3):
        send(far, col_a(x), 4 + k, s, y_to[k])
    hand_on(far, col_b(x), 66)

    attended_ref[...] = jnp.zeros_like(attended_ref)

    def spatial(h, carry):
        forward_head(flat_loader(spatial_ref, None), adder(attended_ref), h)
        return carry

    lax.fori_loop(0, HEADS, spatial, 0, unroll=2)

    for k in range(3):
        arrived(far, col_b(x_from[k]), 57 + k)
    for k in range(3):
        send(far, all_b, 63 + k, s, y_to[k])
    for k in range(3):
        hand_on(far, col_b(x_from[k]), 67 + k)
    sources = [far] + y_from + y_far
    for j, dd in enumerate(sources):
        if j:
            arrived(dd, col_a(x), j)
        for k in range(3):
            send(dd, col_a(x), 7 + j * 3 + k, x_to[k], d)
        hand_on(dd, col_a(x), 28 + j)
    for k in range(3):
        arrived(y_from[k], all_b, 60 + k)
        hand_on(y_from[k], all_b, 70 + k)
    for j, dd in enumerate(sources):
        for k in range(3):
            arrived(dd, col_a(x_from[k]), 7 + j * 3 + k)
            hand_on(dd, col_a(x_from[k]), 35 + j * 3 + k)
    for k in range(3):
        arrived(y_far[k], all_b, 63 + k)
        hand_on(y_far[k], all_b, 73 + k)

    at = lax.broadcasted_iota(jnp.int32, (256, 256), 0) % 8
    to = lax.broadcasted_iota(jnp.int32, (256, 256), 1) % 8
    bias_ref[...] = jnp.where(at == to, 0.0, -1e30)
    gqkv_ref[...] = jnp.zeros_like(gqkv_ref)
    a2a_wait(p, pairs, asend, arecv)
    own[1].wait()
    own[2].wait()

    def temporal(h, carry):
        backward_head(block_loader(qkvm_ref, gm_ref), adder(gqkv_ref), h, bias_ref[...])
        return carry

    lax.fori_loop(0, HEADS, temporal, 0, unroll=2)

    for dd, cols, sem in expected:
        arrived(dd, cols, sem, other_rows)
    for c in sent:
        c.wait_send()
    own[0].wait()


def gather_call(w_own, qkv, grad, spatial):
    any_space = pl.BlockSpec(memory_space=pl.ANY)
    vmem = pl.BlockSpec(memory_space=pltpu.VMEM)
    return pl.pallas_call(
        gather_kernel,
        out_shape=(
            jax.ShapeDtypeStruct((DP, 18, 8, 4 * D), BF),
            jax.ShapeDtypeStruct((256, D), BF),
            jax.ShapeDtypeStruct((256, 3 * D), BF),
        ),
        in_specs=[any_space] * 3 + [vmem],
        out_specs=[any_space, vmem, vmem],
        scratch_shapes=[
            pltpu.VMEM((SEQ, 8, 3 * D), BF),
            pltpu.VMEM((SEQ, 8, D), BF),
            pltpu.VMEM((256, 256), F32),
            pltpu.SemaphoreType.DMA((3,)),
            pltpu.SemaphoreType.DMA((2,)),
            pltpu.SemaphoreType.DMA((2,)),
            pltpu.SemaphoreType.DMA((76,)),
            pltpu.SemaphoreType.DMA((76,)),
        ],
        compiler_params=pltpu.CompilerParams(
            collective_id=0, has_side_effects=True, vmem_limit_bytes=VMEM_LIMIT
        ),
        name="gather_and_exchange",
    )(w_own, qkv, grad, spatial)


def exchange_kernel(a_ref, b_ref, am_ref, bm_ref, lsem, asend, arecv):
    p = position()
    s = p["s"]
    own = [
        pltpu.make_async_copy(a_ref.at[s], am_ref.at[s], lsem.at[0]),
        pltpu.make_async_copy(b_ref.at[s], bm_ref.at[s], lsem.at[1]),
    ]
    for c in own:
        c.start()
    greet_seq(p)
    pl.semaphore_wait(pltpu.get_barrier_semaphore(), SEQ - 1)
    pairs = [(a_ref, am_ref), (b_ref, bm_ref)]
    a2a_start(p, pairs, asend, arecv)
    a2a_wait(p, pairs, asend, arecv)
    for c in own:
        c.wait()


def exchange_call(a, b):
    return pl.pallas_call(
        exchange_kernel,
        out_shape=(jax.ShapeDtypeStruct(a.shape, BF), jax.ShapeDtypeStruct(b.shape, BF)),
        in_specs=[pl.BlockSpec(memory_space=pl.ANY)] * 2,
        out_specs=[pl.BlockSpec(memory_space=pl.ANY)] * 2,
        scratch_shapes=[
            pltpu.SemaphoreType.DMA((2,)),
            pltpu.SemaphoreType.DMA((2,)),
            pltpu.SemaphoreType.DMA((2,)),
        ],
        compiler_params=pltpu.CompilerParams(collective_id=1, has_side_effects=True),
        name="exchange",
    )(a, b)


ROWS = 144
QX, OX = 8 * 128, 3 * 128
CZ = 256


def x_start(xx):
    q = xx * 27 // 4
    return q - xx // 3, xx * 2


def z_start(ss):
    xx = ss // 8
    q0, o0 = x_start(xx)
    q = ss * 27 // 32
    q = q - ss // 31
    o = ss * 9 // 32
    o = jnp.minimum(o, o0 + 1)
    return q - q0, o - o0


def reduce_kernel(
    p_ref,
    out_ref,
    mine,
    from_core,
    from_y,
    xq,
    xo,
    zq,
    zo,
    lsem,
    csend,
    crecv,
    ysend,
    yrecv,
    xsend,
    xrecv,
    zsend,
    zrecv,
):
    p = position()
    s, d, x, y, core, zhi, zlo = p["s"], p["d"], p["x"], p["y"], p["core"], p["zhi"], p["zlo"]
    sibling = s + 1 - 2 * core
    z_me = zhi * 4 + zlo
    order = [(y + k) % 4 for k in (1, 2, 3, 0)]
    loads = []
    for i, r in enumerate(order):
        c = pltpu.make_async_copy(p_ref.at[core * 4 + r], mine.at[r], lsem.at[i])
        c.start()
        loads.append(c)
    for z in range(8):
        for c in range(2):
            ps = x * 8 + (z % 4) * 2 + c
            pd = (z // 4) * 4 + y

            @pl.when(jnp.logical_or(ps != s, pd != d))
            def _():
                greet(ps, pd)

    for k in (1, 2, 3):
        greet(s, zhi * 4 + (y + k) % 4)
        greet(((x + k) % 4) * 8 + s % 8, d)
    pl.semaphore_wait(pltpu.get_barrier_semaphore(), 21)

    sent = []

    def send(src, dst, ssem, rsem, ps, pd):
        c = rcopy(src, dst, ssem, rsem, ps, pd)
        c.start()
        sent.append(c)
        return c

    core_copies = []
    for i, r in enumerate(order):
        core_copies.append(
            send(
                p_ref.at[(1 - core) * 4 + r], from_core.at[r], csend.at[i], crecv.at[i], sibling, d
            )
        )
    for i, r in enumerate(order):
        loads[i].wait()
        core_copies[i].wait_recv()

        @pl.loop(0, 9)
        def _(t):
            cols = pl.ds(pl.multiple_of(t * 512, 512), 512)
            mine[r, :, cols] = (
                mine[r, :, cols].astype(F32) + from_core[r, :, cols].astype(F32)
            ).astype(BF)

        if i < 3:
            send(
                mine.at[r], from_y.at[i], ysend.at[i], yrecv.at[i], s, zhi * 4 + (y + i + 1) % 4
            )
    for i in range(3):
        rcopy(from_y.at[i], from_y.at[i], ysend.at[i], yrecv.at[i], sibling, d).wait_recv()

    @pl.loop(0, 9)
    def _(t):
        cols = pl.ds(pl.multiple_of(t * 512, 512), 512)
        total = mine[y, :, cols].astype(F32)
        for i in range(3):
            total = total + from_y[i, :, cols].astype(F32)
        mine[y, :, cols] = total.astype(BF)

    def share(xx):
        q0, o0 = x_start(xx)
        return (
            pl.ds(pl.multiple_of((q0 + 9) * 128, 128), QX),
            pl.ds(pl.multiple_of(o0 * 128, 128), OX),
        )

    for k in (1, 2, 3):
        xx = (x + k) % 4
        qc, oc = share(xx)
        ps = xx * 8 + s % 8
        send(mine.at[y, :, qc], xq.at[k - 1], xsend.at[k - 1], xrecv.at[k - 1], ps, d)
        send(mine.at[y, :, oc], xo.at[k - 1], xsend.at[k + 2], xrecv.at[k + 2], ps, d)
    for k in range(3):
        rcopy(xq.at[k], xq.at[k], xsend.at[k], xrecv.at[k], sibling, d).wait_recv()
        rcopy(xo.at[k], xo.at[k], xsend.at[k + 3], xrecv.at[k + 3], sibling, d).wait_recv()
    qc, oc = share(x)
    xq[3] = (
        (mine[y, :, qc].astype(F32) + xq[0].astype(F32)) + (xq[1].astype(F32) + xq[2].astype(F32))
    ).astype(BF)
    xo[3] = (
        (mine[y, :, oc].astype(F32) + xo[0].astype(F32)) + (xo[1].astype(F32) + xo[2].astype(F32))
    ).astype(BF)

    def z_copies(z2, c2):
        ss = x * 8 + z2 * 2 + c2
        q, o = z_start(ss)
        i = z2 * 2 + c2
        qs = xq.at[3, :, pl.ds(pl.multiple_of(q * 128, 128), CZ)]
        os = xo.at[3, :, pl.ds(pl.multiple_of(o * 128, 128), CZ)]
        return ss, i, qs, os

    for z2 in range(4):
        for c2 in range(2):
            ss, i, qs, os = z_copies(z2, c2)
            pd = core * 4 + y
            is_me = jnp.logical_and(ss == s, pd == d)

            @pl.when(jnp.logical_not(is_me))
            def _():
                rcopy(qs, zq.at[z_me], zsend.at[i], zrecv.at[z_me], ss, pd).start()
                rcopy(os, zo.at[z_me], zsend.at[i + 8], zrecv.at[z_me + 8], ss, pd).start()

            @pl.when(is_me)
            def _():
                pltpu.make_async_copy(qs, zq.at[z_me], zrecv.at[z_me]).start()
                pltpu.make_async_copy(os, zo.at[z_me], zrecv.at[z_me + 8]).start()

    for z in range(8):
        pltpu.make_async_copy(zq.at[z], zq.at[z], zrecv.at[z]).wait()
        pltpu.make_async_copy(zo.at[z], zo.at[z], zrecv.at[z + 8]).wait()
    total_q = zq[0].astype(F32)
    total_o = zo[0].astype(F32)
    for z in range(1, 8):
        total_q = total_q + zq[z].astype(F32)
        total_o = total_o + zo[z].astype(F32)
    out_ref[:, :CZ] = total_q
    out_ref[:, CZ:] = total_o
    for c in sent:
        c.wait_send()
    for z2 in range(4):
        for c2 in range(2):
            ss, i, qs, os = z_copies(z2, c2)
            pd = core * 4 + y

            @pl.when(jnp.logical_or(ss != s, pd != d))
            def _():
                rcopy(qs, zq.at[z_me], zsend.at[i], zrecv.at[z_me], ss, pd).wait_send()
                rcopy(os, zo.at[z_me], zsend.at[i + 8], zrecv.at[z_me + 8], ss, pd).wait_send()


def reduce_call(partial):
    return pl.pallas_call(
        reduce_kernel,
        out_shape=jax.ShapeDtypeStruct((ROWS, 2 * CZ), F32),
        in_specs=[pl.BlockSpec(memory_space=pl.ANY)],
        out_specs=pl.BlockSpec(memory_space=pltpu.VMEM),
        scratch_shapes=[
            pltpu.VMEM((4, ROWS, 4 * D), BF),
            pltpu.VMEM((4, ROWS, 4 * D), BF),
            pltpu.VMEM((3, ROWS, 4 * D), BF),
            pltpu.VMEM((4, ROWS, QX), BF),
            pltpu.VMEM((4, ROWS, OX), BF),
            pltpu.VMEM((8, ROWS, CZ), BF),
            pltpu.VMEM((8, ROWS, CZ), BF),
            pltpu.SemaphoreType.DMA((4,)),
            pltpu.SemaphoreType.DMA((4,)),
            pltpu.SemaphoreType.DMA((4,)),
            pltpu.SemaphoreType.DMA((3,)),
            pltpu.SemaphoreType.DMA((3,)),
            pltpu.SemaphoreType.DMA((6,)),
            pltpu.SemaphoreType.DMA((6,)),
            pltpu.SemaphoreType.DMA((16,)),
            pltpu.SemaphoreType.DMA((16,)),
        ],
        compiler_params=pltpu.CompilerParams(
            collective_id=2, has_side_effects=True, vmem_limit_bytes=VMEM_LIMIT
        ),
        name="reduce_weight_gradients",
    )(partial)


def per_device(
    hidden_in,
    qkv_spatial,
    qkv_temporal,
    grad_out,
    grad_temporal,
    gate_spatial,
    modulation,
    w_out_spatial,
    w_qkv_temporal,
):
    token_rows = 256
    contract_last = (((1,), (1,)), ((), ()))
    contract_rows = (((0,), (0,)), ((), ()))
    w_own = jnp.concatenate([w_out_spatial, w_qkv_temporal], axis=1).reshape(18, 8, 4 * D)
    frame_rows = qkv_spatial.reshape(token_rows, 3 * D)
    w_all, attended_flat, grad_qkv_moved = gather_call(
        w_own,
        qkv_temporal.reshape(SEQ, 8, 3 * D),
        grad_temporal.reshape(SEQ, 8, D),
        frame_rows,
    )
    w_all = w_all.reshape(D, 4 * D)
    w_out_all = w_all[:, :D]
    w_qkv_all = w_all[:, D:]

    projected = jnp.dot(attended_flat, w_out_all, preferred_element_type=F32)
    gate_row = gate_spatial.astype(F32)
    residual = hidden_in.reshape(token_rows, D).astype(F32) + gate_row * projected
    centered = residual - jnp.mean(residual, axis=-1, keepdims=True)
    inv_std = lax.rsqrt(jnp.mean(centered * centered, axis=-1, keepdims=True) + EPSILON)
    unit = centered * inv_std
    shift_row = modulation[:, 0].astype(F32)
    scale_row = modulation[:, 1].astype(F32)
    normed = (unit * (1.0 + scale_row) + shift_row).astype(BF)

    grad_normed_moved = lax.dot_general(
        grad_qkv_moved, w_qkv_all, contract_last, preferred_element_type=F32
    ).astype(BF)
    normed_moved, grad_normed = exchange_call(
        normed.reshape(SEQ, 8, D), grad_normed_moved.reshape(SEQ, 8, D)
    )
    grad_normed = grad_normed.reshape(token_rows, D)

    grad_hat = grad_normed.astype(F32) * (1.0 + scale_row)
    grad_resid = grad_out.reshape(token_rows, D).astype(F32) + inv_std * (
        grad_hat
        - jnp.mean(grad_hat, axis=-1, keepdims=True)
        - unit * jnp.mean(grad_hat * unit, axis=-1, keepdims=True)
    )
    grad_proj = (gate_row * grad_resid).astype(BF)
    grad_attended = lax.dot_general(
        grad_proj, w_out_all, contract_last, preferred_element_type=F32
    ).astype(BF)
    grad_qkv_s = spatial_backward(frame_rows, grad_attended).reshape(qkv_spatial.shape)
    grad_scale = 1.0 / math.sqrt(DP * SEQ * token_rows)
    first = lax.dot_general(attended_flat, grad_proj, contract_rows, preferred_element_type=F32)
    second = lax.dot_general(
        normed_moved.reshape(token_rows, D),
        grad_qkv_moved,
        contract_rows,
        preferred_element_type=F32,
    )
    partial = (jnp.concatenate([first, second], axis=1) * grad_scale).astype(BF)
    sums = reduce_call(partial.reshape(DP, ROWS, 4 * D))
    s = lax.axis_index("seq")
    q_at, o_at = z_start(s)
    q0, o0 = x_start(s // 8)
    grad_w_qkv = lax.dynamic_slice(sums, (0, 108 * s - 128 * (q_at + q0)), (ROWS, 108))
    grad_w_out = lax.dynamic_slice(sums, (0, CZ + 36 * s - 128 * (o_at + o0)), (ROWS, 36))
    return (
        grad_resid.astype(BF).reshape(hidden_in.shape),
        grad_qkv_s,
        grad_w_out,
        grad_w_qkv,
    )


def solution(mesh):
    in_specs = (
        P("dp", "seq", None, None),
        P("dp", "seq", None, None),
        P("dp", "seq", None, None),
        P("dp", "seq", None, None),
        P("dp", "seq", None, None),
        P("dp", None),
        P("dp", None, None),
        P("dp", None),
        P("dp", None),
    )
    out_specs = (
        P("dp", "seq", None, None),
        P("dp", "seq", None, None),
        P("dp", "seq"),
        P("dp", "seq"),
    )
    return jax.shard_map(
        per_device, mesh=mesh, in_specs=in_specs, out_specs=out_specs, check_vma=False
    )
```

```python
import functools
import math

import jax
import jax.numpy as jnp
from jax import lax
from jax.experimental import pallas as pl
from jax.experimental.pallas import tpu as pltpu
from jax.sharding import PartitionSpec as P

HEADS = 16
D = 1152
SEQ = 32
DP = 8
EPSILON = 1e-06
VMEM_LIMIT = 56 * 1024 * 1024
BF = jnp.bfloat16
F32 = jnp.float32


SCALE = 1.0 / math.sqrt(D // HEADS)
LOG2E = math.log2(math.e)


def nt(a, b):
    return lax.dot_general(a, b, (((1,), (1,)), ((), ())), preferred_element_type=F32)


def tn(a, b):
    return lax.dot_general(a, b, (((0,), (0,)), ((), ())), preferred_element_type=F32)


def nn(a, b):
    return jnp.dot(a, b, preferred_element_type=F32)


def window(h):
    chunk = jnp.minimum(h * 9 // 16, 7)
    lane = lax.broadcasted_iota(jnp.int32, (1, 256), 1) + chunk * 128 - h * 72
    keep = jnp.where(jnp.logical_and(lane >= 0, lane < 72), 1.0, 0.0).astype(BF)
    return chunk * 128, keep


def head_probs(q, k, bias):
    s = nt(q, k)
    if bias is not None:
        s = s + bias
    top = jnp.max(s, axis=-1, keepdims=True)
    e = jnp.exp2((s - top) * (SCALE * LOG2E))
    return e * (1.0 / jnp.sum(e, axis=-1, keepdims=True))


def forward_head(load, add, h):
    c, keep = window(h)
    p = head_probs(load(0, c) * keep, load(1, c), None)
    add(0, c, nn(p.astype(BF), load(2, c) * keep))


def backward_head(load, add, h, bias):
    c, keep = window(h)
    q, k, v, g = load(0, c), load(1, c), load(2, c), load(3, c)
    qm, km, gm = q * keep, k * keep, g * keep
    p = head_probs(qm, k, bias)
    pb = p.astype(BF)
    dp = nt(gm, v)
    delta = jnp.sum(dp * p, axis=-1, keepdims=True)
    ds = (p * ((dp - delta) * SCALE)).astype(BF)
    add(2, c, tn(pb, gm))
    add(0, c, nn(ds, km))
    add(1, c, tn(ds, qm))


def columns(j, c):
    return pl.ds(pl.multiple_of(j * D + c, 128), 256)


def adder(ref):
    def add(j, c, value):
        at = columns(j, c)
        ref[:, at] = ref[:, at] + value.astype(BF)

    return add


def flat_loader(qkv_ref, g_ref):
    def load(j, c):
        return qkv_ref[:, columns(j, c)] if j < 3 else g_ref[:, columns(0, c)]

    return load


def block_loader(qkv_ref, g_ref):
    def load(j, c):
        x = qkv_ref[:, :, columns(j, c)] if j < 3 else g_ref[:, :, columns(0, c)]
        return x.reshape(256, 256)

    return load


def position():
    s = lax.axis_index("seq")
    d = lax.axis_index("dp")
    return dict(s=s, d=d, core=s % 2, zlo=(s // 2) % 4, x=s // 8, y=d % 4, zhi=d // 4)


def rcopy(src, dst, ssem, rsem, ps, pd):
    return pltpu.make_async_remote_copy(
        src_ref=src,
        dst_ref=dst,
        send_sem=ssem,
        recv_sem=rsem,
        device_id={"seq": ps, "dp": pd},
        device_id_type=pl.DeviceIdType.MESH,
    )


def greet(ps, pd):
    pl.semaphore_signal(
        pltpu.get_barrier_semaphore(),
        inc=1,
        device_id={"seq": ps, "dp": pd},
        device_id_type=pl.DeviceIdType.MESH,
    )


def a2a_start(p, pairs, ssems, rsems):
    def body(k, carry):
        peer = (p["s"] + k) % SEQ
        for i, (src, dst) in enumerate(pairs):
            rcopy(src.at[peer], dst.at[p["s"]], ssems.at[i], rsems.at[i], peer, p["d"]).start()
        return carry

    lax.fori_loop(1, SEQ, body, 0)


def a2a_wait(p, pairs, ssems, rsems):
    for i, (src, dst) in enumerate(pairs):
        part = pl.ds(0, SEQ - 1)
        rcopy(
            src.at[part], dst.at[part], ssems.at[i], rsems.at[i], (p["s"] + 1) % SEQ, p["d"]
        ).wait()


def greet_seq(p):
    def body(k, carry):
        greet((p["s"] + k) % SEQ, p["d"])
        return carry

    lax.fori_loop(1, SEQ, body, 0)


SPLIT = 2048
WA, WB = SPLIT // 4, (4 * D - SPLIT) // 4


def gather_kernel(
    w_ref,
    qkv_ref,
    g_ref,
    spatial_ref,
    hidden_ref,
    rows_ref,
    attended_ref,
    gqkv_ref,
    wout_ref,
    unit_ref,
    std_ref,
    normedm_ref,
    gn_ref,
    wall_ref,
    qkvm_ref,
    gm_ref,
    bias_ref,
    normed_ref,
    gnt_ref,
    lsem,
    asend,
    arecv,
    wsend,
    wrecv,
):
    p = position()
    s, d, x, y, core, zhi = p["s"], p["d"], p["x"], p["y"], p["core"], p["zhi"]
    own = [
        pltpu.make_async_copy(w_ref, wall_ref.at[d], lsem.at[0]),
        pltpu.make_async_copy(qkv_ref.at[s], qkvm_ref.at[s], lsem.at[1]),
        pltpu.make_async_copy(g_ref.at[s], gm_ref.at[s], lsem.at[2]),
    ]
    for c in own:
        c.start()
    greet_seq(p)
    far = (d + 4) % DP
    greet(s, far)
    y_to = [zhi * 4 + (y + k) % 4 for k in (1, 2, 3)]
    y_from = [zhi * 4 + (y + 4 - k) % 4 for k in (1, 2, 3)]
    y_far = [(1 - zhi) * 4 + (y + 4 - k) % 4 for k in (1, 2, 3)]
    x_to = [((x + k) % 4) * 8 + s % 8 for k in (1, 2, 3)]
    x_from = [(x + 4 - k) % 4 for k in (1, 2, 3)]
    sibling = s + 1 - 2 * core
    for peer in y_to:
        greet(s, peer)
    pl.semaphore_wait(pltpu.get_barrier_semaphore(), SEQ - 1 + 4)

    rows = pl.ds(core * 9, 9)
    other_rows = pl.ds((1 - core) * 9, 9)

    def col_a(xx):
        return pl.ds(pl.multiple_of(xx * WA, 128), WA)

    def col_b(xx):
        return pl.ds(pl.multiple_of(SPLIT + xx * WB, 128), WB)

    all_b = pl.ds(SPLIT, 4 * WB)
    sent = []
    expected = []

    def send(dd, cols, sem, ps, pd, mine=False):
        dst = wall_ref.at[dd, rows, :, cols]
        src = w_ref.at[rows, :, cols] if mine else dst
        c = rcopy(src, dst, wsend.at[sem], wrecv.at[sem], ps, pd)
        c.start()
        sent.append(c)

    def arrived(dd, cols, sem, which=None):
        ref = wall_ref.at[dd, rows if which is None else which, :, cols]
        rcopy(ref, ref, wsend.at[sem], wrecv.at[sem], s, far).wait_recv()

    def hand_on(dd, cols, sem):
        send(dd, cols, sem, sibling, d)
        expected.append((dd, cols, sem))

    send(d, col_b(x), 56, s, far, True)
    send(d, col_a(x), 0, s, far, True)
    for k in range(3):
        send(d, col_a(x), 1 + k, s, y_to[k], True)
    for k in range(3):
        send(d, all_b, 60 + k, s, y_to[k], True)
    pairs = [(qkv_ref, qkvm_ref), (g_ref, gm_ref)]
    a2a_start(p, pairs, asend, arecv)

    arrived(far, col_b(x), 56)
    for k in range(3):
        send(far, col_b(x), 57 + k, x_to[k], d)
    arrived(far, col_a(x), 0)
    for k in range(3):
        send(far, col_a(x), 4 + k, s, y_to[k])
    hand_on(far, col_b(x), 66)

    attended_ref[...] = jnp.zeros_like(attended_ref)

    def spatial(h, carry):
        forward_head(flat_loader(spatial_ref, None), adder(attended_ref), h)
        return carry

    lax.fori_loop(0, HEADS, spatial, 0, unroll=2)

    for k in range(3):
        arrived(far, col_b(x_from[k]), 57 + k)
    for k in range(3):
        send(far, all_b, 63 + k, s, y_to[k])
    for k in range(3):
        hand_on(far, col_b(x_from[k]), 67 + k)
    sources = [far] + y_from + y_far
    for j, dd in enumerate(sources):
        if j:
            arrived(dd, col_a(x), j)
        for k in range(3):
            send(dd, col_a(x), 7 + j * 3 + k, x_to[k], d)
        hand_on(dd, col_a(x), 28 + j)
    for k in range(3):
        arrived(y_from[k], all_b, 60 + k)
        hand_on(y_from[k], all_b, 70 + k)
    for j, dd in enumerate(sources):
        for k in range(3):
            arrived(dd, col_a(x_from[k]), 7 + j * 3 + k)
            hand_on(dd, col_a(x_from[k]), 35 + j * 3 + k)
    for k in range(3):
        arrived(y_far[k], all_b, 63 + k)
        hand_on(y_far[k], all_b, 73 + k)

    at = lax.broadcasted_iota(jnp.int32, (256, 256), 0) % 8
    to = lax.broadcasted_iota(jnp.int32, (256, 256), 1) % 8
    bias_ref[...] = jnp.where(at == to, 0.0, -1e30)
    gqkv_ref[...] = jnp.zeros_like(gqkv_ref)

    own[0].wait()
    for dd, cols, sem in expected:
        if sem < 66:
            arrived(dd, cols, sem, other_rows)

    def assemble(dd, carry):
        at = pl.ds(pl.multiple_of(dd * ROWS, 16), ROWS)
        wout_ref[at, :] = wall_ref[dd, :, :, :D].reshape(ROWS, D)
        return carry

    lax.fori_loop(0, DP, assemble, 0)

    def project(t, carry):
        at = pl.ds(pl.multiple_of(t * 384, 128), 384)
        unit_ref[:, at] = hidden_ref[:, at].astype(F32) + rows_ref[0:1, at] * nn(
            attended_ref[...], wout_ref[:, at]
        )
        return carry

    lax.fori_loop(0, 3, project, 0)

    def normalise(t, carry):
        at = pl.ds(pl.multiple_of(t * 32, 32), 32)
        residual = unit_ref[at, :]
        centered = residual - jnp.mean(residual, axis=-1, keepdims=True)
        inv_std = lax.rsqrt(jnp.mean(centered * centered, axis=-1, keepdims=True) + EPSILON)
        unit = centered * inv_std
        unit_ref[at, :] = unit
        std_ref[at, :] = jnp.broadcast_to(inv_std, (32, 128))
        normed = unit * (1.0 + rows_ref[2:3, :]) + rows_ref[1:2, :]
        normed_ref[pl.ds(t * 4, 4)] = normed.reshape(4, 8, D).astype(BF)
        return carry

    lax.fori_loop(0, 8, normalise, 0)
    own_normed = pltpu.make_async_copy(normed_ref.at[s], normedm_ref.at[s], lsem.at[3])
    own_normed.start()
    normed_pair = [(normed_ref, normedm_ref)]
    a2a_start(p, normed_pair, asend.at[pl.ds(2, 1)], arecv.at[pl.ds(2, 1)])

    a2a_wait(p, pairs, asend, arecv)
    own[1].wait()
    own[2].wait()

    def temporal(h, carry):
        backward_head(block_loader(qkvm_ref, gm_ref), adder(gqkv_ref), h, bias_ref[...])
        return carry

    lax.fori_loop(0, HEADS, temporal, 0, unroll=2)

    for dd, cols, sem in expected:
        if sem >= 66:
            arrived(dd, cols, sem, other_rows)

    def back_project(dd, carry):
        at = pl.ds(pl.multiple_of(dd * ROWS, 16), ROWS)
        gnt_ref[at, :] = nt(wall_ref[dd, :, :, D:].reshape(ROWS, 3 * D), gqkv_ref[...])
        return carry

    lax.fori_loop(0, DP, back_project, 0)

    def turn(t, carry):
        at = pl.ds(pl.multiple_of(t * 128, 128), 128)
        gn_ref[:, :, at] = gnt_ref[at, :].T.reshape(SEQ, 8, 128).astype(BF)
        return carry

    lax.fori_loop(0, 9, turn, 0)
    a2a_wait(p, normed_pair, asend.at[pl.ds(2, 1)], arecv.at[pl.ds(2, 1)])
    own_normed.wait()
    for c in sent:
        c.wait_send()


def gather_call(w_own, qkv, grad, spatial, hidden, rows):
    any_space = pl.BlockSpec(memory_space=pl.ANY)
    vmem = pl.BlockSpec(memory_space=pltpu.VMEM)
    return pl.pallas_call(
        gather_kernel,
        out_shape=(
            jax.ShapeDtypeStruct((256, D), BF),
            jax.ShapeDtypeStruct((256, 3 * D), BF),
            jax.ShapeDtypeStruct((D, D), BF),
            jax.ShapeDtypeStruct((256, D), F32),
            jax.ShapeDtypeStruct((256, 128), F32),
            jax.ShapeDtypeStruct((SEQ, 8, D), BF),
            jax.ShapeDtypeStruct((SEQ, 8, D), BF),
        ),
        in_specs=[any_space] * 3 + [vmem] * 3,
        out_specs=[vmem] * 5 + [any_space, vmem],
        scratch_shapes=[
            pltpu.VMEM((DP, 18, 8, 4 * D), BF),
            pltpu.VMEM((SEQ, 8, 3 * D), BF),
            pltpu.VMEM((SEQ, 8, D), BF),
            pltpu.VMEM((256, 256), F32),
            pltpu.VMEM((SEQ, 8, D), BF),
            pltpu.VMEM((D, 256), F32),
            pltpu.SemaphoreType.DMA((4,)),
            pltpu.SemaphoreType.DMA((3,)),
            pltpu.SemaphoreType.DMA((3,)),
            pltpu.SemaphoreType.DMA((76,)),
            pltpu.SemaphoreType.DMA((76,)),
        ],
        compiler_params=pltpu.CompilerParams(
            collective_id=0, has_side_effects=True, vmem_limit_bytes=VMEM_LIMIT
        ),
        name="gather_and_exchange",
    )(w_own, qkv, grad, spatial, hidden, rows)


ROWS = 144
QX, OX = 8 * 128, 3 * 128
CZ = 256


def x_start(xx):
    q = xx * 27 // 4
    return q - xx // 3, xx * 2


def z_start(ss):
    xx = ss // 8
    q0, o0 = x_start(xx)
    q = ss * 27 // 32
    q = q - ss // 31
    o = ss * 9 // 32
    o = jnp.minimum(o, o0 + 1)
    return q - q0, o - o0


class Reducer:
    def __init__(self, p, which, width, cover, bufs, sems):
        self.p, self.which, self.width, self.cover = p, which, width, cover
        self.lhs_t, self.to_core, self.mine, self.from_core, self.b1y, self.b1x = bufs[:6]
        self.part, self.b2, self.total, self.zbuf = bufs[6:]
        self.csend, self.crecv, self.s1send, self.s1recv = sems[:4]
        self.s2send, self.s2recv, self.zsend, self.zrecv = sems[4:]
        y, x, s = p["y"], p["x"], p["s"]
        self.order = [(y + k) % 4 for k in (1, 2, 3, 0)]
        self.y_to = [p["zhi"] * 4 + r for r in self.order[:3]]
        self.xs = [(x + k) % 4 for k in (1, 2, 3)]
        self.x_to = [xx * 8 + s % 8 for xx in self.xs]

    def cols(self, xx, t=0, size=None):
        first = x_start(xx)[self.which] * 128
        return pl.ds(pl.multiple_of(first + t, 128), self.cover if size is None else size)

    def core_copy(self, i):
        r = self.order[i]
        p = self.p
        return rcopy(
            self.to_core.at[r],
            self.from_core.at[r],
            self.csend.at[i],
            self.crecv.at[i],
            p["s"] + 1 - 2 * p["core"],
            p["d"],
        )

    def first_y(self, i):
        return rcopy(
            self.mine.at[self.order[i]],
            self.b1y.at[i],
            self.s1send.at[i],
            self.s1recv.at[i],
            self.p["s"],
            self.y_to[i],
        )

    def first_x(self, k, i):
        r = self.order[i]
        return rcopy(
            self.mine.at[r, :, self.cols(self.xs[k])],
            self.b1x.at[k, r],
            self.s1send.at[k * 4 + i],
            self.s1recv.at[k * 4 + i],
            self.x_to[k],
            self.p["d"],
        )

    def second_x(self, k):
        return rcopy(
            self.mine.at[self.p["y"], :, self.cols(self.xs[k])],
            self.b2.at[k],
            self.s2send.at[k],
            self.s2recv.at[k],
            self.x_to[k],
            self.p["d"],
        )

    def second_y(self, i):
        return rcopy(
            self.part.at[self.order[i]],
            self.b2.at[i],
            self.s2send.at[i],
            self.s2recv.at[i],
            self.p["s"],
            self.y_to[i],
        )

    def z_target(self, i):
        p = self.p
        ss = p["x"] * 8 + i
        pd = p["core"] * 4 + p["y"]
        at = z_start(ss)[self.which]
        src = self.total.at[:, pl.ds(pl.multiple_of(at * 128, 128), CZ)]
        z_me = p["zhi"] * 4 + p["zlo"]
        return ss, pd, src, z_me

    def z_copy(self, i):
        ss, pd, src, z_me = self.z_target(i)
        return rcopy(src, self.zbuf.at[z_me], self.zsend.at[i], self.zrecv.at[z_me], ss, pd)

    def z_local(self, i):
        ss, pd, src, z_me = self.z_target(i)
        return pltpu.make_async_copy(src, self.zbuf.at[z_me], self.zrecv.at[z_me])

    def product(self, block, rhs_ref, dst, r, add):
        lhs = self.lhs_t[pl.ds(pl.multiple_of(block * ROWS, 16), ROWS), :]
        step = self.width // 9

        def body(t, carry):
            at = pl.ds(pl.multiple_of(t * step, 128), step)
            value = nn(lhs, rhs_ref[:, at]) * GRAD_SCALE
            if add is not None:
                value = value + add[r, :, at].astype(F32)
            dst[r, :, at] = value.astype(BF)
            return carry

        lax.fori_loop(0, 9, body, 0)

    def start(self, load_lhs, rhs_ref):
        def turn(t, carry):
            at = pl.ds(pl.multiple_of(t * 128, 128), 128)
            self.lhs_t[at, :] = load_lhs(at).T
            return carry

        lax.fori_loop(0, 9, turn, 0)
        for i, r in enumerate(self.order):
            self.product((1 - self.p["core"]) * 4 + r, rhs_ref, self.to_core, r, None)
            self.core_copy(i).start()

    def first(self, rhs_ref):
        core = self.p["core"]
        for i, r in enumerate(self.order):
            self.core_copy(i).wait_recv()
            self.product(core * 4 + r, rhs_ref, self.mine, r, self.from_core)

            if i < 3:

                @pl.when(core == 0)
                def _():
                    self.first_y(i).start()

            @pl.when(core == 1)
            def _():
                for k in range(3):
                    self.first_x(k, i).start()

    def second(self):
        p = self.p
        y = p["y"]

        @pl.when(p["core"] == 0)
        def _():
            for i in range(3):
                self.first_y(i).wait_recv()
            step = self.width // 9

            def body(t, carry):
                at = pl.ds(pl.multiple_of(t * step, 128), step)
                total = self.mine[y, :, at].astype(F32)
                for i in range(3):
                    total = total + self.b1y[i, :, at].astype(F32)
                self.mine[y, :, at] = total.astype(BF)
                return carry

            lax.fori_loop(0, 9, body, 0)
            for k in range(3):
                self.second_x(k).start()

        @pl.when(p["core"] == 1)
        def _():
            for i, r in enumerate(self.order):
                for k in range(3):
                    self.first_x(k, i).wait_recv()

                def body(t, carry):
                    at = pl.ds(pl.multiple_of(t * 128, 128), 128)
                    total = self.mine[r, :, self.cols(p["x"], t * 128, 128)].astype(F32)
                    for k in range(3):
                        total = total + self.b1x[k, r, :, at].astype(F32)
                    self.part[r, :, at] = total.astype(BF)
                    return carry

                lax.fori_loop(0, self.cover // 128, body, 0)
                if i < 3:
                    self.second_y(i).start()

    def third(self):
        p = self.p
        y, x, core = p["y"], p["x"], p["core"]

        def finish(load):
            def body(t, carry):
                at = pl.ds(pl.multiple_of(t * 128, 128), 128)
                total = load(t).astype(F32)
                for k in range(3):
                    total = total + self.b2[k, :, at].astype(F32)
                self.total[:, at] = total.astype(BF)
                return carry

            lax.fori_loop(0, self.cover // 128, body, 0)

        @pl.when(core == 0)
        def _():
            for k in range(3):
                self.second_x(k).wait_recv()
            finish(lambda t: self.mine[y, :, self.cols(x, t * 128, 128)])

        @pl.when(core == 1)
        def _():
            for i in range(3):
                self.second_y(i).wait_recv()
            finish(lambda t: self.part[y, :, pl.ds(pl.multiple_of(t * 128, 128), 128)])

        for i in range(8):
            ss, pd, _, _ = self.z_target(i)
            is_me = jnp.logical_and(ss == p["s"], pd == p["d"])

            @pl.when(jnp.logical_not(is_me))
            def _():
                self.z_copy(i).start()

            @pl.when(is_me)
            def _():
                self.z_local(i).start()

    def last(self, out_ref, at):
        for z in range(8):
            pltpu.make_async_copy(self.zbuf.at[z], self.zbuf.at[z], self.zrecv.at[z]).wait()
        total = self.zbuf[0].astype(F32)
        for z in range(1, 8):
            total = total + self.zbuf[z].astype(F32)
        out_ref[:, at : at + CZ] = total

    def drain(self):
        p = self.p
        for i in range(4):
            self.core_copy(i).wait_send()

        @pl.when(p["core"] == 0)
        def _():
            for i in range(3):
                self.first_y(i).wait_send()
                self.second_x(i).wait_send()

        @pl.when(p["core"] == 1)
        def _():
            for k in range(3):
                for i in range(4):
                    self.first_x(k, i).wait_send()
                self.second_y(k).wait_send()

        for i in range(8):
            ss, pd, _, _ = self.z_target(i)

            @pl.when(jnp.logical_or(ss != p["s"], pd != p["d"]))
            def _():
                self.z_copy(i).wait_send()


def reducer_scratch(width, cover):
    bufs = [
        pltpu.VMEM((D, 256), BF),
        pltpu.VMEM((4, ROWS, width), BF),
        pltpu.VMEM((4, ROWS, width), BF),
        pltpu.VMEM((4, ROWS, width), BF),
        pltpu.VMEM((3, ROWS, width), BF),
        pltpu.VMEM((3, 4, ROWS, cover), BF),
        pltpu.VMEM((4, ROWS, cover), BF),
        pltpu.VMEM((3, ROWS, cover), BF),
        pltpu.VMEM((ROWS, cover), BF),
        pltpu.VMEM((8, ROWS, CZ), BF),
    ]
    sems = [pltpu.SemaphoreType.DMA((n,)) for n in (4, 4, 12, 12, 3, 3, 8, 8)]
    return bufs + sems


GRAD_SCALE = 1.0 / math.sqrt(DP * SEQ * 256)


def reduce_kernel(
    gn_ref,
    normedm_ref,
    gqkv_ref,
    wout_ref,
    attended_ref,
    spatial_ref,
    unit_ref,
    std_ref,
    gout_ref,
    rows_ref,
    hidden_out,
    spatial_out,
    sums_out,
    *scratch,
):
    p = position()
    s, d, x, y, zhi = p["s"], p["d"], p["x"], p["y"], p["zhi"]
    rq = Reducer(p, 0, 3 * D, QX, scratch[0:10], scratch[10:18])
    ro = Reducer(p, 1, D, OX, scratch[18:28], scratch[28:36])
    gnm_ref, proj_ref, gatt_ref, lsem, asend, arecv = scratch[36:]
    own = pltpu.make_async_copy(gn_ref.at[s], gnm_ref.at[s], lsem)
    own.start()
    greet_seq(p)
    for k in (1, 2, 3):
        greet(s, zhi * 4 + (y + k) % 4)
    for i in range(8):
        greet(x * 8 + i, (1 - zhi) * 4 + y)
    pl.semaphore_wait(pltpu.get_barrier_semaphore(), SEQ - 1 + 3 + 8)

    pairs = [(gn_ref, gnm_ref)]
    a2a_start(p, pairs, asend, arecv)
    rq.start(lambda at: normedm_ref[:, :, at].reshape(256, 128), gqkv_ref)
    rq.first(gqkv_ref)

    a2a_wait(p, pairs, asend, arecv)
    own.wait()

    def norm_backward(t, carry):
        at = pl.ds(pl.multiple_of(t * 32, 32), 32)
        unit = unit_ref[at, :]
        inv_std = std_ref[at, 0:1]
        grad_normed = gnm_ref[pl.ds(t * 4, 4)].astype(F32).reshape(32, D)
        grad_hat = grad_normed * (1.0 + rows_ref[2:3, :])
        grad_resid = gout_ref[at, :].astype(F32) + inv_std * (
            grad_hat
            - jnp.mean(grad_hat, axis=-1, keepdims=True)
            - unit * jnp.mean(grad_hat * unit, axis=-1, keepdims=True)
        )
        hidden_out[at, :] = grad_resid.astype(BF)
        proj_ref[at, :] = (rows_ref[0:1, :] * grad_resid).astype(BF)
        return carry

    lax.fori_loop(0, 8, norm_backward, 0)
    ro.start(lambda at: attended_ref[:, at], proj_ref)

    def back_project(t, carry):
        at = pl.ds(pl.multiple_of(t * 128, 128), 128)
        gatt_ref[:, at] = nt(proj_ref[...], wout_ref[at, :]).astype(BF)
        return carry

    lax.fori_loop(0, 9, back_project, 0)
    ro.first(proj_ref)
    spatial_out[...] = jnp.zeros_like(spatial_out)

    def spatial(h, carry):
        backward_head(flat_loader(spatial_ref, gatt_ref), adder(spatial_out), h, None)
        return carry

    lax.fori_loop(0, HEADS // 2, spatial, 0, unroll=2)
    rq.second()
    lax.fori_loop(HEADS // 2, HEADS, spatial, 0, unroll=2)
    rq.third()
    ro.second()
    ro.third()
    rq.last(sums_out, 0)
    ro.last(sums_out, CZ)
    rq.drain()
    ro.drain()


def reduce_call(*args):
    any_space = pl.BlockSpec(memory_space=pl.ANY)
    vmem = pl.BlockSpec(memory_space=pltpu.VMEM)
    return pl.pallas_call(
        reduce_kernel,
        out_shape=(
            jax.ShapeDtypeStruct((256, D), BF),
            jax.ShapeDtypeStruct((256, 3 * D), BF),
            jax.ShapeDtypeStruct((ROWS, 2 * CZ), F32),
        ),
        in_specs=[any_space] + [vmem] * 9,
        out_specs=[vmem] * 3,
        scratch_shapes=reducer_scratch(3 * D, QX)
        + reducer_scratch(D, OX)
        + [
            pltpu.VMEM((SEQ, 8, D), BF),
            pltpu.VMEM((256, D), BF),
            pltpu.VMEM((256, D), BF),
            pltpu.SemaphoreType.DMA,
            pltpu.SemaphoreType.DMA((1,)),
            pltpu.SemaphoreType.DMA((1,)),
        ],
        compiler_params=pltpu.CompilerParams(
            collective_id=1, has_side_effects=True, vmem_limit_bytes=VMEM_LIMIT
        ),
        name="reduce_weight_gradients",
    )(*args)


def per_device(
    hidden_in,
    qkv_spatial,
    qkv_temporal,
    grad_out,
    grad_temporal,
    gate_spatial,
    modulation,
    w_out_spatial,
    w_qkv_temporal,
):
    token_rows = 256
    w_own = jnp.concatenate([w_out_spatial, w_qkv_temporal], axis=1).reshape(18, 8, 4 * D)
    frame_rows = qkv_spatial.reshape(token_rows, 3 * D)
    rows = jnp.concatenate([gate_spatial, modulation[0]], axis=0).astype(F32)
    attended, grad_qkv_moved, w_out, unit, inv_std, normed_moved, grad_normed = gather_call(
        w_own,
        qkv_temporal.reshape(SEQ, 8, 3 * D),
        grad_temporal.reshape(SEQ, 8, D),
        frame_rows,
        hidden_in.reshape(token_rows, D),
        rows,
    )
    grad_hidden, grad_qkv_s, sums = reduce_call(
        grad_normed,
        normed_moved,
        grad_qkv_moved,
        w_out,
        attended,
        frame_rows,
        unit,
        inv_std,
        grad_out.reshape(token_rows, D),
        rows,
    )
    s = lax.axis_index("seq")
    q_at, o_at = z_start(s)
    q0, o0 = x_start(s // 8)
    grad_w_qkv = lax.dynamic_slice(sums, (0, 108 * s - 128 * (q_at + q0)), (ROWS, 108))
    grad_w_out = lax.dynamic_slice(sums, (0, CZ + 36 * s - 128 * (o_at + o0)), (ROWS, 36))
    return (
        grad_hidden.reshape(hidden_in.shape),
        grad_qkv_s.reshape(qkv_spatial.shape),
        grad_w_out,
        grad_w_qkv,
    )


def solution(mesh):
    in_specs = (
        P("dp", "seq", None, None),
        P("dp", "seq", None, None),
        P("dp", "seq", None, None),
        P("dp", "seq", None, None),
        P("dp", "seq", None, None),
        P("dp", None),
        P("dp", None, None),
        P("dp", None),
        P("dp", None),
    )
    out_specs = (
        P("dp", "seq", None, None),
        P("dp", "seq", None, None),
        P("dp", "seq"),
        P("dp", "seq"),
    )
    return jax.shard_map(
        per_device, mesh=mesh, in_specs=in_specs, out_specs=out_specs, check_vma=False
    )
```

```python
import functools
import math

import jax
import jax.numpy as jnp
from jax import lax
from jax.experimental import pallas as pl
from jax.experimental.pallas import tpu as pltpu
from jax.sharding import PartitionSpec as P

HEADS = 16
D = 1152
SEQ = 32
DP = 8
EPSILON = 1e-06
VMEM_LIMIT = 56 * 1024 * 1024
BF = jnp.bfloat16
F32 = jnp.float32


SCALE = 1.0 / math.sqrt(D // HEADS)
LOG2E = math.log2(math.e)


def nt(a, b):
    return lax.dot_general(a, b, (((1,), (1,)), ((), ())), preferred_element_type=F32)


def tn(a, b):
    return lax.dot_general(a, b, (((0,), (0,)), ((), ())), preferred_element_type=F32)


def nn(a, b):
    return jnp.dot(a, b, preferred_element_type=F32)


def window(h):
    chunk = jnp.minimum(h * 9 // 16, 7)
    lane = lax.broadcasted_iota(jnp.int32, (1, 256), 1) + chunk * 128 - h * 72
    keep = jnp.where(jnp.logical_and(lane >= 0, lane < 72), 1.0, 0.0).astype(BF)
    return chunk * 128, keep


def head_probs(q, k, bias):
    s = nt(q, k)
    if bias is not None:
        s = s + bias
    top = jnp.max(s, axis=-1, keepdims=True)
    e = jnp.exp2((s - top) * (SCALE * LOG2E))
    return e * (1.0 / jnp.sum(e, axis=-1, keepdims=True))


def forward_head(load, add, h):
    c, keep = window(h)
    p = head_probs(load(0, c) * keep, load(1, c), None)
    add(0, c, nn(p.astype(BF), load(2, c) * keep))


def backward_head(load, add, h, bias):
    c, keep = window(h)
    q, k, v, g = load(0, c), load(1, c), load(2, c), load(3, c)
    qm, km, gm = q * keep, k * keep, g * keep
    p = head_probs(qm, k, bias)
    pb = p.astype(BF)
    dp = nt(gm, v)
    delta = jnp.sum(dp * p, axis=-1, keepdims=True)
    ds = (p * ((dp - delta) * SCALE)).astype(BF)
    add(2, c, tn(pb, gm))
    add(0, c, nn(ds, km))
    add(1, c, tn(ds, qm))


def columns(j, c):
    return pl.ds(pl.multiple_of(j * D + c, 128), 256)


def adder(ref):
    def add(j, c, value):
        at = columns(j, c)
        ref[:, at] = ref[:, at] + value.astype(BF)

    return add


def flat_loader(qkv_ref, g_ref):
    def load(j, c):
        return qkv_ref[:, columns(j, c)] if j < 3 else g_ref[:, columns(0, c)]

    return load


def block_loader(qkv_ref, g_ref):
    def load(j, c):
        x = qkv_ref[:, :, columns(j, c)] if j < 3 else g_ref[:, :, columns(0, c)]
        return x.reshape(256, 256)

    return load


def position():
    s = lax.axis_index("seq")
    d = lax.axis_index("dp")
    return dict(s=s, d=d, core=s % 2, zlo=(s // 2) % 4, x=s // 8, y=d % 4, zhi=d // 4)


def rcopy(src, dst, ssem, rsem, ps, pd):
    return pltpu.make_async_remote_copy(
        src_ref=src,
        dst_ref=dst,
        send_sem=ssem,
        recv_sem=rsem,
        device_id={"seq": ps, "dp": pd},
        device_id_type=pl.DeviceIdType.MESH,
    )


def greet(ps, pd):
    pl.semaphore_signal(
        pltpu.get_barrier_semaphore(),
        inc=1,
        device_id={"seq": ps, "dp": pd},
        device_id_type=pl.DeviceIdType.MESH,
    )


def a2a_start(p, pairs, ssems, rsems):
    def body(k, carry):
        peer = (p["s"] + k) % SEQ
        for i, (src, dst) in enumerate(pairs):
            rcopy(src.at[peer], dst.at[p["s"]], ssems.at[i], rsems.at[i], peer, p["d"]).start()
        return carry

    lax.fori_loop(1, SEQ, body, 0)


def a2a_wait(p, pairs, ssems, rsems):
    for i, (src, dst) in enumerate(pairs):
        part = pl.ds(0, SEQ - 1)
        rcopy(
            src.at[part], dst.at[part], ssems.at[i], rsems.at[i], (p["s"] + 1) % SEQ, p["d"]
        ).wait()


def greet_seq(p):
    def body(k, carry):
        greet((p["s"] + k) % SEQ, p["d"])
        return carry

    lax.fori_loop(1, SEQ, body, 0)


ROWS = 144
QX, OX = 8 * 128, 3 * 128
CZ = 256


def x_start(xx):
    q = xx * 27 // 4
    return q - xx // 3, xx * 2


def z_start(ss):
    xx = ss // 8
    q0, o0 = x_start(xx)
    q = ss * 27 // 32
    q = q - ss // 31
    o = ss * 9 // 32
    o = jnp.minimum(o, o0 + 1)
    return q - q0, o - o0


class Reducer:
    def __init__(self, p, which, width, cover, bufs, sems):
        self.p, self.which, self.width, self.cover = p, which, width, cover
        self.lhs_t, self.mine, self.from_core, self.b1 = bufs[:4]
        self.part, self.b2, self.total, self.zbuf = bufs[4:]
        self.pieces = [
            (j, j * cover, min(cover, width - j * cover)) for j in range(-(-width // cover))
        ]
        self.csend, self.crecv, self.s1send, self.s1recv = sems[:4]
        self.s2send, self.s2recv, self.zsend, self.zrecv = sems[4:]
        y, x, s = p["y"], p["x"], p["s"]
        self.order = [(y + k) % 4 for k in (1, 2, 3, 0)]
        self.y_to = [p["zhi"] * 4 + r for r in self.order[:3]]
        self.xs = [(x + k) % 4 for k in (1, 2, 3)]
        self.x_to = [xx * 8 + s % 8 for xx in self.xs]

    def cols(self, xx, t=0, size=None):
        first = x_start(xx)[self.which] * 128
        return pl.ds(pl.multiple_of(first + t, 128), self.cover if size is None else size)

    def core_copy(self, i):
        r = self.order[i]
        p = self.p
        return rcopy(
            self.mine.at[r],
            self.from_core.at[r],
            self.csend.at[i],
            self.crecv.at[i],
            p["s"] + 1 - 2 * p["core"],
            p["d"],
        )

    def first_y(self, i):
        return [
            rcopy(
                self.mine.at[self.order[i], :, pl.ds(at, size)],
                self.b1.at[i * 4 + j, :, pl.ds(0, size)],
                self.s1send.at[i * 4 + j],
                self.s1recv.at[i * 4 + j],
                self.p["s"],
                self.y_to[i],
            )
            for j, at, size in self.pieces
        ]

    def first_x(self, k, i):
        r = self.order[i]
        return rcopy(
            self.mine.at[r, :, self.cols(self.xs[k])],
            self.b1.at[k * 4 + r],
            self.s1send.at[k * 4 + i],
            self.s1recv.at[k * 4 + i],
            self.x_to[k],
            self.p["d"],
        )

    def second_x(self, k):
        return rcopy(
            self.mine.at[self.p["y"], :, self.cols(self.xs[k])],
            self.b2.at[k],
            self.s2send.at[k],
            self.s2recv.at[k],
            self.x_to[k],
            self.p["d"],
        )

    def second_y(self, i):
        return rcopy(
            self.part.at[self.order[i]],
            self.b2.at[i],
            self.s2send.at[i],
            self.s2recv.at[i],
            self.p["s"],
            self.y_to[i],
        )

    def z_target(self, i):
        p = self.p
        ss = p["x"] * 8 + i
        pd = p["core"] * 4 + p["y"]
        at = z_start(ss)[self.which]
        src = self.total.at[:, pl.ds(pl.multiple_of(at * 128, 128), CZ)]
        z_me = p["zhi"] * 4 + p["zlo"]
        return ss, pd, src, z_me

    def z_copy(self, i):
        ss, pd, src, z_me = self.z_target(i)
        return rcopy(src, self.zbuf.at[z_me], self.zsend.at[i], self.zrecv.at[z_me], ss, pd)

    def z_local(self, i):
        ss, pd, src, z_me = self.z_target(i)
        return pltpu.make_async_copy(src, self.zbuf.at[z_me], self.zrecv.at[z_me])

    def product(self, block, rhs_ref, dst, r, add):
        lhs = self.lhs_t[pl.ds(pl.multiple_of(block * ROWS, 16), ROWS), :]
        step = self.width // 9

        def body(t, carry):
            at = pl.ds(pl.multiple_of(t * step, 128), step)
            value = nn(lhs, rhs_ref[:, at]) * GRAD_SCALE
            if add is not None:
                value = value + add[r, :, at].astype(F32)
            dst[r, :, at] = value.astype(BF)
            return carry

        lax.fori_loop(0, 9, body, 0)

    def start(self, load_lhs, rhs_ref):
        def turn(t, carry):
            at = pl.ds(pl.multiple_of(t * 128, 128), 128)
            self.lhs_t[at, :] = load_lhs(at).T
            return carry

        lax.fori_loop(0, 9, turn, 0)
        for i, r in enumerate(self.order):
            self.product((1 - self.p["core"]) * 4 + r, rhs_ref, self.mine, r, None)
            self.core_copy(i).start()

    def first(self, rhs_ref):
        core = self.p["core"]
        for i, r in enumerate(self.order):
            self.core_copy(i).wait()
            self.product(core * 4 + r, rhs_ref, self.mine, r, self.from_core)

            if i < 3:

                @pl.when(core == 0)
                def _():
                    for c in self.first_y(i):
                        c.start()

            @pl.when(core == 1)
            def _():
                for k in range(3):
                    self.first_x(k, i).start()

    def second(self):
        p = self.p
        y = p["y"]

        @pl.when(p["core"] == 0)
        def _():
            for i in range(3):
                for c in self.first_y(i):
                    c.wait_recv()
            n = self.cover // 128

            def body(t, carry):
                at = pl.ds(pl.multiple_of(t * 128, 128), 128)
                there = pl.ds(pl.multiple_of(t % n * 128, 128), 128)
                total = self.mine[y, :, at].astype(F32)
                for i in range(3):
                    total = total + self.b1[i * 4 + t // n, :, there].astype(F32)
                self.mine[y, :, at] = total.astype(BF)
                return carry

            lax.fori_loop(0, self.width // 128, body, 0, unroll=3)
            for k in range(3):
                self.second_x(k).start()

        @pl.when(p["core"] == 1)
        def _():
            for i, r in enumerate(self.order):
                for k in range(3):
                    self.first_x(k, i).wait_recv()

                def body(t, carry):
                    at = pl.ds(pl.multiple_of(t * 128, 128), 128)
                    total = self.mine[r, :, self.cols(p["x"], t * 128, 128)].astype(F32)
                    for k in range(3):
                        total = total + self.b1[k * 4 + r, :, at].astype(F32)
                    self.part[r, :, at] = total.astype(BF)
                    return carry

                lax.fori_loop(0, self.cover // 128, body, 0)
                if i < 3:
                    self.second_y(i).start()

    def third(self):
        p = self.p
        y, x, core = p["y"], p["x"], p["core"]

        def finish(load):
            def body(t, carry):
                at = pl.ds(pl.multiple_of(t * 128, 128), 128)
                total = load(t).astype(F32)
                for k in range(3):
                    total = total + self.b2[k, :, at].astype(F32)
                self.total[:, at] = total.astype(BF)
                return carry

            lax.fori_loop(0, self.cover // 128, body, 0)

        @pl.when(core == 0)
        def _():
            for k in range(3):
                self.second_x(k).wait_recv()
            finish(lambda t: self.mine[y, :, self.cols(x, t * 128, 128)])

        @pl.when(core == 1)
        def _():
            for i in range(3):
                self.second_y(i).wait_recv()
            finish(lambda t: self.part[y, :, pl.ds(pl.multiple_of(t * 128, 128), 128)])

        for i in range(8):
            ss, pd, _, _ = self.z_target(i)
            is_me = jnp.logical_and(ss == p["s"], pd == p["d"])

            @pl.when(jnp.logical_not(is_me))
            def _():
                self.z_copy(i).start()

            @pl.when(is_me)
            def _():
                self.z_local(i).start()

    def last(self, out_ref, size):
        for z in range(8):
            pltpu.make_async_copy(self.zbuf.at[z], self.zbuf.at[z], self.zrecv.at[z]).wait()
        total = self.zbuf[0].astype(F32)
        for z in range(1, 8):
            total = total + self.zbuf[z].astype(F32)
        first = (x_start(self.p["x"])[self.which] + z_start(self.p["s"])[self.which]) * 128
        skip = self.p["s"] * size - first
        out_ref[...] = pltpu.roll(total, (CZ - skip) % CZ, 1)[:, :size]

    def drain(self):
        p = self.p

        @pl.when(p["core"] == 0)
        def _():
            for i in range(3):
                for c in self.first_y(i):
                    c.wait_send()
                self.second_x(i).wait_send()

        @pl.when(p["core"] == 1)
        def _():
            for k in range(3):
                for i in range(4):
                    self.first_x(k, i).wait_send()
                self.second_y(k).wait_send()

        for i in range(8):
            ss, pd, _, _ = self.z_target(i)

            @pl.when(jnp.logical_or(ss != p["s"], pd != p["d"]))
            def _():
                self.z_copy(i).wait_send()


def reducer_scratch(width, cover):
    bufs = [
        pltpu.VMEM((D, 256), BF),
        pltpu.VMEM((4, ROWS, width), BF),
        pltpu.VMEM((4, ROWS, width), BF),
        pltpu.VMEM((12, ROWS, cover), BF),
        pltpu.VMEM((4, ROWS, cover), BF),
        pltpu.VMEM((3, ROWS, cover), BF),
        pltpu.VMEM((ROWS, cover), BF),
        pltpu.VMEM((8, ROWS, CZ), BF),
    ]
    sems = [pltpu.SemaphoreType.DMA((n,)) for n in (4, 4, 12, 12, 3, 3, 8, 8)]
    return bufs + sems


GRAD_SCALE = 1.0 / math.sqrt(DP * SEQ * 256)


SPLIT = 1536
WA, WB = SPLIT // 4, (4 * D - SPLIT) // 4


def whole_kernel(
    w_out_ref,
    w_qkv_ref,
    qkv_ref,
    g_ref,
    spatial_hbm,
    hidden_hbm,
    gout_hbm,
    rows_ref,
    hidden_out,
    spatial_out,
    w_out_out,
    w_qkv_out,
    *scratch,
):
    (
        wall_ref,
        qkvm_ref,
        gm_ref,
        spatial_ref,
        hidden_ref,
        gout_ref,
        attended_ref,
        gqkv_ref,
        wout_ref,
        unit_ref,
        std_ref,
        normed_ref,
        normedm_ref,
        bias_ref,
        gnt_ref,
        gn_ref,
        gnm_ref,
        proj_ref,
        gatt_ref,
        lsem,
        asend,
        arecv,
        wsend,
        wrecv,
    ) = scratch[32:]
    p = position()
    s, d, x, y, core, zhi = p["s"], p["d"], p["x"], p["y"], p["core"], p["zhi"]
    own = [
        pltpu.make_async_copy(w_out_ref, wall_ref.at[d, :, :, pl.ds(0, D)], lsem.at[0]),
        pltpu.make_async_copy(w_qkv_ref, wall_ref.at[d, :, :, pl.ds(D, 3 * D)], lsem.at[4]),
        pltpu.make_async_copy(spatial_hbm, spatial_ref, lsem.at[5]),
        pltpu.make_async_copy(hidden_hbm, hidden_ref, lsem.at[6]),
        pltpu.make_async_copy(gout_hbm, gout_ref, lsem.at[7]),
        pltpu.make_async_copy(qkv_ref.at[s], qkvm_ref.at[s], lsem.at[1]),
        pltpu.make_async_copy(g_ref.at[s], gm_ref.at[s], lsem.at[2]),
    ]
    for c in own:
        c.start()
    greet_seq(p)
    far = (d + 4) % DP
    y_to = [zhi * 4 + (y + k) % 4 for k in (1, 2, 3)]
    y_from = [zhi * 4 + (y + 4 - k) % 4 for k in (1, 2, 3)]
    y_far = [(1 - zhi) * 4 + (y + 4 - k) % 4 for k in (1, 2, 3)]
    x_to = [((x + k) % 4) * 8 + s % 8 for k in (1, 2, 3)]
    x_from = [(x + 4 - k) % 4 for k in (1, 2, 3)]
    sibling = s + 1 - 2 * core
    for peer in y_to:
        greet(s, peer)
    for i in range(8):
        greet(x * 8 + i, (1 - zhi) * 4 + y)
    pl.semaphore_wait(pltpu.get_barrier_semaphore(), SEQ - 1 + 3 + 8)
    own[0].wait()
    own[1].wait()

    rows = pl.ds(core * 9, 9)
    other_rows = pl.ds((1 - core) * 9, 9)

    def col_a(xx):
        return pl.ds(pl.multiple_of(xx * WA, 128), WA)

    def col_b(xx):
        return pl.ds(pl.multiple_of(SPLIT + xx * WB, 128), WB)

    all_b = pl.ds(SPLIT, 4 * WB)
    sent = []
    expected = []

    def send(dd, cols, sem, ps, pd):
        ref = wall_ref.at[dd, rows, :, cols]
        c = rcopy(ref, ref, wsend.at[sem], wrecv.at[sem], ps, pd)
        c.start()
        sent.append(c)

    def arrived(dd, cols, sem, which=None):
        ref = wall_ref.at[dd, rows if which is None else which, :, cols]
        rcopy(ref, ref, wsend.at[sem], wrecv.at[sem], s, far).wait_recv()

    def hand_on(dd, cols, sem):
        send(dd, cols, sem, sibling, d)
        expected.append((dd, cols, sem))

    send(d, col_b(x), 56, s, far)
    send(d, col_a(x), 0, s, far)
    for k in range(3):
        send(d, col_a(x), 1 + k, s, y_to[k])
    for k in range(3):
        send(d, all_b, 60 + k, s, y_to[k])
    pairs = [(qkv_ref, qkvm_ref), (g_ref, gm_ref)]
    a2a_start(p, pairs, asend, arecv)

    arrived(far, col_b(x), 56)
    for k in range(3):
        send(far, col_b(x), 57 + k, x_to[k], d)
    arrived(far, col_a(x), 0)
    for k in range(3):
        send(far, col_a(x), 4 + k, s, y_to[k])
    hand_on(far, col_b(x), 66)

    attended_ref[...] = jnp.zeros_like(attended_ref)
    own[2].wait()

    def spatial(h, carry):
        forward_head(flat_loader(spatial_ref, None), adder(attended_ref), h)
        return carry

    lax.fori_loop(0, HEADS, spatial, 0, unroll=2)

    for k in range(3):
        arrived(far, col_b(x_from[k]), 57 + k)
    for k in range(3):
        send(far, all_b, 63 + k, s, y_to[k])
    for k in range(3):
        hand_on(far, col_b(x_from[k]), 67 + k)
    sources = [far] + y_from + y_far
    for j, dd in enumerate(sources):
        if j:
            arrived(dd, col_a(x), j)
        for k in range(3):
            send(dd, col_a(x), 7 + j * 3 + k, x_to[k], d)
        hand_on(dd, col_a(x), 28 + j)
    for k in range(3):
        arrived(y_from[k], all_b, 60 + k)
        hand_on(y_from[k], all_b, 70 + k)
    for j, dd in enumerate(sources):
        for k in range(3):
            arrived(dd, col_a(x_from[k]), 7 + j * 3 + k)
            hand_on(dd, col_a(x_from[k]), 35 + j * 3 + k)
    for k in range(3):
        arrived(y_far[k], all_b, 63 + k)
        hand_on(y_far[k], all_b, 73 + k)

    at = lax.broadcasted_iota(jnp.int32, (256, 256), 0) % 8
    to = lax.broadcasted_iota(jnp.int32, (256, 256), 1) % 8
    bias_ref[...] = jnp.where(at == to, 0.0, -1e30)
    gqkv_ref[...] = jnp.zeros_like(gqkv_ref)

    own[3].wait()
    for dd, cols, sem in expected:
        if sem < 66:
            arrived(dd, cols, sem, other_rows)

    def assemble(dd, carry):
        at = pl.ds(pl.multiple_of(dd * ROWS, 16), ROWS)
        wout_ref[at, :] = wall_ref[dd, :, :, :D].reshape(ROWS, D)
        return carry

    lax.fori_loop(0, DP, assemble, 0)

    def project(t, carry):
        at = pl.ds(pl.multiple_of(t * 384, 128), 384)
        unit_ref[:, at] = hidden_ref[:, at].astype(F32) + rows_ref[0:1, at] * nn(
            attended_ref[...], wout_ref[:, at]
        )
        return carry

    lax.fori_loop(0, 3, project, 0)

    def normalise(t, carry):
        at = pl.ds(pl.multiple_of(t * 32, 32), 32)
        residual = unit_ref[at, :]
        centered = residual - jnp.mean(residual, axis=-1, keepdims=True)
        inv_std = lax.rsqrt(jnp.mean(centered * centered, axis=-1, keepdims=True) + EPSILON)
        unit = centered * inv_std
        unit_ref[at, :] = unit
        std_ref[at, :] = jnp.broadcast_to(inv_std, (32, 128))
        normed = unit * (1.0 + rows_ref[2:3, :]) + rows_ref[1:2, :]
        normed_ref[pl.ds(t * 4, 4)] = normed.reshape(4, 8, D).astype(BF)
        return carry

    lax.fori_loop(0, 8, normalise, 0)
    own_normed = pltpu.make_async_copy(normed_ref.at[s], normedm_ref.at[s], lsem.at[3])
    own_normed.start()
    normed_pair = [(normed_ref, normedm_ref)]
    a2a_start(p, normed_pair, asend.at[pl.ds(2, 1)], arecv.at[pl.ds(2, 1)])

    a2a_wait(p, pairs, asend, arecv)
    own[5].wait()
    own[6].wait()

    def temporal(h, carry):
        backward_head(block_loader(qkvm_ref, gm_ref), adder(gqkv_ref), h, bias_ref[...])
        return carry

    lax.fori_loop(0, HEADS, temporal, 0, unroll=2)

    for dd, cols, sem in expected:
        if sem >= 66:
            arrived(dd, cols, sem, other_rows)

    def back_project(dd, carry):
        at = pl.ds(pl.multiple_of(dd * ROWS, 16), ROWS)
        gnt_ref[at, :] = nt(wall_ref[dd, :, :, D:].reshape(ROWS, 3 * D), gqkv_ref[...])
        return carry

    lax.fori_loop(0, DP, back_project, 0)

    def turn(t, carry):
        at = pl.ds(pl.multiple_of(t * 128, 128), 128)
        gn_ref[:, :, at] = gnt_ref[at, :].T.reshape(SEQ, 8, 128).astype(BF)
        return carry

    lax.fori_loop(0, 9, turn, 0)
    own_back = pltpu.make_async_copy(gn_ref.at[s], gnm_ref.at[s], lsem.at[8])
    own_back.start()
    back_pair = [(gn_ref, gnm_ref)]
    a2a_start(p, back_pair, asend.at[pl.ds(3, 1)], arecv.at[pl.ds(3, 1)])
    a2a_wait(p, normed_pair, asend.at[pl.ds(2, 1)], arecv.at[pl.ds(2, 1)])
    own_normed.wait()

    rq = Reducer(p, 0, 3 * D, QX, scratch[0:8], scratch[8:16])
    ro = Reducer(p, 1, D, OX, scratch[16:24], scratch[24:32])
    rq.start(lambda at: normedm_ref[:, :, at].reshape(256, 128), gqkv_ref)
    rq.first(gqkv_ref)

    a2a_wait(p, back_pair, asend.at[pl.ds(3, 1)], arecv.at[pl.ds(3, 1)])
    own_back.wait()
    own[4].wait()

    def norm_backward(t, carry):
        at = pl.ds(pl.multiple_of(t * 32, 32), 32)
        unit = unit_ref[at, :]
        inv_std = std_ref[at, 0:1]
        grad_normed = gnm_ref[pl.ds(t * 4, 4)].astype(F32).reshape(32, D)
        grad_hat = grad_normed * (1.0 + rows_ref[2:3, :])
        grad_resid = gout_ref[at, :].astype(F32) + inv_std * (
            grad_hat
            - jnp.mean(grad_hat, axis=-1, keepdims=True)
            - unit * jnp.mean(grad_hat * unit, axis=-1, keepdims=True)
        )
        hidden_out[at, :] = grad_resid.astype(BF)
        proj_ref[at, :] = (rows_ref[0:1, :] * grad_resid).astype(BF)
        return carry

    lax.fori_loop(0, 8, norm_backward, 0)
    ro.start(lambda at: attended_ref[:, at], proj_ref)

    def attend_grad(t, carry):
        at = pl.ds(pl.multiple_of(t * 128, 128), 128)
        gatt_ref[:, at] = nt(proj_ref[...], wout_ref[at, :]).astype(BF)
        return carry

    lax.fori_loop(0, 9, attend_grad, 0)
    ro.first(proj_ref)
    spatial_out[...] = jnp.zeros_like(spatial_out)

    def spatial_back(h, carry):
        backward_head(flat_loader(spatial_ref, gatt_ref), adder(spatial_out), h, None)
        return carry

    lax.fori_loop(0, HEADS // 2, spatial_back, 0, unroll=2)
    rq.second()
    lax.fori_loop(HEADS // 2, HEADS, spatial_back, 0, unroll=2)
    rq.third()
    ro.second()
    ro.third()
    rq.last(w_qkv_out, 108)
    ro.last(w_out_out, 36)
    for c in sent:
        c.wait_send()
    rq.drain()
    ro.drain()


def whole_call(*args):
    any_space = pl.BlockSpec(memory_space=pl.ANY)
    vmem = pl.BlockSpec(memory_space=pltpu.VMEM)
    return pl.pallas_call(
        whole_kernel,
        out_shape=(
            jax.ShapeDtypeStruct((256, D), BF),
            jax.ShapeDtypeStruct((256, 3 * D), BF),
            jax.ShapeDtypeStruct((ROWS, 36), F32),
            jax.ShapeDtypeStruct((ROWS, 108), F32),
        ),
        in_specs=[any_space] * 7 + [vmem],
        out_specs=[vmem] * 4,
        scratch_shapes=reducer_scratch(3 * D, QX)
        + reducer_scratch(D, OX)
        + [
            pltpu.VMEM((DP, 18, 8, 4 * D), BF),
            pltpu.VMEM((SEQ, 8, 3 * D), BF),
            pltpu.VMEM((SEQ, 8, D), BF),
            pltpu.VMEM((256, 3 * D), BF),
            pltpu.VMEM((256, D), BF),
            pltpu.VMEM((256, D), BF),
            pltpu.VMEM((256, D), BF),
            pltpu.VMEM((256, 3 * D), BF),
            pltpu.VMEM((D, D), BF),
            pltpu.VMEM((256, D), F32),
            pltpu.VMEM((256, 128), F32),
            pltpu.VMEM((SEQ, 8, D), BF),
            pltpu.VMEM((SEQ, 8, D), BF),
            pltpu.VMEM((256, 256), F32),
            pltpu.VMEM((D, 256), F32),
            pltpu.VMEM((SEQ, 8, D), BF),
            pltpu.VMEM((SEQ, 8, D), BF),
            pltpu.VMEM((256, D), BF),
            pltpu.VMEM((256, D), BF),
            pltpu.SemaphoreType.DMA((9,)),
            pltpu.SemaphoreType.DMA((4,)),
            pltpu.SemaphoreType.DMA((4,)),
            pltpu.SemaphoreType.DMA((76,)),
            pltpu.SemaphoreType.DMA((76,)),
        ],
        compiler_params=pltpu.CompilerParams(
            collective_id=0, has_side_effects=True, vmem_limit_bytes=VMEM_LIMIT
        ),
        name="whole",
    )(*args)


def per_device(
    hidden_in,
    qkv_spatial,
    qkv_temporal,
    grad_out,
    grad_temporal,
    gate_spatial,
    modulation,
    w_out_spatial,
    w_qkv_temporal,
):
    rows = jnp.concatenate([gate_spatial, modulation[0]], axis=0).astype(F32)
    grad_hidden, grad_qkv_s, grad_w_out, grad_w_qkv = whole_call(
        w_out_spatial.reshape(18, 8, D),
        w_qkv_temporal.reshape(18, 8, 3 * D),
        qkv_temporal.reshape(SEQ, 8, 3 * D),
        grad_temporal.reshape(SEQ, 8, D),
        qkv_spatial.reshape(256, 3 * D),
        hidden_in.reshape(256, D),
        grad_out.reshape(256, D),
        rows,
    )
    return (
        grad_hidden.reshape(hidden_in.shape),
        grad_qkv_s.reshape(qkv_spatial.shape),
        grad_w_out,
        grad_w_qkv,
    )


def solution(mesh):
    in_specs = (
        P("dp", "seq", None, None),
        P("dp", "seq", None, None),
        P("dp", "seq", None, None),
        P("dp", "seq", None, None),
        P("dp", "seq", None, None),
        P("dp", None),
        P("dp", None, None),
        P("dp", None),
        P("dp", None),
    )
    out_specs = (
        P("dp", "seq", None, None),
        P("dp", "seq", None, None),
        P("dp", "seq"),
        P("dp", "seq"),
    )
    return jax.shard_map(
        per_device, mesh=mesh, in_specs=in_specs, out_specs=out_specs, check_vma=False
    )
```

```python
import functools
import math

import jax
import jax.numpy as jnp
from jax import lax
from jax.experimental import pallas as pl
from jax.experimental.pallas import tpu as pltpu
from jax.sharding import PartitionSpec as P

HEADS = 16
D = 1152
SEQ = 32
DP = 8
EPSILON = 1e-06
VMEM_LIMIT = 56 * 1024 * 1024
BF = jnp.bfloat16
F32 = jnp.float32


SCALE = 1.0 / math.sqrt(D // HEADS)
LOG2E = math.log2(math.e)


def nt(a, b):
    return lax.dot_general(a, b, (((1,), (1,)), ((), ())), preferred_element_type=F32)


def tn(a, b):
    return lax.dot_general(a, b, (((0,), (0,)), ((), ())), preferred_element_type=F32)


def nn(a, b):
    return jnp.dot(a, b, preferred_element_type=F32)


def window(h):
    chunk = jnp.minimum(h * 9 // 16, 7)
    lane = lax.broadcasted_iota(jnp.int32, (1, 256), 1) + chunk * 128 - h * 72
    keep = jnp.where(jnp.logical_and(lane >= 0, lane < 72), 1.0, 0.0).astype(BF)
    return chunk * 128, keep


def head_probs(q, k, bias):
    s = nt(q, k)
    if bias is not None:
        s = s + bias
    top = jnp.max(s, axis=-1, keepdims=True)
    e = jnp.exp2((s - top) * (SCALE * LOG2E))
    return e * (1.0 / jnp.sum(e, axis=-1, keepdims=True))


def forward_head(load, add, h):
    c, keep = window(h)
    p = head_probs(load(0, c) * keep, load(1, c), None)
    add(0, c, nn(p.astype(BF), load(2, c) * keep))


def backward_head(load, add, h, bias):
    c, keep = window(h)
    q, k, v, g = load(0, c), load(1, c), load(2, c), load(3, c)
    qm, km, gm = q * keep, k * keep, g * keep
    p = head_probs(qm, k, bias)
    pb = p.astype(BF)
    dp = nt(gm, v)
    delta = jnp.sum(dp * p, axis=-1, keepdims=True)
    ds = (p * ((dp - delta) * SCALE)).astype(BF)
    add(2, c, tn(pb, gm))
    add(0, c, nn(ds, km))
    add(1, c, tn(ds, qm))


def columns(j, c):
    return pl.ds(pl.multiple_of(j * D + c, 128), 256)


def adder(ref):
    def add(j, c, value):
        at = columns(j, c)
        ref[:, at] = ref[:, at] + value.astype(BF)

    return add


def flat_loader(qkv_ref, g_ref):
    def load(j, c):
        return qkv_ref[:, columns(j, c)] if j < 3 else g_ref[:, columns(0, c)]

    return load


def block_loader(qkv_ref, g_ref):
    def load(j, c):
        x = qkv_ref[:, :, columns(j, c)] if j < 3 else g_ref[:, :, columns(0, c)]
        return x.reshape(256, 256)

    return load


def position():
    s = lax.axis_index("seq")
    d = lax.axis_index("dp")
    return dict(s=s, d=d, core=s % 2, zlo=(s // 2) % 4, x=s // 8, y=d % 4, zhi=d // 4)


def rcopy(src, dst, ssem, rsem, ps, pd):
    return pltpu.make_async_remote_copy(
        src_ref=src,
        dst_ref=dst,
        send_sem=ssem,
        recv_sem=rsem,
        device_id={"seq": ps, "dp": pd},
        device_id_type=pl.DeviceIdType.MESH,
    )


def greet(ps, pd):
    pl.semaphore_signal(
        pltpu.get_barrier_semaphore(),
        inc=1,
        device_id={"seq": ps, "dp": pd},
        device_id_type=pl.DeviceIdType.MESH,
    )


def a2a_start(p, pairs, ssems, rsems):
    def body(k, carry):
        peer = (p["s"] + k) % SEQ
        for i, (src, dst) in enumerate(pairs):
            rcopy(src.at[peer], dst.at[p["s"]], ssems.at[i], rsems.at[i], peer, p["d"]).start()
        return carry

    lax.fori_loop(1, SEQ, body, 0)


def a2a_wait(p, pairs, ssems, rsems):
    for i, (src, dst) in enumerate(pairs):
        part = pl.ds(0, SEQ - 1)
        rcopy(
            src.at[part], dst.at[part], ssems.at[i], rsems.at[i], (p["s"] + 1) % SEQ, p["d"]
        ).wait()


def greet_seq(p):
    def body(k, carry):
        greet((p["s"] + k) % SEQ, p["d"])
        return carry

    lax.fori_loop(1, SEQ, body, 0)


ROWS = 144
QX, OX = 8 * 128, 3 * 128
CZ = 256
LANES = 128


def x_start(xx):
    q = xx * 27 // 4
    return q - xx // 3, xx * 2


def z_start(ss):
    xx = ss // 8
    q0, o0 = x_start(xx)
    q = ss * 27 // 32
    q = q - ss // 31
    o = ss * 9 // 32
    o = jnp.minimum(o, o0 + 1)
    return q - q0, o - o0


class Reducer:
    def __init__(self, p, which, width, cover, bufs, sems):
        self.p, self.which, self.width, self.cover = p, which, width, cover
        self.size = width // SEQ
        self.lhs_t, self.mine, self.from_core, self.b1 = bufs[:4]
        self.part, self.b2, self.total, self.zout, self.zbuf = bufs[4:]
        self.pieces = [
            (j, j * cover, min(cover, width - j * cover)) for j in range(-(-width // cover))
        ]
        self.csend, self.crecv, self.s1send, self.s1recv = sems[:4]
        self.s2send, self.s2recv, self.zsend, self.zrecv = sems[4:]
        y, x, s = p["y"], p["x"], p["s"]
        self.order = [(y + k) % 4 for k in (1, 2, 3, 0)]
        self.y_to = [p["zhi"] * 4 + r for r in self.order[:3]]
        self.xs = [(x + k) % 4 for k in (1, 2, 3)]
        self.x_to = [xx * 8 + s % 8 for xx in self.xs]

    def cols(self, xx, t=0, size=None):
        first = x_start(xx)[self.which] * 128
        return pl.ds(pl.multiple_of(first + t, 128), self.cover if size is None else size)

    def core_copy(self, i):
        r = self.order[i]
        p = self.p
        return rcopy(
            self.mine.at[r],
            self.from_core.at[r],
            self.csend.at[i],
            self.crecv.at[i],
            p["s"] + 1 - 2 * p["core"],
            p["d"],
        )

    def first_y(self, i):
        return [
            rcopy(
                self.mine.at[self.order[i], :, pl.ds(at, size)],
                self.b1.at[i * 4 + j, :, pl.ds(0, size)],
                self.s1send.at[i * 4 + j],
                self.s1recv.at[i * 4 + j],
                self.p["s"],
                self.y_to[i],
            )
            for j, at, size in self.pieces
        ]

    def first_x(self, k, i):
        r = self.order[i]
        return rcopy(
            self.mine.at[r, :, self.cols(self.xs[k])],
            self.b1.at[k * 4 + r],
            self.s1send.at[k * 4 + i],
            self.s1recv.at[k * 4 + i],
            self.x_to[k],
            self.p["d"],
        )

    def second_x(self, k):
        return rcopy(
            self.mine.at[self.p["y"], :, self.cols(self.xs[k])],
            self.b2.at[k],
            self.s2send.at[k],
            self.s2recv.at[k],
            self.x_to[k],
            self.p["d"],
        )

    def second_y(self, i):
        return rcopy(
            self.part.at[self.order[i]],
            self.b2.at[i],
            self.s2send.at[i],
            self.s2recv.at[i],
            self.p["s"],
            self.y_to[i],
        )

    def z_target(self, i):
        p = self.p
        ss = p["x"] * 8 + i
        pd = p["core"] * 4 + p["y"]
        z_me = p["zhi"] * 4 + p["zlo"]
        return ss, pd, self.zout.at[i], z_me

    def z_copy(self, i):
        ss, pd, src, z_me = self.z_target(i)
        return rcopy(src, self.zbuf.at[z_me], self.zsend.at[i], self.zrecv.at[z_me], ss, pd)

    def z_local(self, i):
        ss, pd, src, z_me = self.z_target(i)
        return pltpu.make_async_copy(src, self.zbuf.at[z_me], self.zrecv.at[z_me])

    def product(self, block, rhs_ref, dst, r, add):
        lhs = self.lhs_t[pl.ds(pl.multiple_of(block * ROWS, 16), ROWS), :]
        step = self.width // 9

        def body(t, carry):
            at = pl.ds(pl.multiple_of(t * step, 128), step)
            value = nn(lhs, rhs_ref[:, at]) * GRAD_SCALE
            if add is not None:
                value = value + add[r, :, at].astype(F32)
            dst[r, :, at] = value.astype(BF)
            return carry

        lax.fori_loop(0, 9, body, 0)

    def start(self, load_lhs, rhs_ref):
        def turn(t, carry):
            at = pl.ds(pl.multiple_of(t * 128, 128), 128)
            self.lhs_t[at, :] = load_lhs(at).T
            return carry

        lax.fori_loop(0, 9, turn, 0)
        for i, r in enumerate(self.order):
            self.product((1 - self.p["core"]) * 4 + r, rhs_ref, self.mine, r, None)
            self.core_copy(i).start()

    def first(self, rhs_ref):
        core = self.p["core"]
        for i, r in enumerate(self.order):
            self.core_copy(i).wait()
            self.product(core * 4 + r, rhs_ref, self.mine, r, self.from_core)

            if i < 3:

                @pl.when(core == 0)
                def _():
                    for c in self.first_y(i):
                        c.start()

            @pl.when(core == 1)
            def _():
                for k in range(3):
                    self.first_x(k, i).start()

    def second(self):
        p = self.p
        y = p["y"]

        @pl.when(p["core"] == 0)
        def _():
            for i in range(3):
                for c in self.first_y(i):
                    c.wait_recv()
            n = self.cover // 128

            def body(t, carry):
                at = pl.ds(pl.multiple_of(t * 128, 128), 128)
                there = pl.ds(pl.multiple_of(t % n * 128, 128), 128)
                total = self.mine[y, :, at].astype(F32)
                for i in range(3):
                    total = total + self.b1[i * 4 + t // n, :, there].astype(F32)
                self.mine[y, :, at] = total.astype(BF)
                return carry

            lax.fori_loop(0, self.width // 128, body, 0, unroll=3)
            for k in range(3):
                self.second_x(k).start()

        @pl.when(p["core"] == 1)
        def _():
            for i, r in enumerate(self.order):
                for k in range(3):
                    self.first_x(k, i).wait_recv()

                def body(t, carry):
                    at = pl.ds(pl.multiple_of(t * 128, 128), 128)
                    total = self.mine[r, :, self.cols(p["x"], t * 128, 128)].astype(F32)
                    for k in range(3):
                        total = total + self.b1[k * 4 + r, :, at].astype(F32)
                    self.part[r, :, at] = total.astype(BF)
                    return carry

                lax.fori_loop(0, self.cover // 128, body, 0)
                if i < 3:
                    self.second_y(i).start()

    def third(self):
        p = self.p
        y, x, core = p["y"], p["x"], p["core"]

        def finish(load):
            def body(t, carry):
                at = pl.ds(pl.multiple_of(t * 128, 128), 128)
                total = load(t).astype(F32)
                for k in range(3):
                    total = total + self.b2[k, :, at].astype(F32)
                self.total[:, at] = total.astype(BF)
                return carry

            lax.fori_loop(0, self.cover // 128, body, 0)

        @pl.when(core == 0)
        def _():
            for k in range(3):
                self.second_x(k).wait_recv()
            finish(lambda t: self.mine[y, :, self.cols(x, t * 128, 128)])

        @pl.when(core == 1)
        def _():
            for i in range(3):
                self.second_y(i).wait_recv()
            finish(lambda t: self.part[y, :, pl.ds(pl.multiple_of(t * 128, 128), 128)])

        def pack(i, carry):
            ss = x * 8 + i
            at = z_start(ss)[self.which]
            skip = ss * self.size - (x_start(x)[self.which] + at) * 128
            value = self.total[:, pl.ds(pl.multiple_of(at * 128, 128), CZ)].astype(F32)
            self.zout[i] = pltpu.roll(value, (CZ - skip) % CZ, 1)[:, :LANES].astype(BF)
            return carry

        lax.fori_loop(0, 8, pack, 0)
        for i in range(8):
            ss, pd, _, _ = self.z_target(i)
            is_me = jnp.logical_and(ss == p["s"], pd == p["d"])

            @pl.when(jnp.logical_not(is_me))
            def _():
                self.z_copy(i).start()

            @pl.when(is_me)
            def _():
                self.z_local(i).start()

    def last(self, out_ref):
        for z in range(8):
            pltpu.make_async_copy(self.zbuf.at[z], self.zbuf.at[z], self.zrecv.at[z]).wait()
        total = self.zbuf[0].astype(F32)
        for z in range(1, 8):
            total = total + self.zbuf[z].astype(F32)
        out_ref[...] = total[:, : self.size]

    def drain(self):
        p = self.p

        @pl.when(p["core"] == 0)
        def _():
            for i in range(3):
                for c in self.first_y(i):
                    c.wait_send()
                self.second_x(i).wait_send()

        @pl.when(p["core"] == 1)
        def _():
            for k in range(3):
                for i in range(4):
                    self.first_x(k, i).wait_send()
                self.second_y(k).wait_send()

        for i in range(8):
            ss, pd, _, _ = self.z_target(i)

            @pl.when(jnp.logical_or(ss != p["s"], pd != p["d"]))
            def _():
                self.z_copy(i).wait_send()


def reducer_scratch(width, cover):
    bufs = [
        pltpu.VMEM((D, 256), BF),
        pltpu.VMEM((4, ROWS, width), BF),
        pltpu.VMEM((4, ROWS, width), BF),
        pltpu.VMEM((12, ROWS, cover), BF),
        pltpu.VMEM((4, ROWS, cover), BF),
        pltpu.VMEM((3, ROWS, cover), BF),
        pltpu.VMEM((ROWS, cover), BF),
        pltpu.VMEM((8, ROWS, LANES), BF),
        pltpu.VMEM((8, ROWS, LANES), BF),
    ]
    sems = [pltpu.SemaphoreType.DMA((n,)) for n in (4, 4, 12, 12, 3, 3, 8, 8)]
    return bufs + sems


GRAD_SCALE = 1.0 / math.sqrt(DP * SEQ * 256)


SPLIT = 1536
WA, WB = SPLIT // 4, (4 * D - SPLIT) // 4


def whole_kernel(
    w_out_ref,
    w_qkv_ref,
    qkv_ref,
    g_ref,
    spatial_hbm,
    hidden_hbm,
    gout_hbm,
    rows_ref,
    hidden_out,
    spatial_out,
    w_out_out,
    w_qkv_out,
    *scratch,
):
    (
        wall_ref,
        qkvm_ref,
        gm_ref,
        spatial_ref,
        hidden_ref,
        gout_ref,
        attended_ref,
        gqkv_ref,
        wout_ref,
        unit_ref,
        std_ref,
        normed_ref,
        normedm_ref,
        bias_ref,
        gnt_ref,
        gn_ref,
        gnm_ref,
        proj_ref,
        gatt_ref,
        lsem,
        asend,
        arecv,
        wsend,
        wrecv,
    ) = scratch[34:]
    p = position()
    s, d, x, y, core, zhi = p["s"], p["d"], p["x"], p["y"], p["core"], p["zhi"]
    own = [
        pltpu.make_async_copy(w_out_ref, wall_ref.at[d, :, :, pl.ds(0, D)], lsem.at[0]),
        pltpu.make_async_copy(w_qkv_ref, wall_ref.at[d, :, :, pl.ds(D, 3 * D)], lsem.at[4]),
        pltpu.make_async_copy(spatial_hbm, spatial_ref, lsem.at[5]),
        pltpu.make_async_copy(hidden_hbm, hidden_ref, lsem.at[6]),
        pltpu.make_async_copy(gout_hbm, gout_ref, lsem.at[7]),
        pltpu.make_async_copy(qkv_ref.at[s], qkvm_ref.at[s], lsem.at[1]),
        pltpu.make_async_copy(g_ref.at[s], gm_ref.at[s], lsem.at[2]),
    ]
    for c in own:
        c.start()
    greet_seq(p)
    far = (d + 4) % DP
    y_to = [zhi * 4 + (y + k) % 4 for k in (1, 2, 3)]
    y_from = [zhi * 4 + (y + 4 - k) % 4 for k in (1, 2, 3)]
    y_far = [(1 - zhi) * 4 + (y + 4 - k) % 4 for k in (1, 2, 3)]
    x_to = [((x + k) % 4) * 8 + s % 8 for k in (1, 2, 3)]
    x_from = [(x + 4 - k) % 4 for k in (1, 2, 3)]
    sibling = s + 1 - 2 * core
    for peer in y_to:
        greet(s, peer)
    for i in range(8):
        greet(x * 8 + i, (1 - zhi) * 4 + y)
    pl.semaphore_wait(pltpu.get_barrier_semaphore(), SEQ - 1 + 3 + 8)
    own[0].wait()
    own[1].wait()

    rows = pl.ds(core * 9, 9)
    other_rows = pl.ds((1 - core) * 9, 9)

    def col_a(xx):
        return pl.ds(pl.multiple_of(xx * WA, 128), WA)

    def col_b(xx):
        return pl.ds(pl.multiple_of(SPLIT + xx * WB, 128), WB)

    all_b = pl.ds(SPLIT, 4 * WB)
    sent = []
    expected = []

    def send(dd, cols, sem, ps, pd):
        ref = wall_ref.at[dd, rows, :, cols]
        c = rcopy(ref, ref, wsend.at[sem], wrecv.at[sem], ps, pd)
        c.start()
        sent.append(c)

    def arrived(dd, cols, sem, which=None):
        ref = wall_ref.at[dd, rows if which is None else which, :, cols]
        rcopy(ref, ref, wsend.at[sem], wrecv.at[sem], s, far).wait_recv()

    def hand_on(dd, cols, sem):
        send(dd, cols, sem, sibling, d)
        expected.append((dd, cols, sem))

    send(d, col_b(x), 56, s, far)
    send(d, col_a(x), 0, s, far)
    for k in range(3):
        send(d, col_a(x), 1 + k, s, y_to[k])
    for k in range(3):
        send(d, all_b, 60 + k, s, y_to[k])
    pairs = [(qkv_ref, qkvm_ref), (g_ref, gm_ref)]
    a2a_start(p, pairs, asend, arecv)

    arrived(far, col_b(x), 56)
    for k in range(3):
        send(far, col_b(x), 57 + k, x_to[k], d)
    arrived(far, col_a(x), 0)
    for k in range(3):
        send(far, col_a(x), 4 + k, s, y_to[k])
    hand_on(far, col_b(x), 66)

    attended_ref[...] = jnp.zeros_like(attended_ref)
    own[2].wait()

    def spatial(h, carry):
        forward_head(flat_loader(spatial_ref, None), adder(attended_ref), h)
        return carry

    lax.fori_loop(0, HEADS, spatial, 0, unroll=2)

    for k in range(3):
        arrived(far, col_b(x_from[k]), 57 + k)
    for k in range(3):
        send(far, all_b, 63 + k, s, y_to[k])
    for k in range(3):
        hand_on(far, col_b(x_from[k]), 67 + k)
    sources = [far] + y_from + y_far
    for j, dd in enumerate(sources):
        if j:
            arrived(dd, col_a(x), j)
        for k in range(3):
            send(dd, col_a(x), 7 + j * 3 + k, x_to[k], d)
        hand_on(dd, col_a(x), 28 + j)
    for k in range(3):
        arrived(y_from[k], all_b, 60 + k)
        hand_on(y_from[k], all_b, 70 + k)
    for j, dd in enumerate(sources):
        for k in range(3):
            arrived(dd, col_a(x_from[k]), 7 + j * 3 + k)
            hand_on(dd, col_a(x_from[k]), 35 + j * 3 + k)
    for k in range(3):
        arrived(y_far[k], all_b, 63 + k)
        hand_on(y_far[k], all_b, 73 + k)

    at = lax.broadcasted_iota(jnp.int32, (256, 256), 0) % 8
    to = lax.broadcasted_iota(jnp.int32, (256, 256), 1) % 8
    bias_ref[...] = jnp.where(at == to, 0.0, -1e30)
    gqkv_ref[...] = jnp.zeros_like(gqkv_ref)

    own[3].wait()
    for dd, cols, sem in expected:
        if sem < 66:
            arrived(dd, cols, sem, other_rows)

    def assemble(dd, carry):
        at = pl.ds(pl.multiple_of(dd * ROWS, 16), ROWS)
        wout_ref[at, :] = wall_ref[dd, :, :, :D].reshape(ROWS, D)
        return carry

    lax.fori_loop(0, DP, assemble, 0)

    def project(t, carry):
        at = pl.ds(pl.multiple_of(t * 384, 128), 384)
        unit_ref[:, at] = hidden_ref[:, at].astype(F32) + rows_ref[0:1, at] * nn(
            attended_ref[...], wout_ref[:, at]
        )
        return carry

    lax.fori_loop(0, 3, project, 0)

    def normalise(t, carry):
        at = pl.ds(pl.multiple_of(t * 32, 32), 32)
        residual = unit_ref[at, :]
        centered = residual - jnp.mean(residual, axis=-1, keepdims=True)
        inv_std = lax.rsqrt(jnp.mean(centered * centered, axis=-1, keepdims=True) + EPSILON)
        unit = centered * inv_std
        unit_ref[at, :] = unit
        std_ref[at, :] = jnp.broadcast_to(inv_std, (32, 128))
        normed = unit * (1.0 + rows_ref[2:3, :]) + rows_ref[1:2, :]
        normed_ref[pl.ds(t * 4, 4)] = normed.reshape(4, 8, D).astype(BF)
        return carry

    lax.fori_loop(0, 8, normalise, 0)
    own_normed = pltpu.make_async_copy(normed_ref.at[s], normedm_ref.at[s], lsem.at[3])
    own_normed.start()
    normed_pair = [(normed_ref, normedm_ref)]
    a2a_start(p, normed_pair, asend.at[pl.ds(2, 1)], arecv.at[pl.ds(2, 1)])

    a2a_wait(p, pairs, asend, arecv)
    own[5].wait()
    own[6].wait()

    def temporal(h, carry):
        backward_head(block_loader(qkvm_ref, gm_ref), adder(gqkv_ref), h, bias_ref[...])
        return carry

    lax.fori_loop(0, HEADS, temporal, 0, unroll=2)

    for dd, cols, sem in expected:
        if sem >= 66:
            arrived(dd, cols, sem, other_rows)

    def back_project(dd, carry):
        at = pl.ds(pl.multiple_of(dd * ROWS, 16), ROWS)
        gnt_ref[at, :] = nt(wall_ref[dd, :, :, D:].reshape(ROWS, 3 * D), gqkv_ref[...])
        return carry

    lax.fori_loop(0, DP, back_project, 0)

    def turn(t, carry):
        at = pl.ds(pl.multiple_of(t * 128, 128), 128)
        gn_ref[:, :, at] = gnt_ref[at, :].T.reshape(SEQ, 8, 128).astype(BF)
        return carry

    lax.fori_loop(0, 9, turn, 0)
    own_back = pltpu.make_async_copy(gn_ref.at[s], gnm_ref.at[s], lsem.at[8])
    own_back.start()
    back_pair = [(gn_ref, gnm_ref)]
    a2a_start(p, back_pair, asend.at[pl.ds(3, 1)], arecv.at[pl.ds(3, 1)])
    a2a_wait(p, normed_pair, asend.at[pl.ds(2, 1)], arecv.at[pl.ds(2, 1)])
    own_normed.wait()

    rq = Reducer(p, 0, 3 * D, QX, scratch[0:9], scratch[9:17])
    ro = Reducer(p, 1, D, OX, scratch[17:26], scratch[26:34])
    rq.start(lambda at: normedm_ref[:, :, at].reshape(256, 128), gqkv_ref)
    rq.first(gqkv_ref)

    a2a_wait(p, back_pair, asend.at[pl.ds(3, 1)], arecv.at[pl.ds(3, 1)])
    own_back.wait()
    own[4].wait()

    def norm_backward(t, carry):
        at = pl.ds(pl.multiple_of(t * 32, 32), 32)
        unit = unit_ref[at, :]
        inv_std = std_ref[at, 0:1]
        grad_normed = gnm_ref[pl.ds(t * 4, 4)].astype(F32).reshape(32, D)
        grad_hat = grad_normed * (1.0 + rows_ref[2:3, :])
        grad_resid = gout_ref[at, :].astype(F32) + inv_std * (
            grad_hat
            - jnp.mean(grad_hat, axis=-1, keepdims=True)
            - unit * jnp.mean(grad_hat * unit, axis=-1, keepdims=True)
        )
        hidden_out[at, :] = grad_resid.astype(BF)
        proj_ref[at, :] = (rows_ref[0:1, :] * grad_resid).astype(BF)
        return carry

    lax.fori_loop(0, 8, norm_backward, 0)
    ro.start(lambda at: attended_ref[:, at], proj_ref)

    def attend_grad(t, carry):
        at = pl.ds(pl.multiple_of(t * 128, 128), 128)
        gatt_ref[:, at] = nt(proj_ref[...], wout_ref[at, :]).astype(BF)
        return carry

    lax.fori_loop(0, 9, attend_grad, 0)
    ro.first(proj_ref)
    spatial_out[...] = jnp.zeros_like(spatial_out)

    def spatial_back(h, carry):
        backward_head(flat_loader(spatial_ref, gatt_ref), adder(spatial_out), h, None)
        return carry

    lax.fori_loop(0, HEADS // 2, spatial_back, 0, unroll=2)
    rq.second()
    lax.fori_loop(HEADS // 2, HEADS, spatial_back, 0, unroll=2)
    rq.third()
    ro.second()
    ro.third()
    rq.last(w_qkv_out)
    ro.last(w_out_out)
    for c in sent:
        c.wait_send()
    rq.drain()
    ro.drain()


def whole_call(*args):
    any_space = pl.BlockSpec(memory_space=pl.ANY)
    vmem = pl.BlockSpec(memory_space=pltpu.VMEM)
    return pl.pallas_call(
        whole_kernel,
        out_shape=(
            pltpu.VMEM((256, D), BF),
            pltpu.VMEM((256, 3 * D), BF),
            pltpu.VMEM((ROWS, 36), F32),
            pltpu.VMEM((ROWS, 108), F32),
        ),
        in_specs=[any_space] * 7 + [vmem],
        out_specs=[vmem] * 4,
        scratch_shapes=reducer_scratch(3 * D, QX)
        + reducer_scratch(D, OX)
        + [
            pltpu.VMEM((DP, 18, 8, 4 * D), BF),
            pltpu.VMEM((SEQ, 8, 3 * D), BF),
            pltpu.VMEM((SEQ, 8, D), BF),
            pltpu.VMEM((256, 3 * D), BF),
            pltpu.VMEM((256, D), BF),
            pltpu.VMEM((256, D), BF),
            pltpu.VMEM((256, D), BF),
            pltpu.VMEM((256, 3 * D), BF),
            pltpu.VMEM((D, D), BF),
            pltpu.VMEM((256, D), F32),
            pltpu.VMEM((256, 128), F32),
            pltpu.VMEM((SEQ, 8, D), BF),
            pltpu.VMEM((SEQ, 8, D), BF),
            pltpu.VMEM((256, 256), F32),
            pltpu.VMEM((D, 256), F32),
            pltpu.VMEM((SEQ, 8, D), BF),
            pltpu.VMEM((SEQ, 8, D), BF),
            pltpu.VMEM((256, D), BF),
            pltpu.VMEM((256, D), BF),
            pltpu.SemaphoreType.DMA((9,)),
            pltpu.SemaphoreType.DMA((4,)),
            pltpu.SemaphoreType.DMA((4,)),
            pltpu.SemaphoreType.DMA((76,)),
            pltpu.SemaphoreType.DMA((76,)),
        ],
        compiler_params=pltpu.CompilerParams(
            collective_id=0, has_side_effects=True, vmem_limit_bytes=VMEM_LIMIT
        ),
        name="whole",
    )(*args)


def per_device(
    hidden_in,
    qkv_spatial,
    qkv_temporal,
    grad_out,
    grad_temporal,
    gate_spatial,
    modulation,
    w_out_spatial,
    w_qkv_temporal,
):
    rows = jnp.concatenate([gate_spatial, modulation[0]], axis=0).astype(F32)
    grad_hidden, grad_qkv_s, grad_w_out, grad_w_qkv = whole_call(
        w_out_spatial.reshape(18, 8, D),
        w_qkv_temporal.reshape(18, 8, 3 * D),
        qkv_temporal.reshape(SEQ, 8, 3 * D),
        grad_temporal.reshape(SEQ, 8, D),
        qkv_spatial.reshape(256, 3 * D),
        hidden_in.reshape(256, D),
        grad_out.reshape(256, D),
        rows,
    )
    return (
        grad_hidden.reshape(hidden_in.shape),
        grad_qkv_s.reshape(qkv_spatial.shape),
        grad_w_out,
        grad_w_qkv,
    )


def solution(mesh):
    in_specs = (
        P("dp", "seq", None, None),
        P("dp", "seq", None, None),
        P("dp", "seq", None, None),
        P("dp", "seq", None, None),
        P("dp", "seq", None, None),
        P("dp", None),
        P("dp", None, None),
        P("dp", None),
        P("dp", None),
    )
    out_specs = (
        P("dp", "seq", None, None),
        P("dp", "seq", None, None),
        P("dp", "seq"),
        P("dp", "seq"),
    )
    return jax.shard_map(
        per_device, mesh=mesh, in_specs=in_specs, out_specs=out_specs, check_vma=False
    )
```

```python
import functools
import math

import jax
import jax.numpy as jnp
from jax import lax
from jax.experimental import pallas as pl
from jax.experimental.pallas import tpu as pltpu
from jax.sharding import PartitionSpec as P

HEADS = 16
D = 1152
SEQ = 32
DP = 8
EPSILON = 1e-06
VMEM_LIMIT = 56 * 1024 * 1024
BF = jnp.bfloat16
F32 = jnp.float32


SCALE = 1.0 / math.sqrt(D // HEADS)
LOG2E = math.log2(math.e)


def nt(a, b):
    return lax.dot_general(a, b, (((1,), (1,)), ((), ())), preferred_element_type=F32)


def tn(a, b):
    return lax.dot_general(a, b, (((0,), (0,)), ((), ())), preferred_element_type=F32)


def nn(a, b):
    return jnp.dot(a, b, preferred_element_type=F32)


def window(h):
    chunk = jnp.minimum(h * 9 // 16, 7)
    lane = lax.broadcasted_iota(jnp.int32, (1, 256), 1) + chunk * 128 - h * 72
    keep = jnp.where(jnp.logical_and(lane >= 0, lane < 72), 1.0, 0.0).astype(BF)
    return chunk * 128, keep


def head_probs(q, k, bias):
    s = nt(q, k)
    if bias is not None:
        s = s + bias
    top = jnp.max(s, axis=-1, keepdims=True)
    e = jnp.exp2((s - top) * (SCALE * LOG2E))
    return e * (1.0 / jnp.sum(e, axis=-1, keepdims=True))


def forward_head(load, add, h):
    c, keep = window(h)
    p = head_probs(load(0, c) * keep, load(1, c), None)
    add(0, c, nn(p.astype(BF), load(2, c) * keep))


def backward_head(load, add, h, bias):
    c, keep = window(h)
    q, k, v, g = load(0, c), load(1, c), load(2, c), load(3, c)
    qm, km, gm = q * keep, k * keep, g * keep
    p = head_probs(qm, k, bias)
    pb = p.astype(BF)
    dp = nt(gm, v)
    delta = jnp.sum(dp * p, axis=-1, keepdims=True)
    ds = (p * ((dp - delta) * SCALE)).astype(BF)
    add(2, c, tn(pb, gm))
    add(0, c, nn(ds, km))
    add(1, c, tn(ds, qm))


def columns(j, c):
    return pl.ds(pl.multiple_of(j * D + c, 128), 256)


def adder(ref):
    def add(j, c, value):
        at = columns(j, c)
        ref[:, at] = ref[:, at] + value.astype(BF)

    return add


def flat_loader(qkv_ref, g_ref):
    def load(j, c):
        return qkv_ref[:, columns(j, c)] if j < 3 else g_ref[:, columns(0, c)]

    return load


def block_loader(qkv_ref, g_ref):
    def load(j, c):
        x = qkv_ref[:, :, columns(j, c)] if j < 3 else g_ref[:, :, columns(0, c)]
        return x.reshape(256, 256)

    return load


def position():
    s = lax.axis_index("seq")
    d = lax.axis_index("dp")
    return dict(s=s, d=d, core=s % 2, zlo=(s // 2) % 4, x=s // 8, y=d % 4, zhi=d // 4)


def rcopy(src, dst, ssem, rsem, ps, pd):
    return pltpu.make_async_remote_copy(
        src_ref=src,
        dst_ref=dst,
        send_sem=ssem,
        recv_sem=rsem,
        device_id={"seq": ps, "dp": pd},
        device_id_type=pl.DeviceIdType.MESH,
    )


def greet(ps, pd):
    pl.semaphore_signal(
        pltpu.get_barrier_semaphore(),
        inc=1,
        device_id={"seq": ps, "dp": pd},
        device_id_type=pl.DeviceIdType.MESH,
    )


def a2a_start(p, pairs, ssems, rsems):
    def body(k, carry):
        peer = (p["s"] + k) % SEQ
        for i, (src, dst) in enumerate(pairs):
            rcopy(src.at[peer], dst.at[p["s"]], ssems.at[i], rsems.at[i], peer, p["d"]).start()
        return carry

    lax.fori_loop(1, SEQ, body, 0)


def a2a_wait(p, pairs, ssems, rsems):
    for i, (src, dst) in enumerate(pairs):
        part = pl.ds(0, SEQ - 1)
        rcopy(
            src.at[part], dst.at[part], ssems.at[i], rsems.at[i], (p["s"] + 1) % SEQ, p["d"]
        ).wait()


def greet_seq(p):
    def body(k, carry):
        greet((p["s"] + k) % SEQ, p["d"])
        return carry

    lax.fori_loop(1, SEQ, body, 0)


ROWS = 144
QX, OX = 8 * 128, 3 * 128
CZ = 256
LANES = 128


def x_start(xx):
    q = xx * 27 // 4
    return q - xx // 3, xx * 2


def z_start(ss):
    xx = ss // 8
    q0, o0 = x_start(xx)
    q = ss * 27 // 32
    q = q - ss // 31
    o = ss * 9 // 32
    o = jnp.minimum(o, o0 + 1)
    return q - q0, o - o0


class Reducer:
    def __init__(self, p, which, width, cover, bufs, sems):
        self.p, self.which, self.width, self.cover = p, which, width, cover
        self.size = width // SEQ
        self.lhs_t, self.mine, self.from_core, self.b1 = bufs[:4]
        self.part, self.b2, self.total, self.zout, self.zbuf = bufs[4:]
        self.pieces = [
            (j, j * cover, min(cover, width - j * cover)) for j in range(-(-width // cover))
        ]
        self.csend, self.crecv, self.s1send, self.s1recv = sems[:4]
        self.s2send, self.s2recv, self.zsend, self.zrecv = sems[4:]
        y, x, s = p["y"], p["x"], p["s"]
        self.order = [(y + k) % 4 for k in (1, 2, 3, 0)]
        self.y_to = [p["zhi"] * 4 + r for r in self.order[:3]]
        self.xs = [(x + k) % 4 for k in (1, 2, 3)]
        self.x_to = [xx * 8 + s % 8 for xx in self.xs]

    def cols(self, xx, t=0, size=None):
        first = x_start(xx)[self.which] * 128
        return pl.ds(pl.multiple_of(first + t, 128), self.cover if size is None else size)

    def core_copy(self, i):
        r = self.order[i]
        p = self.p
        return rcopy(
            self.mine.at[r],
            self.from_core.at[r],
            self.csend.at[i],
            self.crecv.at[i],
            p["s"] + 1 - 2 * p["core"],
            p["d"],
        )

    def first_y(self, i):
        return [
            rcopy(
                self.mine.at[self.order[i], :, pl.ds(at, size)],
                self.b1.at[i * 4 + j, :, pl.ds(0, size)],
                self.s1send.at[i * 4 + j],
                self.s1recv.at[i * 4 + j],
                self.p["s"],
                self.y_to[i],
            )
            for j, at, size in self.pieces
        ]

    def first_x(self, k, i):
        r = self.order[i]
        return rcopy(
            self.mine.at[r, :, self.cols(self.xs[k])],
            self.b1.at[k * 4 + r],
            self.s1send.at[k * 4 + i],
            self.s1recv.at[k * 4 + i],
            self.x_to[k],
            self.p["d"],
        )

    def second_x(self, k):
        return rcopy(
            self.mine.at[self.p["y"], :, self.cols(self.xs[k])],
            self.b2.at[k],
            self.s2send.at[k],
            self.s2recv.at[k],
            self.x_to[k],
            self.p["d"],
        )

    def second_y(self, i):
        return rcopy(
            self.part.at[self.order[i]],
            self.b2.at[i],
            self.s2send.at[i],
            self.s2recv.at[i],
            self.p["s"],
            self.y_to[i],
        )

    def z_target(self, i):
        p = self.p
        ss = p["x"] * 8 + i
        pd = p["core"] * 4 + p["y"]
        z_me = p["zhi"] * 4 + p["zlo"]
        return ss, pd, self.zout.at[i], z_me

    def z_copy(self, i):
        ss, pd, src, z_me = self.z_target(i)
        return rcopy(src, self.zbuf.at[z_me], self.zsend.at[i], self.zrecv.at[z_me], ss, pd)

    def z_local(self, i):
        ss, pd, src, z_me = self.z_target(i)
        return pltpu.make_async_copy(src, self.zbuf.at[z_me], self.zrecv.at[z_me])

    def own_product(self, r, rhs_ref):
        block = self.p["core"] * 4 + r
        lhs = self.lhs_t[pl.ds(pl.multiple_of(block * ROWS, 16), ROWS), :]
        step = self.width // 9

        def body(t, carry):
            at = pl.ds(pl.multiple_of(t * step, 128), step)
            value = nn(lhs, rhs_ref[:, at]) * GRAD_SCALE
            self.mine[r, :, at] = (value + self.from_core[r, :, at].astype(F32)).astype(BF)
            return carry

        lax.fori_loop(0, 9, body, 0)

    def start(self, load_lhs, rhs_ref):
        def turn(t, carry):
            at = pl.ds(pl.multiple_of(t * 128, 128), 128)
            self.lhs_t[at, :] = load_lhs(at).T
            return carry

        lax.fori_loop(0, 9, turn, 0)
        half = pl.ds(pl.multiple_of((1 - self.p["core"]) * 4 * ROWS, 16), 4 * ROWS)
        step = self.width // 9

        def body(t, carry):
            at = pl.ds(pl.multiple_of(t * step, 128), step)
            value = (nn(self.lhs_t[half, :], rhs_ref[:, at]) * GRAD_SCALE).astype(BF)
            self.mine[:, :, at] = value.reshape(4, ROWS, step)
            return carry

        lax.fori_loop(0, 9, body, 0)
        for i in range(4):
            self.core_copy(i).start()

    def first(self, rhs_ref):
        core = self.p["core"]
        for i, r in enumerate(self.order):
            self.core_copy(i).wait()
            self.own_product(r, rhs_ref)

            if i < 3:

                @pl.when(core == 0)
                def _():
                    for c in self.first_y(i):
                        c.start()

            @pl.when(core == 1)
            def _():
                for k in range(3):
                    self.first_x(k, i).start()

    def second(self):
        p = self.p
        y = p["y"]

        @pl.when(p["core"] == 0)
        def _():
            for i in range(3):
                for c in self.first_y(i):
                    c.wait_recv()
            n = self.cover // 128

            def body(t, carry):
                at = pl.ds(pl.multiple_of(t * 128, 128), 128)
                there = pl.ds(pl.multiple_of(t % n * 128, 128), 128)
                total = self.mine[y, :, at].astype(F32)
                for i in range(3):
                    total = total + self.b1[i * 4 + t // n, :, there].astype(F32)
                self.mine[y, :, at] = total.astype(BF)
                return carry

            lax.fori_loop(0, self.width // 128, body, 0, unroll=9)
            for k in range(3):
                self.second_x(k).start()

        @pl.when(p["core"] == 1)
        def _():
            for i, r in enumerate(self.order):
                for k in range(3):
                    self.first_x(k, i).wait_recv()

                def body(t, carry):
                    at = pl.ds(pl.multiple_of(t * 128, 128), 128)
                    total = self.mine[r, :, self.cols(p["x"], t * 128, 128)].astype(F32)
                    for k in range(3):
                        total = total + self.b1[k * 4 + r, :, at].astype(F32)
                    self.part[r, :, at] = total.astype(BF)
                    return carry

                lax.fori_loop(0, self.cover // 128, body, 0, unroll=True)
                if i < 3:
                    self.second_y(i).start()

    def third(self):
        p = self.p
        y, x, core = p["y"], p["x"], p["core"]

        def finish(load):
            def body(t, carry):
                at = pl.ds(pl.multiple_of(t * 128, 128), 128)
                total = load(t).astype(F32)
                for k in range(3):
                    total = total + self.b2[k, :, at].astype(F32)
                self.total[:, at] = total.astype(BF)
                return carry

            lax.fori_loop(0, self.cover // 128, body, 0, unroll=True)

        @pl.when(core == 0)
        def _():
            for k in range(3):
                self.second_x(k).wait_recv()
            finish(lambda t: self.mine[y, :, self.cols(x, t * 128, 128)])

        @pl.when(core == 1)
        def _():
            for i in range(3):
                self.second_y(i).wait_recv()
            finish(lambda t: self.part[y, :, pl.ds(pl.multiple_of(t * 128, 128), 128)])

        def pack(i, carry):
            ss = x * 8 + i
            at = z_start(ss)[self.which]
            skip = ss * self.size - (x_start(x)[self.which] + at) * 128
            value = self.total[:, pl.ds(pl.multiple_of(at * 128, 128), CZ)].astype(F32)
            self.zout[i] = pltpu.roll(value, (CZ - skip) % CZ, 1)[:, :LANES].astype(BF)
            return carry

        lax.fori_loop(0, 8, pack, 0, unroll=4)
        for i in range(8):
            ss, pd, _, _ = self.z_target(i)
            is_me = jnp.logical_and(ss == p["s"], pd == p["d"])

            @pl.when(jnp.logical_not(is_me))
            def _():
                self.z_copy(i).start()

            @pl.when(is_me)
            def _():
                self.z_local(i).start()

    def last(self, out_ref):
        for z in range(8):
            pltpu.make_async_copy(self.zbuf.at[z], self.zbuf.at[z], self.zrecv.at[z]).wait()
        total = self.zbuf[0].astype(F32)
        for z in range(1, 8):
            total = total + self.zbuf[z].astype(F32)
        out_ref[...] = total[:, : self.size]

    def drain(self):
        p = self.p

        @pl.when(p["core"] == 0)
        def _():
            for i in range(3):
                for c in self.first_y(i):
                    c.wait_send()
                self.second_x(i).wait_send()

        @pl.when(p["core"] == 1)
        def _():
            for k in range(3):
                for i in range(4):
                    self.first_x(k, i).wait_send()
                self.second_y(k).wait_send()

        for i in range(8):
            ss, pd, _, _ = self.z_target(i)

            @pl.when(jnp.logical_or(ss != p["s"], pd != p["d"]))
            def _():
                self.z_copy(i).wait_send()


def reducer_scratch(width, cover):
    bufs = [
        pltpu.VMEM((D, 256), BF),
        pltpu.VMEM((4, ROWS, width), BF),
        pltpu.VMEM((4, ROWS, width), BF),
        pltpu.VMEM((12, ROWS, cover), BF),
        pltpu.VMEM((4, ROWS, cover), BF),
        pltpu.VMEM((3, ROWS, cover), BF),
        pltpu.VMEM((ROWS, cover), BF),
        pltpu.VMEM((8, ROWS, LANES), BF),
        pltpu.VMEM((8, ROWS, LANES), BF),
    ]
    sems = [pltpu.SemaphoreType.DMA((n,)) for n in (4, 4, 12, 12, 3, 3, 8, 8)]
    return bufs + sems


GRAD_SCALE = 1.0 / math.sqrt(DP * SEQ * 256)


SPLIT = 1536
WA, WB = SPLIT // 4, (4 * D - SPLIT) // 4


def whole_kernel(
    w_out_ref,
    w_qkv_ref,
    qkv_ref,
    g_ref,
    spatial_hbm,
    hidden_hbm,
    gout_hbm,
    gate_ref,
    modulation_ref,
    hidden_out,
    spatial_out,
    w_out_out,
    w_qkv_out,
    *scratch,
):
    (
        wall_ref,
        qkvm_ref,
        gm_ref,
        spatial_ref,
        hidden_ref,
        gout_ref,
        attended_ref,
        gqkv_ref,
        wout_ref,
        unit_ref,
        std_ref,
        normed_ref,
        normedm_ref,
        bias_ref,
        gnt_ref,
        gn_ref,
        gnm_ref,
        proj_ref,
        gatt_ref,
        rows_ref,
        lsem,
        asend,
        arecv,
        wsend,
        wrecv,
    ) = scratch[34:]
    p = position()
    s, d, x, y, core, zhi = p["s"], p["d"], p["x"], p["y"], p["core"], p["zhi"]
    own = [
        pltpu.make_async_copy(w_out_ref, wall_ref.at[d, :, :, pl.ds(0, D)], lsem.at[0]),
        pltpu.make_async_copy(w_qkv_ref, wall_ref.at[d, :, :, pl.ds(D, 3 * D)], lsem.at[4]),
        pltpu.make_async_copy(spatial_hbm, spatial_ref, lsem.at[5]),
        pltpu.make_async_copy(hidden_hbm, hidden_ref, lsem.at[6]),
        pltpu.make_async_copy(gout_hbm, gout_ref, lsem.at[7]),
        pltpu.make_async_copy(qkv_ref.at[s], qkvm_ref.at[s], lsem.at[1]),
        pltpu.make_async_copy(g_ref.at[s], gm_ref.at[s], lsem.at[2]),
    ]
    for c in own:
        c.start()
    greet_seq(p)
    far = (d + 4) % DP
    y_to = [zhi * 4 + (y + k) % 4 for k in (1, 2, 3)]
    y_from = [zhi * 4 + (y + 4 - k) % 4 for k in (1, 2, 3)]
    y_far = [(1 - zhi) * 4 + (y + 4 - k) % 4 for k in (1, 2, 3)]
    x_to = [((x + k) % 4) * 8 + s % 8 for k in (1, 2, 3)]
    x_from = [(x + 4 - k) % 4 for k in (1, 2, 3)]
    sibling = s + 1 - 2 * core
    for peer in y_to:
        greet(s, peer)
    for i in range(8):
        greet(x * 8 + i, (1 - zhi) * 4 + y)
    pl.semaphore_wait(pltpu.get_barrier_semaphore(), SEQ - 1 + 3 + 8)
    own[0].wait()
    own[1].wait()

    rows = pl.ds(core * 9, 9)
    other_rows = pl.ds((1 - core) * 9, 9)

    def col_a(xx):
        return pl.ds(pl.multiple_of(xx * WA, 128), WA)

    def col_b(xx):
        return pl.ds(pl.multiple_of(SPLIT + xx * WB, 128), WB)

    all_b = pl.ds(SPLIT, 4 * WB)
    sent = []
    expected = []

    def send(dd, cols, sem, ps, pd):
        ref = wall_ref.at[dd, rows, :, cols]
        c = rcopy(ref, ref, wsend.at[sem], wrecv.at[sem], ps, pd)
        c.start()
        sent.append(c)

    def arrived(dd, cols, sem, which=None):
        ref = wall_ref.at[dd, rows if which is None else which, :, cols]
        rcopy(ref, ref, wsend.at[sem], wrecv.at[sem], s, far).wait_recv()

    def hand_on(dd, cols, sem):
        send(dd, cols, sem, sibling, d)
        expected.append((dd, cols, sem))

    send(d, col_b(x), 56, s, far)
    send(d, col_a(x), 0, s, far)
    for k in range(3):
        send(d, col_a(x), 1 + k, s, y_to[k])
    for k in range(3):
        send(d, all_b, 60 + k, s, y_to[k])
    pairs = [(qkv_ref, qkvm_ref), (g_ref, gm_ref)]
    a2a_start(p, pairs, asend, arecv)

    arrived(far, col_b(x), 56)
    for k in range(3):
        send(far, col_b(x), 57 + k, x_to[k], d)
    arrived(far, col_a(x), 0)
    for k in range(3):
        send(far, col_a(x), 4 + k, s, y_to[k])
    hand_on(far, col_b(x), 66)

    rows_ref[0:1, :] = gate_ref[...].astype(F32)
    rows_ref[1:3, :] = modulation_ref[...].astype(F32)
    attended_ref[...] = jnp.zeros_like(attended_ref)
    own[2].wait()

    def spatial(h, carry):
        forward_head(flat_loader(spatial_ref, None), adder(attended_ref), h)
        return carry

    lax.fori_loop(0, HEADS, spatial, 0, unroll=2)

    for k in range(3):
        arrived(far, col_b(x_from[k]), 57 + k)
    for k in range(3):
        send(far, all_b, 63 + k, s, y_to[k])
    for k in range(3):
        hand_on(far, col_b(x_from[k]), 67 + k)
    sources = [far] + y_from + y_far
    for j, dd in enumerate(sources):
        if j:
            arrived(dd, col_a(x), j)
        for k in range(3):
            send(dd, col_a(x), 7 + j * 3 + k, x_to[k], d)
        hand_on(dd, col_a(x), 28 + j)
    for k in range(3):
        arrived(y_from[k], all_b, 60 + k)
        hand_on(y_from[k], all_b, 70 + k)
    for j, dd in enumerate(sources):
        for k in range(3):
            arrived(dd, col_a(x_from[k]), 7 + j * 3 + k)
            hand_on(dd, col_a(x_from[k]), 35 + j * 3 + k)
    for k in range(3):
        arrived(y_far[k], all_b, 63 + k)
        hand_on(y_far[k], all_b, 73 + k)

    at = lax.broadcasted_iota(jnp.int32, (256, 256), 0) % 8
    to = lax.broadcasted_iota(jnp.int32, (256, 256), 1) % 8
    bias_ref[...] = jnp.where(at == to, 0.0, -1e30)
    gqkv_ref[...] = jnp.zeros_like(gqkv_ref)

    own[3].wait()
    for dd, cols, sem in expected:
        if sem < 66:
            arrived(dd, cols, sem, other_rows)

    def assemble(dd, carry):
        at = pl.ds(pl.multiple_of(dd * ROWS, 16), ROWS)
        wout_ref[at, :] = wall_ref[dd, :, :, :D].reshape(ROWS, D)
        return carry

    lax.fori_loop(0, DP, assemble, 0)

    def project(t, carry):
        at = pl.ds(pl.multiple_of(t * 384, 128), 384)
        unit_ref[:, at] = hidden_ref[:, at].astype(F32) + rows_ref[0:1, at] * nn(
            attended_ref[...], wout_ref[:, at]
        )
        return carry

    lax.fori_loop(0, 3, project, 0)

    def normalise(t, carry):
        at = pl.ds(pl.multiple_of(t * 32, 32), 32)
        residual = unit_ref[at, :]
        centered = residual - jnp.mean(residual, axis=-1, keepdims=True)
        inv_std = lax.rsqrt(jnp.mean(centered * centered, axis=-1, keepdims=True) + EPSILON)
        unit = centered * inv_std
        unit_ref[at, :] = unit
        std_ref[at, :] = jnp.broadcast_to(inv_std, (32, 128))
        normed = unit * (1.0 + rows_ref[2:3, :]) + rows_ref[1:2, :]
        normed_ref[pl.ds(t * 4, 4)] = normed.reshape(4, 8, D).astype(BF)
        return carry

    lax.fori_loop(0, 8, normalise, 0)
    own_normed = pltpu.make_async_copy(normed_ref.at[s], normedm_ref.at[s], lsem.at[3])
    own_normed.start()
    normed_pair = [(normed_ref, normedm_ref)]
    a2a_start(p, normed_pair, asend.at[pl.ds(2, 1)], arecv.at[pl.ds(2, 1)])

    a2a_wait(p, pairs, asend, arecv)
    own[5].wait()
    own[6].wait()

    def temporal(h, carry):
        backward_head(block_loader(qkvm_ref, gm_ref), adder(gqkv_ref), h, bias_ref[...])
        return carry

    lax.fori_loop(0, HEADS, temporal, 0, unroll=4)

    for dd, cols, sem in expected:
        if sem >= 66:
            arrived(dd, cols, sem, other_rows)

    def back_project(half, carry):
        at = pl.ds(pl.multiple_of(half * 4 * ROWS, 16), 4 * ROWS)
        weights = wall_ref[pl.ds(half * 4, 4), :, :, D:].reshape(4 * ROWS, 3 * D)
        gnt_ref[at, :] = nt(weights, gqkv_ref[...])
        return carry

    lax.fori_loop(0, 2, back_project, 0)

    def turn(t, carry):
        at = pl.ds(pl.multiple_of(t * 128, 128), 128)
        gn_ref[:, :, at] = gnt_ref[at, :].T.reshape(SEQ, 8, 128).astype(BF)
        return carry

    lax.fori_loop(0, 9, turn, 0)
    own_back = pltpu.make_async_copy(gn_ref.at[s], gnm_ref.at[s], lsem.at[8])
    own_back.start()
    back_pair = [(gn_ref, gnm_ref)]
    a2a_start(p, back_pair, asend.at[pl.ds(3, 1)], arecv.at[pl.ds(3, 1)])
    a2a_wait(p, normed_pair, asend.at[pl.ds(2, 1)], arecv.at[pl.ds(2, 1)])
    own_normed.wait()

    rq = Reducer(p, 0, 3 * D, QX, scratch[0:9], scratch[9:17])
    ro = Reducer(p, 1, D, OX, scratch[17:26], scratch[26:34])
    rq.start(lambda at: normedm_ref[:, :, at].reshape(256, 128), gqkv_ref)
    rq.first(gqkv_ref)

    a2a_wait(p, back_pair, asend.at[pl.ds(3, 1)], arecv.at[pl.ds(3, 1)])
    own_back.wait()
    own[4].wait()

    def norm_backward(t, carry):
        at = pl.ds(pl.multiple_of(t * 32, 32), 32)
        unit = unit_ref[at, :]
        inv_std = std_ref[at, 0:1]
        grad_normed = gnm_ref[pl.ds(t * 4, 4)].astype(F32).reshape(32, D)
        grad_hat = grad_normed * (1.0 + rows_ref[2:3, :])
        grad_resid = gout_ref[at, :].astype(F32) + inv_std * (
            grad_hat
            - jnp.mean(grad_hat, axis=-1, keepdims=True)
            - unit * jnp.mean(grad_hat * unit, axis=-1, keepdims=True)
        )
        hidden_out[at, :] = grad_resid.astype(BF)
        proj_ref[at, :] = (rows_ref[0:1, :] * grad_resid).astype(BF)
        return carry

    lax.fori_loop(0, 8, norm_backward, 0)
    ro.start(lambda at: attended_ref[:, at], proj_ref)

    def attend_grad(t, carry):
        at = pl.ds(pl.multiple_of(t * 384, 128), 384)
        gatt_ref[:, at] = nt(proj_ref[...], wout_ref[at, :]).astype(BF)
        return carry

    lax.fori_loop(0, 3, attend_grad, 0)
    ro.first(proj_ref)
    spatial_out[...] = jnp.zeros_like(spatial_out)

    def spatial_back(h, carry):
        backward_head(flat_loader(spatial_ref, gatt_ref), adder(spatial_out), h, None)
        return carry

    lax.fori_loop(0, HEADS // 2, spatial_back, 0, unroll=2)
    rq.second()
    lax.fori_loop(HEADS // 2, HEADS, spatial_back, 0, unroll=2)
    rq.third()
    ro.second()
    ro.third()
    rq.last(w_qkv_out)
    ro.last(w_out_out)
    for c in sent:
        c.wait_send()
    rq.drain()
    ro.drain()


def whole_call(*args):
    any_space = pl.BlockSpec(memory_space=pl.ANY)
    vmem = pl.BlockSpec(memory_space=pltpu.VMEM)
    return pl.pallas_call(
        whole_kernel,
        out_shape=(
            pltpu.VMEM((256, D), BF),
            pltpu.VMEM((256, 3 * D), BF),
            pltpu.VMEM((ROWS, 36), F32),
            pltpu.VMEM((ROWS, 108), F32),
        ),
        in_specs=[any_space] * 7 + [vmem] * 2,
        out_specs=[vmem] * 4,
        scratch_shapes=reducer_scratch(3 * D, QX)
        + reducer_scratch(D, OX)
        + [
            pltpu.VMEM((DP, 18, 8, 4 * D), BF),
            pltpu.VMEM((SEQ, 8, 3 * D), BF),
            pltpu.VMEM((SEQ, 8, D), BF),
            pltpu.VMEM((256, 3 * D), BF),
            pltpu.VMEM((256, D), BF),
            pltpu.VMEM((256, D), BF),
            pltpu.VMEM((256, D), BF),
            pltpu.VMEM((256, 3 * D), BF),
            pltpu.VMEM((D, D), BF),
            pltpu.VMEM((256, D), F32),
            pltpu.VMEM((256, 128), F32),
            pltpu.VMEM((SEQ, 8, D), BF),
            pltpu.VMEM((SEQ, 8, D), BF),
            pltpu.VMEM((256, 256), F32),
            pltpu.VMEM((D, 256), F32),
            pltpu.VMEM((SEQ, 8, D), BF),
            pltpu.VMEM((SEQ, 8, D), BF),
            pltpu.VMEM((256, D), BF),
            pltpu.VMEM((256, D), BF),
            pltpu.VMEM((3, D), F32),
            pltpu.SemaphoreType.DMA((9,)),
            pltpu.SemaphoreType.DMA((4,)),
            pltpu.SemaphoreType.DMA((4,)),
            pltpu.SemaphoreType.DMA((76,)),
            pltpu.SemaphoreType.DMA((76,)),
        ],
        compiler_params=pltpu.CompilerParams(
            collective_id=0, has_side_effects=True, vmem_limit_bytes=VMEM_LIMIT
        ),
        name="whole",
    )(*args)


def per_device(
    hidden_in,
    qkv_spatial,
    qkv_temporal,
    grad_out,
    grad_temporal,
    gate_spatial,
    modulation,
    w_out_spatial,
    w_qkv_temporal,
):
    grad_hidden, grad_qkv_s, grad_w_out, grad_w_qkv = whole_call(
        w_out_spatial.reshape(18, 8, D),
        w_qkv_temporal.reshape(18, 8, 3 * D),
        qkv_temporal.reshape(SEQ, 8, 3 * D),
        grad_temporal.reshape(SEQ, 8, D),
        qkv_spatial.reshape(256, 3 * D),
        hidden_in.reshape(256, D),
        grad_out.reshape(256, D),
        gate_spatial,
        modulation.reshape(2, D),
    )
    return (
        grad_hidden.reshape(hidden_in.shape),
        grad_qkv_s.reshape(qkv_spatial.shape),
        grad_w_out,
        grad_w_qkv,
    )


def solution(mesh):
    in_specs = (
        P("dp", "seq", None, None),
        P("dp", "seq", None, None),
        P("dp", "seq", None, None),
        P("dp", "seq", None, None),
        P("dp", "seq", None, None),
        P("dp", None),
        P("dp", None, None),
        P("dp", None),
        P("dp", None),
    )
    out_specs = (
        P("dp", "seq", None, None),
        P("dp", "seq", None, None),
        P("dp", "seq"),
        P("dp", "seq"),
    )
    return jax.shard_map(
        per_device, mesh=mesh, in_specs=in_specs, out_specs=out_specs, check_vma=False
    )
```

```python
import functools
import math

import jax
import jax.numpy as jnp
from jax import lax
from jax.experimental import pallas as pl
from jax.experimental.pallas import tpu as pltpu
from jax.sharding import PartitionSpec as P

HEADS = 16
D = 1152
SEQ = 32
DP = 8
EPSILON = 1e-06
VMEM_LIMIT = 56 * 1024 * 1024
BF = jnp.bfloat16
F32 = jnp.float32


SCALE = 1.0 / math.sqrt(D // HEADS)
LOG2E = math.log2(math.e)


def nt(a, b):
    return lax.dot_general(a, b, (((1,), (1,)), ((), ())), preferred_element_type=F32)


def tn(a, b):
    return lax.dot_general(a, b, (((0,), (0,)), ((), ())), preferred_element_type=F32)


def nn(a, b):
    return jnp.dot(a, b, preferred_element_type=F32)


def window(h):
    chunk = jnp.minimum(h * 9 // 16, 7)
    lane = lax.broadcasted_iota(jnp.int32, (1, 256), 1) + chunk * 128 - h * 72
    keep = jnp.where(jnp.logical_and(lane >= 0, lane < 72), 1.0, 0.0).astype(BF)
    return chunk * 128, keep


def head_probs(q, k, bias):
    s = nt(q, k)
    if bias is not None:
        s = s + bias
    top = jnp.max(s, axis=-1, keepdims=True)
    e = jnp.exp2((s - top) * (SCALE * LOG2E))
    return e * (1.0 / jnp.sum(e, axis=-1, keepdims=True))


def forward_head(load, add, h):
    c, keep = window(h)
    p = head_probs(load(0, c) * keep, load(1, c), None)
    add(0, c, nn(p.astype(BF), load(2, c) * keep))


def backward_head(load, add, h, bias):
    c, keep = window(h)
    q, k, v, g = load(0, c), load(1, c), load(2, c), load(3, c)
    qm, km, gm = q * keep, k * keep, g * keep
    p = head_probs(qm, k, bias)
    pb = p.astype(BF)
    dp = nt(gm, v)
    delta = jnp.sum(dp * p, axis=-1, keepdims=True)
    ds = (p * ((dp - delta) * SCALE)).astype(BF)
    add(2, c, tn(pb, gm))
    add(0, c, nn(ds, km))
    add(1, c, tn(ds, qm))


def columns(j, c):
    return pl.ds(pl.multiple_of(j * D + c, 128), 256)


def adder(ref):
    def add(j, c, value):
        at = columns(j, c)
        ref[:, at] = ref[:, at] + value.astype(BF)

    return add


def flat_loader(qkv_ref, g_ref):
    def load(j, c):
        return qkv_ref[:, columns(j, c)] if j < 3 else g_ref[:, columns(0, c)]

    return load


def block_loader(qkv_ref, g_ref):
    def load(j, c):
        x = qkv_ref[:, :, columns(j, c)] if j < 3 else g_ref[:, :, columns(0, c)]
        return x.reshape(256, 256)

    return load


def position():
    s = lax.axis_index("seq")
    d = lax.axis_index("dp")
    return dict(s=s, d=d, core=s % 2, zlo=(s // 2) % 4, x=s // 8, y=d % 4, zhi=d // 4)


def rcopy(src, dst, ssem, rsem, ps, pd):
    return pltpu.make_async_remote_copy(
        src_ref=src,
        dst_ref=dst,
        send_sem=ssem,
        recv_sem=rsem,
        device_id={"seq": ps, "dp": pd},
        device_id_type=pl.DeviceIdType.MESH,
    )


def greet(ps, pd):
    pl.semaphore_signal(
        pltpu.get_barrier_semaphore(),
        inc=1,
        device_id={"seq": ps, "dp": pd},
        device_id_type=pl.DeviceIdType.MESH,
    )


def a2a_start(p, pairs, ssems, rsems):
    def body(k, carry):
        peer = (p["s"] + k) % SEQ
        for i, (src, dst) in enumerate(pairs):
            rcopy(src.at[peer], dst.at[p["s"]], ssems.at[i], rsems.at[i], peer, p["d"]).start()
        return carry

    lax.fori_loop(1, SEQ, body, 0)


def a2a_wait(p, pairs, ssems, rsems):
    for i, (src, dst) in enumerate(pairs):
        part = pl.ds(0, SEQ - 1)
        rcopy(
            src.at[part], dst.at[part], ssems.at[i], rsems.at[i], (p["s"] + 1) % SEQ, p["d"]
        ).wait()


def greet_seq(p):
    def body(k, carry):
        greet((p["s"] + k) % SEQ, p["d"])
        return carry

    lax.fori_loop(1, SEQ, body, 0)


ROWS = 144
QX, OX = 8 * 128, 3 * 128
CZ = 256
LANES = 128


def x_start(xx):
    q = xx * 27 // 4
    return q - xx // 3, xx * 2


def z_start(ss):
    xx = ss // 8
    q0, o0 = x_start(xx)
    q = ss * 27 // 32
    q = q - ss // 31
    o = ss * 9 // 32
    o = jnp.minimum(o, o0 + 1)
    return q - q0, o - o0


class Reducer:
    def __init__(self, p, which, width, cover, bufs, sems):
        self.p, self.which, self.width, self.cover = p, which, width, cover
        self.size = width // SEQ
        self.lhs_t, self.mine, self.from_core, self.b1 = bufs[:4]
        self.part, self.b2, self.total, self.zout, self.zbuf = bufs[4:]
        self.pieces = [
            (j, j * cover, min(cover, width - j * cover)) for j in range(-(-width // cover))
        ]
        self.csend, self.crecv, self.s1send, self.s1recv = sems[:4]
        self.s2send, self.s2recv, self.zsend, self.zrecv = sems[4:]
        y, x, s = p["y"], p["x"], p["s"]
        self.order = [(y + k) % 4 for k in (1, 2, 3, 0)]
        self.y_to = [p["zhi"] * 4 + r for r in self.order[:3]]
        self.xs = [(x + k) % 4 for k in (1, 2, 3)]
        self.x_to = [xx * 8 + s % 8 for xx in self.xs]

    def cols(self, xx, t=0, size=None):
        first = x_start(xx)[self.which] * 128
        return pl.ds(pl.multiple_of(first + t, 128), self.cover if size is None else size)

    def core_copy(self, i):
        r = self.order[i]
        p = self.p
        return rcopy(
            self.mine.at[r],
            self.from_core.at[r],
            self.csend.at[i],
            self.crecv.at[i],
            p["s"] + 1 - 2 * p["core"],
            p["d"],
        )

    def first_y(self, i):
        return [
            rcopy(
                self.mine.at[self.order[i], :, pl.ds(at, size)],
                self.b1.at[i * 4 + j, :, pl.ds(0, size)],
                self.s1send.at[i * 4 + j],
                self.s1recv.at[i * 4 + j],
                self.p["s"],
                self.y_to[i],
            )
            for j, at, size in self.pieces
        ]

    def first_x(self, k, i):
        r = self.order[i]
        return rcopy(
            self.mine.at[r, :, self.cols(self.xs[k])],
            self.b1.at[k * 4 + r],
            self.s1send.at[k * 4 + i],
            self.s1recv.at[k * 4 + i],
            self.x_to[k],
            self.p["d"],
        )

    def second_x(self, k):
        return rcopy(
            self.mine.at[self.p["y"], :, self.cols(self.xs[k])],
            self.b2.at[k],
            self.s2send.at[k],
            self.s2recv.at[k],
            self.x_to[k],
            self.p["d"],
        )

    def second_y(self, i):
        return rcopy(
            self.part.at[self.order[i]],
            self.b2.at[i],
            self.s2send.at[i],
            self.s2recv.at[i],
            self.p["s"],
            self.y_to[i],
        )

    def z_target(self, i):
        p = self.p
        ss = p["x"] * 8 + i
        pd = p["core"] * 4 + p["y"]
        z_me = p["zhi"] * 4 + p["zlo"]
        return ss, pd, self.zout.at[i], z_me

    def z_copy(self, i):
        ss, pd, src, z_me = self.z_target(i)
        return rcopy(src, self.zbuf.at[z_me], self.zsend.at[i], self.zrecv.at[z_me], ss, pd)

    def z_local(self, i):
        ss, pd, src, z_me = self.z_target(i)
        return pltpu.make_async_copy(src, self.zbuf.at[z_me], self.zrecv.at[z_me])

    def own_product(self, r, rhs_ref):
        block = self.p["core"] * 4 + r
        lhs = self.lhs_t[pl.ds(pl.multiple_of(block * ROWS, 16), ROWS), :]
        step = self.width // 9

        def body(t, carry):
            at = pl.ds(pl.multiple_of(t * step, 128), step)
            value = nn(lhs, rhs_ref[:, at]) * GRAD_SCALE
            self.mine[r, :, at] = (value + self.from_core[r, :, at].astype(F32)).astype(BF)
            return carry

        lax.fori_loop(0, 9, body, 0, unroll=3)

    def start(self, load_lhs, rhs_ref):
        def turn(t, carry):
            at = pl.ds(pl.multiple_of(t * 128, 128), 128)
            self.lhs_t[at, :] = load_lhs(at).T
            return carry

        lax.fori_loop(0, 9, turn, 0, unroll=3)
        half = pl.ds(pl.multiple_of((1 - self.p["core"]) * 4 * ROWS, 16), 4 * ROWS)
        step = self.width // 9

        def body(t, carry):
            at = pl.ds(pl.multiple_of(t * step, 128), step)
            value = (nn(self.lhs_t[half, :], rhs_ref[:, at]) * GRAD_SCALE).astype(BF)
            self.mine[:, :, at] = value.reshape(4, ROWS, step)
            return carry

        lax.fori_loop(0, 9, body, 0, unroll=3)
        for i in range(4):
            self.core_copy(i).start()

    def first(self, rhs_ref):
        core = self.p["core"]
        for i, r in enumerate(self.order):
            self.core_copy(i).wait()
            self.own_product(r, rhs_ref)

            if i < 3:

                @pl.when(core == 0)
                def _():
                    for c in self.first_y(i):
                        c.start()

            @pl.when(core == 1)
            def _():
                for k in range(3):
                    self.first_x(k, i).start()

    def second(self):
        p = self.p
        y = p["y"]

        @pl.when(p["core"] == 0)
        def _():
            for i in range(3):
                for c in self.first_y(i):
                    c.wait_recv()
            n = self.cover // 128

            def body(t, carry):
                at = pl.ds(pl.multiple_of(t * 128, 128), 128)
                there = pl.ds(pl.multiple_of(t % n * 128, 128), 128)
                total = self.mine[y, :, at].astype(F32)
                for i in range(3):
                    total = total + self.b1[i * 4 + t // n, :, there].astype(F32)
                self.mine[y, :, at] = total.astype(BF)
                return carry

            lax.fori_loop(0, self.width // 128, body, 0, unroll=9)
            for k in range(3):
                self.second_x(k).start()

        @pl.when(p["core"] == 1)
        def _():
            for i, r in enumerate(self.order):
                for k in range(3):
                    self.first_x(k, i).wait_recv()

                def body(t, carry):
                    at = pl.ds(pl.multiple_of(t * 128, 128), 128)
                    total = self.mine[r, :, self.cols(p["x"], t * 128, 128)].astype(F32)
                    for k in range(3):
                        total = total + self.b1[k * 4 + r, :, at].astype(F32)
                    self.part[r, :, at] = total.astype(BF)
                    return carry

                lax.fori_loop(0, self.cover // 128, body, 0, unroll=True)
                if i < 3:
                    self.second_y(i).start()

    def third(self):
        p = self.p
        y, x, core = p["y"], p["x"], p["core"]

        def finish(load):
            def body(t, carry):
                at = pl.ds(pl.multiple_of(t * 128, 128), 128)
                total = load(t).astype(F32)
                for k in range(3):
                    total = total + self.b2[k, :, at].astype(F32)
                self.total[:, at] = total.astype(BF)
                return carry

            lax.fori_loop(0, self.cover // 128, body, 0, unroll=True)

        @pl.when(core == 0)
        def _():
            for k in range(3):
                self.second_x(k).wait_recv()
            finish(lambda t: self.mine[y, :, self.cols(x, t * 128, 128)])

        @pl.when(core == 1)
        def _():
            for i in range(3):
                self.second_y(i).wait_recv()
            finish(lambda t: self.part[y, :, pl.ds(pl.multiple_of(t * 128, 128), 128)])

        def pack(i, carry):
            ss = x * 8 + i
            at = z_start(ss)[self.which]
            skip = ss * self.size - (x_start(x)[self.which] + at) * 128
            value = self.total[:, pl.ds(pl.multiple_of(at * 128, 128), CZ)].astype(F32)
            self.zout[i] = pltpu.roll(value, (CZ - skip) % CZ, 1)[:, :LANES].astype(BF)
            return carry

        lax.fori_loop(0, 8, pack, 0, unroll=4)
        for i in range(8):
            ss, pd, _, _ = self.z_target(i)
            is_me = jnp.logical_and(ss == p["s"], pd == p["d"])

            @pl.when(jnp.logical_not(is_me))
            def _():
                self.z_copy(i).start()

            @pl.when(is_me)
            def _():
                self.z_local(i).start()

    def last(self, out_ref):
        for z in range(8):
            pltpu.make_async_copy(self.zbuf.at[z], self.zbuf.at[z], self.zrecv.at[z]).wait()
        total = self.zbuf[0].astype(F32)
        for z in range(1, 8):
            total = total + self.zbuf[z].astype(F32)
        out_ref[...] = total[:, : self.size]

    def drain(self):
        p = self.p

        @pl.when(p["core"] == 0)
        def _():
            for i in range(3):
                for c in self.first_y(i):
                    c.wait_send()
                self.second_x(i).wait_send()

        @pl.when(p["core"] == 1)
        def _():
            for k in range(3):
                for i in range(4):
                    self.first_x(k, i).wait_send()
                self.second_y(k).wait_send()

        for i in range(8):
            ss, pd, _, _ = self.z_target(i)

            @pl.when(jnp.logical_or(ss != p["s"], pd != p["d"]))
            def _():
                self.z_copy(i).wait_send()


def reducer_scratch(width, cover):
    bufs = [
        pltpu.VMEM((D, 256), BF),
        pltpu.VMEM((4, ROWS, width), BF),
        pltpu.VMEM((4, ROWS, width), BF),
        pltpu.VMEM((12, ROWS, cover), BF),
        pltpu.VMEM((4, ROWS, cover), BF),
        pltpu.VMEM((3, ROWS, cover), BF),
        pltpu.VMEM((ROWS, cover), BF),
        pltpu.VMEM((8, ROWS, LANES), BF),
        pltpu.VMEM((8, ROWS, LANES), BF),
    ]
    sems = [pltpu.SemaphoreType.DMA((n,)) for n in (4, 4, 12, 12, 3, 3, 8, 8)]
    return bufs + sems


GRAD_SCALE = 1.0 / math.sqrt(DP * SEQ * 256)


SPLIT = 1536
WA, WB = SPLIT // 4, (4 * D - SPLIT) // 4


def whole_kernel(
    w_out_ref,
    w_qkv_ref,
    qkv_ref,
    g_ref,
    spatial_hbm,
    hidden_hbm,
    gout_hbm,
    gate_ref,
    modulation_ref,
    hidden_out,
    spatial_out,
    w_out_out,
    w_qkv_out,
    *scratch,
):
    (
        wall_ref,
        qkvm_ref,
        gm_ref,
        spatial_ref,
        hidden_ref,
        gout_ref,
        attended_ref,
        gqkv_ref,
        wout_ref,
        unit_ref,
        std_ref,
        normed_ref,
        normedm_ref,
        bias_ref,
        gnt_ref,
        gn_ref,
        gnm_ref,
        proj_ref,
        gatt_ref,
        rows_ref,
        lsem,
        asend,
        arecv,
        wsend,
        wrecv,
    ) = scratch[34:]
    p = position()
    s, d, x, y, core, zhi = p["s"], p["d"], p["x"], p["y"], p["core"], p["zhi"]
    own = [
        pltpu.make_async_copy(w_out_ref, wall_ref.at[d, :, :, pl.ds(0, D)], lsem.at[0]),
        pltpu.make_async_copy(w_qkv_ref, wall_ref.at[d, :, :, pl.ds(D, 3 * D)], lsem.at[4]),
        pltpu.make_async_copy(spatial_hbm, spatial_ref, lsem.at[5]),
        pltpu.make_async_copy(hidden_hbm, hidden_ref, lsem.at[6]),
        pltpu.make_async_copy(gout_hbm, gout_ref, lsem.at[7]),
        pltpu.make_async_copy(qkv_ref.at[s], qkvm_ref.at[s], lsem.at[1]),
        pltpu.make_async_copy(g_ref.at[s], gm_ref.at[s], lsem.at[2]),
    ]
    for c in own:
        c.start()
    greet_seq(p)
    far = (d + 4) % DP
    y_to = [zhi * 4 + (y + k) % 4 for k in (1, 2, 3)]
    y_from = [zhi * 4 + (y + 4 - k) % 4 for k in (1, 2, 3)]
    y_far = [(1 - zhi) * 4 + (y + 4 - k) % 4 for k in (1, 2, 3)]
    x_to = [((x + k) % 4) * 8 + s % 8 for k in (1, 2, 3)]
    x_from = [(x + 4 - k) % 4 for k in (1, 2, 3)]
    sibling = s + 1 - 2 * core
    for peer in y_to:
        greet(s, peer)
    for i in range(8):
        greet(x * 8 + i, (1 - zhi) * 4 + y)
    pl.semaphore_wait(pltpu.get_barrier_semaphore(), SEQ - 1 + 3 + 8)
    own[0].wait()
    own[1].wait()

    rows = pl.ds(core * 9, 9)
    other_rows = pl.ds((1 - core) * 9, 9)

    def col_a(xx):
        return pl.ds(pl.multiple_of(xx * WA, 128), WA)

    def col_b(xx):
        return pl.ds(pl.multiple_of(SPLIT + xx * WB, 128), WB)

    all_b = pl.ds(SPLIT, 4 * WB)
    sent = []
    expected = []

    def send(dd, cols, sem, ps, pd):
        ref = wall_ref.at[dd, rows, :, cols]
        c = rcopy(ref, ref, wsend.at[sem], wrecv.at[sem], ps, pd)
        c.start()
        sent.append(c)

    def arrived(dd, cols, sem, which=None):
        ref = wall_ref.at[dd, rows if which is None else which, :, cols]
        rcopy(ref, ref, wsend.at[sem], wrecv.at[sem], s, far).wait_recv()

    def hand_on(dd, cols, sem):
        send(dd, cols, sem, sibling, d)
        expected.append((dd, cols, sem))

    send(d, col_b(x), 56, s, far)
    send(d, col_a(x), 0, s, far)
    for k in range(3):
        send(d, col_a(x), 1 + k, s, y_to[k])
    for k in range(3):
        send(d, all_b, 60 + k, s, y_to[k])
    pairs = [(qkv_ref, qkvm_ref), (g_ref, gm_ref)]
    a2a_start(p, pairs, asend, arecv)

    arrived(far, col_b(x), 56)
    for k in range(3):
        send(far, col_b(x), 57 + k, x_to[k], d)
    arrived(far, col_a(x), 0)
    for k in range(3):
        send(far, col_a(x), 4 + k, s, y_to[k])
    hand_on(far, col_b(x), 66)

    rows_ref[0:1, :] = gate_ref[...].astype(F32)
    rows_ref[1:3, :] = modulation_ref[...].astype(F32)
    attended_ref[...] = jnp.zeros_like(attended_ref)
    own[2].wait()

    def spatial(h, carry):
        forward_head(flat_loader(spatial_ref, None), adder(attended_ref), h)
        return carry

    lax.fori_loop(0, HEADS, spatial, 0, unroll=2)

    for k in range(3):
        arrived(far, col_b(x_from[k]), 57 + k)
    for k in range(3):
        send(far, all_b, 63 + k, s, y_to[k])
    for k in range(3):
        hand_on(far, col_b(x_from[k]), 67 + k)
    sources = [far] + y_from + y_far
    for j, dd in enumerate(sources):
        if j:
            arrived(dd, col_a(x), j)
        for k in range(3):
            send(dd, col_a(x), 7 + j * 3 + k, x_to[k], d)
        hand_on(dd, col_a(x), 28 + j)
    for j, dd in enumerate(sources):
        for k in range(3):
            arrived(dd, col_a(x_from[k]), 7 + j * 3 + k)
            hand_on(dd, col_a(x_from[k]), 35 + j * 3 + k)

    at = lax.broadcasted_iota(jnp.int32, (256, 256), 0) % 8
    to = lax.broadcasted_iota(jnp.int32, (256, 256), 1) % 8
    bias_ref[...] = jnp.where(at == to, 0.0, -1e30)
    gqkv_ref[...] = jnp.zeros_like(gqkv_ref)

    own[3].wait()
    for dd, cols, sem in expected:
        if sem < 66:
            arrived(dd, cols, sem, other_rows)

    def assemble(dd, carry):
        at = pl.ds(pl.multiple_of(dd * ROWS, 16), ROWS)
        wout_ref[at, :] = wall_ref[dd, :, :, :D].reshape(ROWS, D)
        return carry

    lax.fori_loop(0, DP, assemble, 0)

    def project(t, carry):
        at = pl.ds(pl.multiple_of(t * 384, 128), 384)
        unit_ref[:, at] = hidden_ref[:, at].astype(F32) + rows_ref[0:1, at] * nn(
            attended_ref[...], wout_ref[:, at]
        )
        return carry

    lax.fori_loop(0, 3, project, 0, unroll=True)

    def normalise(t, carry):
        at = pl.ds(pl.multiple_of(t * 32, 32), 32)
        residual = unit_ref[at, :]
        centered = residual - jnp.mean(residual, axis=-1, keepdims=True)
        inv_std = lax.rsqrt(jnp.mean(centered * centered, axis=-1, keepdims=True) + EPSILON)
        unit = centered * inv_std
        unit_ref[at, :] = unit
        std_ref[at, :] = jnp.broadcast_to(inv_std, (32, 128))
        normed = unit * (1.0 + rows_ref[2:3, :]) + rows_ref[1:2, :]
        normed_ref[pl.ds(t * 4, 4)] = normed.reshape(4, 8, D).astype(BF)
        return carry

    lax.fori_loop(0, 8, normalise, 0, unroll=2)
    own_normed = pltpu.make_async_copy(normed_ref.at[s], normedm_ref.at[s], lsem.at[3])
    own_normed.start()
    normed_pair = [(normed_ref, normedm_ref)]
    a2a_start(p, normed_pair, asend.at[pl.ds(2, 1)], arecv.at[pl.ds(2, 1)])

    for k in range(3):
        arrived(y_from[k], all_b, 60 + k)
        hand_on(y_from[k], all_b, 70 + k)
    for k in range(3):
        arrived(y_far[k], all_b, 63 + k)
        hand_on(y_far[k], all_b, 73 + k)
    a2a_wait(p, pairs, asend, arecv)
    own[5].wait()
    own[6].wait()

    def temporal(h, carry):
        backward_head(block_loader(qkvm_ref, gm_ref), adder(gqkv_ref), h, bias_ref[...])
        return carry

    lax.fori_loop(0, HEADS, temporal, 0, unroll=4)

    for dd, cols, sem in expected:
        if sem >= 66:
            arrived(dd, cols, sem, other_rows)

    def back_project(half, carry):
        at = pl.ds(pl.multiple_of(half * 4 * ROWS, 16), 4 * ROWS)
        weights = wall_ref[pl.ds(half * 4, 4), :, :, D:].reshape(4 * ROWS, 3 * D)
        gnt_ref[at, :] = nt(weights, gqkv_ref[...])
        return carry

    lax.fori_loop(0, 2, back_project, 0)

    def turn(t, carry):
        at = pl.ds(pl.multiple_of(t * 128, 128), 128)
        gn_ref[:, :, at] = gnt_ref[at, :].T.reshape(SEQ, 8, 128).astype(BF)
        return carry

    lax.fori_loop(0, 9, turn, 0, unroll=3)
    own_back = pltpu.make_async_copy(gn_ref.at[s], gnm_ref.at[s], lsem.at[8])
    own_back.start()
    back_pair = [(gn_ref, gnm_ref)]
    a2a_start(p, back_pair, asend.at[pl.ds(3, 1)], arecv.at[pl.ds(3, 1)])
    a2a_wait(p, normed_pair, asend.at[pl.ds(2, 1)], arecv.at[pl.ds(2, 1)])
    own_normed.wait()

    rq = Reducer(p, 0, 3 * D, QX, scratch[0:9], scratch[9:17])
    ro = Reducer(p, 1, D, OX, scratch[17:26], scratch[26:34])
    rq.start(lambda at: normedm_ref[:, :, at].reshape(256, 128), gqkv_ref)
    rq.first(gqkv_ref)

    a2a_wait(p, back_pair, asend.at[pl.ds(3, 1)], arecv.at[pl.ds(3, 1)])
    own_back.wait()
    own[4].wait()

    def norm_backward(t, carry):
        at = pl.ds(pl.multiple_of(t * 32, 32), 32)
        unit = unit_ref[at, :]
        inv_std = std_ref[at, 0:1]
        grad_normed = gnm_ref[pl.ds(t * 4, 4)].astype(F32).reshape(32, D)
        grad_hat = grad_normed * (1.0 + rows_ref[2:3, :])
        grad_resid = gout_ref[at, :].astype(F32) + inv_std * (
            grad_hat
            - jnp.mean(grad_hat, axis=-1, keepdims=True)
            - unit * jnp.mean(grad_hat * unit, axis=-1, keepdims=True)
        )
        hidden_out[at, :] = grad_resid.astype(BF)
        proj_ref[at, :] = (rows_ref[0:1, :] * grad_resid).astype(BF)
        return carry

    lax.fori_loop(0, 8, norm_backward, 0, unroll=2)
    ro.start(lambda at: attended_ref[:, at], proj_ref)

    def attend_grad(t, carry):
        at = pl.ds(pl.multiple_of(t * 384, 128), 384)
        gatt_ref[:, at] = nt(proj_ref[...], wout_ref[at, :]).astype(BF)
        return carry

    lax.fori_loop(0, 3, attend_grad, 0, unroll=True)
    ro.first(proj_ref)
    spatial_out[...] = jnp.zeros_like(spatial_out)

    def spatial_back(h, carry):
        backward_head(flat_loader(spatial_ref, gatt_ref), adder(spatial_out), h, None)
        return carry

    lax.fori_loop(0, HEADS // 2, spatial_back, 0, unroll=2)
    rq.second()
    lax.fori_loop(HEADS // 2, HEADS, spatial_back, 0, unroll=2)
    rq.third()
    ro.second()
    ro.third()
    rq.last(w_qkv_out)
    ro.last(w_out_out)
    for c in sent:
        c.wait_send()
    rq.drain()
    ro.drain()


def whole_call(*args):
    any_space = pl.BlockSpec(memory_space=pl.ANY)
    vmem = pl.BlockSpec(memory_space=pltpu.VMEM)
    return pl.pallas_call(
        whole_kernel,
        out_shape=(
            pltpu.VMEM((256, D), BF),
            pltpu.VMEM((256, 3 * D), BF),
            pltpu.VMEM((ROWS, 36), F32),
            pltpu.VMEM((ROWS, 108), F32),
        ),
        in_specs=[any_space] * 7 + [vmem] * 2,
        out_specs=[vmem] * 4,
        scratch_shapes=reducer_scratch(3 * D, QX)
        + reducer_scratch(D, OX)
        + [
            pltpu.VMEM((DP, 18, 8, 4 * D), BF),
            pltpu.VMEM((SEQ, 8, 3 * D), BF),
            pltpu.VMEM((SEQ, 8, D), BF),
            pltpu.VMEM((256, 3 * D), BF),
            pltpu.VMEM((256, D), BF),
            pltpu.VMEM((256, D), BF),
            pltpu.VMEM((256, D), BF),
            pltpu.VMEM((256, 3 * D), BF),
            pltpu.VMEM((D, D), BF),
            pltpu.VMEM((256, D), F32),
            pltpu.VMEM((256, 128), F32),
            pltpu.VMEM((SEQ, 8, D), BF),
            pltpu.VMEM((SEQ, 8, D), BF),
            pltpu.VMEM((256, 256), F32),
            pltpu.VMEM((D, 256), F32),
            pltpu.VMEM((SEQ, 8, D), BF),
            pltpu.VMEM((SEQ, 8, D), BF),
            pltpu.VMEM((256, D), BF),
            pltpu.VMEM((256, D), BF),
            pltpu.VMEM((3, D), F32),
            pltpu.SemaphoreType.DMA((9,)),
            pltpu.SemaphoreType.DMA((4,)),
            pltpu.SemaphoreType.DMA((4,)),
            pltpu.SemaphoreType.DMA((76,)),
            pltpu.SemaphoreType.DMA((76,)),
        ],
        compiler_params=pltpu.CompilerParams(
            collective_id=0, has_side_effects=True, vmem_limit_bytes=VMEM_LIMIT
        ),
        name="whole",
    )(*args)


def per_device(
    hidden_in,
    qkv_spatial,
    qkv_temporal,
    grad_out,
    grad_temporal,
    gate_spatial,
    modulation,
    w_out_spatial,
    w_qkv_temporal,
):
    grad_hidden, grad_qkv_s, grad_w_out, grad_w_qkv = whole_call(
        w_out_spatial.reshape(18, 8, D),
        w_qkv_temporal.reshape(18, 8, 3 * D),
        qkv_temporal.reshape(SEQ, 8, 3 * D),
        grad_temporal.reshape(SEQ, 8, D),
        qkv_spatial.reshape(256, 3 * D),
        hidden_in.reshape(256, D),
        grad_out.reshape(256, D),
        gate_spatial,
        modulation.reshape(2, D),
    )
    return (
        grad_hidden.reshape(hidden_in.shape),
        grad_qkv_s.reshape(qkv_spatial.shape),
        grad_w_out,
        grad_w_qkv,
    )


def solution(mesh):
    in_specs = (
        P("dp", "seq", None, None),
        P("dp", "seq", None, None),
        P("dp", "seq", None, None),
        P("dp", "seq", None, None),
        P("dp", "seq", None, None),
        P("dp", None),
        P("dp", None, None),
        P("dp", None),
        P("dp", None),
    )
    out_specs = (
        P("dp", "seq", None, None),
        P("dp", "seq", None, None),
        P("dp", "seq"),
        P("dp", "seq"),
    )
    return jax.shard_map(
        per_device, mesh=mesh, in_specs=in_specs, out_specs=out_specs, check_vma=False
    )
```

```python
import functools
import math

import jax
import jax.numpy as jnp
from jax import lax
from jax.experimental import pallas as pl
from jax.experimental.pallas import tpu as pltpu
from jax.sharding import PartitionSpec as P

HEADS = 16
D = 1152
SEQ = 32
DP = 8
EPSILON = 1e-06
VMEM_LIMIT = 56 * 1024 * 1024
BF = jnp.bfloat16
F32 = jnp.float32


SCALE = 1.0 / math.sqrt(D // HEADS)
LOG2E = math.log2(math.e)


def nt(a, b):
    return lax.dot_general(a, b, (((1,), (1,)), ((), ())), preferred_element_type=F32)


def tn(a, b):
    return lax.dot_general(a, b, (((0,), (0,)), ((), ())), preferred_element_type=F32)


def nn(a, b):
    return jnp.dot(a, b, preferred_element_type=F32)


def window(h):
    chunk = jnp.minimum(h * 9 // 16, 7)
    lane = lax.broadcasted_iota(jnp.int32, (1, 256), 1) + chunk * 128 - h * 72
    keep = jnp.where(jnp.logical_and(lane >= 0, lane < 72), 1.0, 0.0).astype(BF)
    return chunk * 128, keep


def head_probs(q, k, bias):
    s = nt(q, k)
    if bias is not None:
        s = s + bias
    top = jnp.max(s, axis=-1, keepdims=True)
    e = jnp.exp2((s - top) * (SCALE * LOG2E))
    return e * (1.0 / jnp.sum(e, axis=-1, keepdims=True))


def forward_head(load, add, h):
    c, keep = window(h)
    p = head_probs(load(0, c) * keep, load(1, c), None)
    add(0, c, nn(p.astype(BF), load(2, c) * keep))


def backward_head(load, add, h, bias):
    c, keep = window(h)
    q, k, v, g = load(0, c), load(1, c), load(2, c), load(3, c)
    qm, km, gm = q * keep, k * keep, g * keep
    p = head_probs(qm, k, bias)
    pb = p.astype(BF)
    dp = nt(gm, v)
    delta = jnp.sum(dp * p, axis=-1, keepdims=True)
    ds = (p * ((dp - delta) * SCALE)).astype(BF)
    add(2, c, tn(pb, gm))
    add(0, c, nn(ds, km))
    add(1, c, tn(ds, qm))


def columns(j, c):
    return pl.ds(pl.multiple_of(j * D + c, 128), 256)


def adder(ref):
    def add(j, c, value):
        at = columns(j, c)
        ref[:, at] = ref[:, at] + value.astype(BF)

    return add


def flat_loader(qkv_ref, g_ref):
    def load(j, c):
        return qkv_ref[:, columns(j, c)] if j < 3 else g_ref[:, columns(0, c)]

    return load


def block_loader(qkv_ref, g_ref):
    def load(j, c):
        x = qkv_ref[:, :, columns(j, c)] if j < 3 else g_ref[:, :, columns(0, c)]
        return x.reshape(256, 256)

    return load


def position():
    s = lax.axis_index("seq")
    d = lax.axis_index("dp")
    return dict(s=s, d=d, core=s % 2, zlo=(s // 2) % 4, x=s // 8, y=d % 4, zhi=d // 4)


def rcopy(src, dst, ssem, rsem, ps, pd):
    return pltpu.make_async_remote_copy(
        src_ref=src,
        dst_ref=dst,
        send_sem=ssem,
        recv_sem=rsem,
        device_id={"seq": ps, "dp": pd},
        device_id_type=pl.DeviceIdType.MESH,
    )


def greet(ps, pd):
    pl.semaphore_signal(
        pltpu.get_barrier_semaphore(),
        inc=1,
        device_id={"seq": ps, "dp": pd},
        device_id_type=pl.DeviceIdType.MESH,
    )


def a2a_start(p, pairs, ssems, rsems):
    def body(k, carry):
        peer = (p["s"] + k) % SEQ
        for i, (src, dst) in enumerate(pairs):
            rcopy(src.at[peer], dst.at[p["s"]], ssems.at[i], rsems.at[i], peer, p["d"]).start()
        return carry

    lax.fori_loop(1, SEQ, body, 0)


def a2a_wait(p, pairs, ssems, rsems):
    for i, (src, dst) in enumerate(pairs):
        part = pl.ds(0, SEQ - 1)
        rcopy(
            src.at[part], dst.at[part], ssems.at[i], rsems.at[i], (p["s"] + 1) % SEQ, p["d"]
        ).wait()


def greet_seq(p):
    def body(k, carry):
        greet((p["s"] + k) % SEQ, p["d"])
        return carry

    lax.fori_loop(1, SEQ, body, 0)


ROWS = 144
QX, OX = 8 * 128, 3 * 128
CZ = 256
LANES = 128


def x_start(xx):
    q = xx * 27 // 4
    return q - xx // 3, xx * 2


def z_start(ss):
    xx = ss // 8
    q0, o0 = x_start(xx)
    q = ss * 27 // 32
    q = q - ss // 31
    o = ss * 9 // 32
    o = jnp.minimum(o, o0 + 1)
    return q - q0, o - o0


class Reducer:
    def __init__(self, p, which, width, cover, bufs, sems):
        self.p, self.which, self.width, self.cover = p, which, width, cover
        self.size = width // SEQ
        self.lhs_t, self.mine, self.from_core, self.b1 = bufs[:4]
        self.part, self.b2, self.total, self.zout, self.zbuf = bufs[4:]
        self.pieces = [
            (j, j * cover, min(cover, width - j * cover)) for j in range(-(-width // cover))
        ]
        self.csend, self.crecv, self.s1send, self.s1recv = sems[:4]
        self.s2send, self.s2recv, self.zsend, self.zrecv = sems[4:]
        y, x, s = p["y"], p["x"], p["s"]
        self.order = [(y + k) % 4 for k in (1, 2, 3, 0)]
        self.y_to = [p["zhi"] * 4 + r for r in self.order[:3]]
        self.xs = [(x + k) % 4 for k in (1, 2, 3)]
        self.x_to = [xx * 8 + s % 8 for xx in self.xs]

    def cols(self, xx, t=0, size=None):
        first = x_start(xx)[self.which] * 128
        return pl.ds(pl.multiple_of(first + t, 128), self.cover if size is None else size)

    def core_copy(self, i):
        r = self.order[i]
        p = self.p
        return rcopy(
            self.mine.at[r],
            self.from_core.at[r],
            self.csend.at[i],
            self.crecv.at[i],
            p["s"] + 1 - 2 * p["core"],
            p["d"],
        )

    def first_y(self, i):
        return [
            rcopy(
                self.mine.at[self.order[i], :, pl.ds(at, size)],
                self.b1.at[i * 4 + j, :, pl.ds(0, size)],
                self.s1send.at[i * 4 + j],
                self.s1recv.at[i * 4 + j],
                self.p["s"],
                self.y_to[i],
            )
            for j, at, size in self.pieces
        ]

    def first_x(self, k, i):
        r = self.order[i]
        return rcopy(
            self.mine.at[r, :, self.cols(self.xs[k])],
            self.b1.at[k * 4 + r],
            self.s1send.at[k * 4 + i],
            self.s1recv.at[k * 4 + i],
            self.x_to[k],
            self.p["d"],
        )

    def second_x(self, k):
        return rcopy(
            self.mine.at[self.p["y"], :, self.cols(self.xs[k])],
            self.b2.at[k],
            self.s2send.at[k],
            self.s2recv.at[k],
            self.x_to[k],
            self.p["d"],
        )

    def second_y(self, i):
        return rcopy(
            self.part.at[self.order[i]],
            self.b2.at[i],
            self.s2send.at[i],
            self.s2recv.at[i],
            self.p["s"],
            self.y_to[i],
        )

    def z_target(self, i):
        p = self.p
        ss = p["x"] * 8 + i
        pd = p["core"] * 4 + p["y"]
        z_me = p["zhi"] * 4 + p["zlo"]
        return ss, pd, self.zout.at[i], z_me

    def z_copy(self, i):
        ss, pd, src, z_me = self.z_target(i)
        return rcopy(src, self.zbuf.at[z_me], self.zsend.at[i], self.zrecv.at[z_me], ss, pd)

    def z_local(self, i):
        ss, pd, src, z_me = self.z_target(i)
        return pltpu.make_async_copy(src, self.zbuf.at[z_me], self.zrecv.at[z_me])

    def own_product(self, r, rhs_ref):
        block = self.p["core"] * 4 + r
        lhs = self.lhs_t[pl.ds(pl.multiple_of(block * ROWS, 16), ROWS), :]
        step = self.width // 9

        def body(t, carry):
            at = pl.ds(pl.multiple_of(t * step, 128), step)
            value = nn(lhs, rhs_ref[:, at]) * GRAD_SCALE
            self.mine[r, :, at] = (value + self.from_core[r, :, at].astype(F32)).astype(BF)
            return carry

        lax.fori_loop(0, 9, body, 0, unroll=3)

    def start(self, load_lhs, rhs_ref):
        def turn(t, carry):
            at = pl.ds(pl.multiple_of(t * 128, 128), 128)
            self.lhs_t[at, :] = load_lhs(at).T
            return carry

        lax.fori_loop(0, 9, turn, 0, unroll=3)
        half = pl.ds(pl.multiple_of((1 - self.p["core"]) * 4 * ROWS, 16), 4 * ROWS)
        step = self.width // 9

        def body(t, carry):
            at = pl.ds(pl.multiple_of(t * step, 128), step)
            value = (nn(self.lhs_t[half, :], rhs_ref[:, at]) * GRAD_SCALE).astype(BF)
            self.mine[:, :, at] = value.reshape(4, ROWS, step)
            return carry

        lax.fori_loop(0, 9, body, 0, unroll=3)
        for i in range(4):
            self.core_copy(i).start()

    def first(self, rhs_ref):
        core = self.p["core"]
        for i, r in enumerate(self.order):
            self.core_copy(i).wait()
            self.own_product(r, rhs_ref)

            if i < 3:

                @pl.when(core == 0)
                def _():
                    for c in self.first_y(i):
                        c.start()

            @pl.when(core == 1)
            def _():
                for k in range(3):
                    self.first_x(k, i).start()

    def second(self):
        p = self.p
        y = p["y"]

        @pl.when(p["core"] == 0)
        def _():
            for i in range(3):
                for c in self.first_y(i):
                    c.wait_recv()
            n = self.cover // 128

            def body(t, carry):
                at = pl.ds(pl.multiple_of(t * 128, 128), 128)
                there = pl.ds(pl.multiple_of(t % n * 128, 128), 128)
                total = self.mine[y, :, at].astype(F32)
                for i in range(3):
                    total = total + self.b1[i * 4 + t // n, :, there].astype(F32)
                self.mine[y, :, at] = total.astype(BF)
                return carry

            lax.fori_loop(0, self.width // 128, body, 0, unroll=9)
            for k in range(3):
                self.second_x(k).start()

        @pl.when(p["core"] == 1)
        def _():
            for i, r in enumerate(self.order):
                for k in range(3):
                    self.first_x(k, i).wait_recv()

                def body(t, carry):
                    at = pl.ds(pl.multiple_of(t * 128, 128), 128)
                    total = self.mine[r, :, self.cols(p["x"], t * 128, 128)].astype(F32)
                    for k in range(3):
                        total = total + self.b1[k * 4 + r, :, at].astype(F32)
                    self.part[r, :, at] = total.astype(BF)
                    return carry

                lax.fori_loop(0, self.cover // 128, body, 0, unroll=True)
                if i < 3:
                    self.second_y(i).start()

    def third(self):
        p = self.p
        y, x, core = p["y"], p["x"], p["core"]

        def finish(load):
            def body(t, carry):
                at = pl.ds(pl.multiple_of(t * 128, 128), 128)
                total = load(t).astype(F32)
                for k in range(3):
                    total = total + self.b2[k, :, at].astype(F32)
                self.total[:, at] = total.astype(BF)
                return carry

            lax.fori_loop(0, self.cover // 128, body, 0, unroll=True)

        @pl.when(core == 0)
        def _():
            for k in range(3):
                self.second_x(k).wait_recv()
            finish(lambda t: self.mine[y, :, self.cols(x, t * 128, 128)])

        @pl.when(core == 1)
        def _():
            for i in range(3):
                self.second_y(i).wait_recv()
            finish(lambda t: self.part[y, :, pl.ds(pl.multiple_of(t * 128, 128), 128)])

        def pack(i, carry):
            ss = x * 8 + i
            at = z_start(ss)[self.which]
            skip = ss * self.size - (x_start(x)[self.which] + at) * 128
            value = self.total[:, pl.ds(pl.multiple_of(at * 128, 128), CZ)].astype(F32)
            self.zout[i] = pltpu.roll(value, (CZ - skip) % CZ, 1)[:, :LANES].astype(BF)
            return carry

        lax.fori_loop(0, 8, pack, 0, unroll=4)
        for i in range(8):
            ss, pd, _, _ = self.z_target(i)
            is_me = jnp.logical_and(ss == p["s"], pd == p["d"])

            @pl.when(jnp.logical_not(is_me))
            def _():
                self.z_copy(i).start()

            @pl.when(is_me)
            def _():
                self.z_local(i).start()

    def last(self, out_ref):
        for z in range(8):
            pltpu.make_async_copy(self.zbuf.at[z], self.zbuf.at[z], self.zrecv.at[z]).wait()
        total = self.zbuf[0].astype(F32)
        for z in range(1, 8):
            total = total + self.zbuf[z].astype(F32)
        out_ref[...] = total[:, : self.size]

    def drain(self):
        p = self.p

        @pl.when(p["core"] == 0)
        def _():
            for i in range(3):
                for c in self.first_y(i):
                    c.wait_send()
                self.second_x(i).wait_send()

        @pl.when(p["core"] == 1)
        def _():
            for k in range(3):
                for i in range(4):
                    self.first_x(k, i).wait_send()
                self.second_y(k).wait_send()

        for i in range(8):
            ss, pd, _, _ = self.z_target(i)

            @pl.when(jnp.logical_or(ss != p["s"], pd != p["d"]))
            def _():
                self.z_copy(i).wait_send()


def reducer_scratch(width, cover):
    bufs = [
        pltpu.VMEM((D, 256), BF),
        pltpu.VMEM((4, ROWS, width), BF),
        pltpu.VMEM((4, ROWS, width), BF),
        pltpu.VMEM((12, ROWS, cover), BF),
        pltpu.VMEM((4, ROWS, cover), BF),
        pltpu.VMEM((3, ROWS, cover), BF),
        pltpu.VMEM((ROWS, cover), BF),
        pltpu.VMEM((8, ROWS, LANES), BF),
        pltpu.VMEM((8, ROWS, LANES), BF),
    ]
    sems = [pltpu.SemaphoreType.DMA((n,)) for n in (4, 4, 12, 12, 3, 3, 8, 8)]
    return bufs + sems


GRAD_SCALE = 1.0 / math.sqrt(DP * SEQ * 256)


SPLIT = 1536
WA, WB = SPLIT // 4, (4 * D - SPLIT) // 4


def whole_kernel(
    w_out_ref,
    w_qkv_ref,
    qkv_ref,
    g_ref,
    spatial_hbm,
    hidden_hbm,
    gout_hbm,
    gate_ref,
    modulation_ref,
    hidden_out,
    spatial_out,
    w_out_out,
    w_qkv_out,
    *scratch,
):
    (
        wall_ref,
        qkvm_ref,
        gm_ref,
        spatial_ref,
        hidden_ref,
        gout_ref,
        attended_ref,
        gqkv_ref,
        wout_ref,
        unit_ref,
        std_ref,
        normed_ref,
        normedm_ref,
        bias_ref,
        gnt_ref,
        gn_ref,
        gnm_ref,
        proj_ref,
        gatt_ref,
        rows_ref,
        lsem,
        asend,
        arecv,
        wsend,
        wrecv,
    ) = scratch[34:]
    p = position()
    s, d, x, y, core, zhi = p["s"], p["d"], p["x"], p["y"], p["core"], p["zhi"]
    own = [
        pltpu.make_async_copy(w_out_ref, wall_ref.at[d, :, :, pl.ds(0, D)], lsem.at[0]),
        pltpu.make_async_copy(w_qkv_ref, wall_ref.at[d, :, :, pl.ds(D, 3 * D)], lsem.at[4]),
        pltpu.make_async_copy(spatial_hbm, spatial_ref, lsem.at[5]),
        pltpu.make_async_copy(hidden_hbm, hidden_ref, lsem.at[6]),
        pltpu.make_async_copy(gout_hbm, gout_ref, lsem.at[7]),
        pltpu.make_async_copy(qkv_ref.at[s], qkvm_ref.at[s], lsem.at[1]),
        pltpu.make_async_copy(g_ref.at[s], gm_ref.at[s], lsem.at[2]),
    ]
    for c in own:
        c.start()
    greet_seq(p)
    far = (d + 4) % DP
    y_to = [zhi * 4 + (y + k) % 4 for k in (1, 2, 3)]
    y_from = [zhi * 4 + (y + 4 - k) % 4 for k in (1, 2, 3)]
    y_far = [(1 - zhi) * 4 + (y + 4 - k) % 4 for k in (1, 2, 3)]
    x_to = [((x + k) % 4) * 8 + s % 8 for k in (1, 2, 3)]
    x_from = [(x + 4 - k) % 4 for k in (1, 2, 3)]
    sibling = s + 1 - 2 * core
    for peer in y_to:
        greet(s, peer)
    for i in range(8):
        greet(x * 8 + i, (1 - zhi) * 4 + y)
    pl.semaphore_wait(pltpu.get_barrier_semaphore(), SEQ - 1 + 3 + 8)
    own[0].wait()
    own[1].wait()

    rows = pl.ds(core * 9, 9)
    other_rows = pl.ds((1 - core) * 9, 9)

    def col_a(xx):
        return pl.ds(pl.multiple_of(xx * WA, 128), WA)

    def col_b(xx):
        return pl.ds(pl.multiple_of(SPLIT + xx * WB, 128), WB)

    all_b = pl.ds(SPLIT, 4 * WB)
    sent = []
    expected = []

    def send(dd, cols, sem, ps, pd):
        ref = wall_ref.at[dd, rows, :, cols]
        c = rcopy(ref, ref, wsend.at[sem], wrecv.at[sem], ps, pd)
        c.start()
        sent.append(c)

    def arrived(dd, cols, sem, which=None):
        ref = wall_ref.at[dd, rows if which is None else which, :, cols]
        rcopy(ref, ref, wsend.at[sem], wrecv.at[sem], s, far).wait_recv()

    def hand_on(dd, cols, sem):
        send(dd, cols, sem, sibling, d)
        expected.append((dd, cols, sem))

    send(d, col_a(x), 0, s, far)
    for k in range(3):
        send(d, col_a(x), 1 + k, s, y_to[k])
    send(d, col_b(x), 56, s, far)
    for k in range(3):
        send(d, all_b, 60 + k, s, y_to[k])
    pairs = [(qkv_ref, qkvm_ref), (g_ref, gm_ref)]
    a2a_start(p, pairs, asend, arecv)

    arrived(far, col_a(x), 0)
    for k in range(3):
        send(far, col_a(x), 4 + k, s, y_to[k])
    arrived(far, col_b(x), 56)
    for k in range(3):
        send(far, col_b(x), 57 + k, x_to[k], d)
    hand_on(far, col_b(x), 66)

    rows_ref[0:1, :] = gate_ref[...].astype(F32)
    rows_ref[1:3, :] = modulation_ref[...].astype(F32)
    attended_ref[...] = jnp.zeros_like(attended_ref)
    own[2].wait()

    def spatial(h, carry):
        forward_head(flat_loader(spatial_ref, None), adder(attended_ref), h)
        return carry

    lax.fori_loop(0, HEADS, spatial, 0, unroll=2)

    sources = [far] + y_from + y_far
    for j, dd in enumerate(sources):
        if j:
            arrived(dd, col_a(x), j)
        for k in range(3):
            send(dd, col_a(x), 7 + j * 3 + k, x_to[k], d)
        hand_on(dd, col_a(x), 28 + j)
    for k in range(3):
        arrived(far, col_b(x_from[k]), 57 + k)
    for k in range(3):
        send(far, all_b, 63 + k, s, y_to[k])
    for k in range(3):
        hand_on(far, col_b(x_from[k]), 67 + k)
    for j, dd in enumerate(sources):
        for k in range(3):
            arrived(dd, col_a(x_from[k]), 7 + j * 3 + k)
            hand_on(dd, col_a(x_from[k]), 35 + j * 3 + k)

    at = lax.broadcasted_iota(jnp.int32, (256, 256), 0) % 8
    to = lax.broadcasted_iota(jnp.int32, (256, 256), 1) % 8
    bias_ref[...] = jnp.where(at == to, 0.0, -1e30)
    gqkv_ref[...] = jnp.zeros_like(gqkv_ref)

    own[3].wait()
    for dd, cols, sem in expected:
        if sem < 66:
            arrived(dd, cols, sem, other_rows)

    def assemble(dd, carry):
        at = pl.ds(pl.multiple_of(dd * ROWS, 16), ROWS)
        wout_ref[at, :] = wall_ref[dd, :, :, :D].reshape(ROWS, D)
        return carry

    lax.fori_loop(0, DP, assemble, 0)

    def project(t, carry):
        at = pl.ds(pl.multiple_of(t * 384, 128), 384)
        unit_ref[:, at] = hidden_ref[:, at].astype(F32) + rows_ref[0:1, at] * nn(
            attended_ref[...], wout_ref[:, at]
        )
        return carry

    lax.fori_loop(0, 3, project, 0, unroll=True)

    def normalise(t, carry):
        at = pl.ds(pl.multiple_of(t * 32, 32), 32)
        residual = unit_ref[at, :]
        centered = residual - jnp.mean(residual, axis=-1, keepdims=True)
        inv_std = lax.rsqrt(jnp.mean(centered * centered, axis=-1, keepdims=True) + EPSILON)
        unit = centered * inv_std
        unit_ref[at, :] = unit
        std_ref[at, :] = jnp.broadcast_to(inv_std, (32, 128))
        normed = unit * (1.0 + rows_ref[2:3, :]) + rows_ref[1:2, :]
        normed_ref[pl.ds(t * 4, 4)] = normed.reshape(4, 8, D).astype(BF)
        return carry

    lax.fori_loop(0, 8, normalise, 0, unroll=2)
    own_normed = pltpu.make_async_copy(normed_ref.at[s], normedm_ref.at[s], lsem.at[3])
    own_normed.start()
    normed_pair = [(normed_ref, normedm_ref)]
    a2a_start(p, normed_pair, asend.at[pl.ds(2, 1)], arecv.at[pl.ds(2, 1)])

    for k in range(3):
        arrived(y_from[k], all_b, 60 + k)
        hand_on(y_from[k], all_b, 70 + k)
    for k in range(3):
        arrived(y_far[k], all_b, 63 + k)
        hand_on(y_far[k], all_b, 73 + k)
    a2a_wait(p, pairs, asend, arecv)
    own[5].wait()
    own[6].wait()

    def temporal(h, carry):
        backward_head(block_loader(qkvm_ref, gm_ref), adder(gqkv_ref), h, bias_ref[...])
        return carry

    lax.fori_loop(0, HEADS, temporal, 0, unroll=4)

    for dd, cols, sem in expected:
        if sem >= 66:
            arrived(dd, cols, sem, other_rows)

    def back_project(half, carry):
        at = pl.ds(pl.multiple_of(half * 4 * ROWS, 16), 4 * ROWS)
        weights = wall_ref[pl.ds(half * 4, 4), :, :, D:].reshape(4 * ROWS, 3 * D)
        gnt_ref[at, :] = nt(weights, gqkv_ref[...])
        return carry

    lax.fori_loop(0, 2, back_project, 0)

    def turn(t, carry):
        at = pl.ds(pl.multiple_of(t * 128, 128), 128)
        gn_ref[:, :, at] = gnt_ref[at, :].T.reshape(SEQ, 8, 128).astype(BF)
        return carry

    lax.fori_loop(0, 9, turn, 0, unroll=3)
    own_back = pltpu.make_async_copy(gn_ref.at[s], gnm_ref.at[s], lsem.at[8])
    own_back.start()
    back_pair = [(gn_ref, gnm_ref)]
    a2a_start(p, back_pair, asend.at[pl.ds(3, 1)], arecv.at[pl.ds(3, 1)])
    a2a_wait(p, normed_pair, asend.at[pl.ds(2, 1)], arecv.at[pl.ds(2, 1)])
    own_normed.wait()

    rq = Reducer(p, 0, 3 * D, QX, scratch[0:9], scratch[9:17])
    ro = Reducer(p, 1, D, OX, scratch[17:26], scratch[26:34])
    rq.start(lambda at: normedm_ref[:, :, at].reshape(256, 128), gqkv_ref)
    rq.first(gqkv_ref)

    a2a_wait(p, back_pair, asend.at[pl.ds(3, 1)], arecv.at[pl.ds(3, 1)])
    own_back.wait()
    own[4].wait()

    def norm_backward(t, carry):
        at = pl.ds(pl.multiple_of(t * 32, 32), 32)
        unit = unit_ref[at, :]
        inv_std = std_ref[at, 0:1]
        grad_normed = gnm_ref[pl.ds(t * 4, 4)].astype(F32).reshape(32, D)
        grad_hat = grad_normed * (1.0 + rows_ref[2:3, :])
        grad_resid = gout_ref[at, :].astype(F32) + inv_std * (
            grad_hat
            - jnp.mean(grad_hat, axis=-1, keepdims=True)
            - unit * jnp.mean(grad_hat * unit, axis=-1, keepdims=True)
        )
        hidden_out[at, :] = grad_resid.astype(BF)
        proj_ref[at, :] = (rows_ref[0:1, :] * grad_resid).astype(BF)
        return carry

    lax.fori_loop(0, 8, norm_backward, 0, unroll=2)
    ro.start(lambda at: attended_ref[:, at], proj_ref)

    def attend_grad(t, carry):
        at = pl.ds(pl.multiple_of(t * 384, 128), 384)
        gatt_ref[:, at] = nt(proj_ref[...], wout_ref[at, :]).astype(BF)
        return carry

    lax.fori_loop(0, 3, attend_grad, 0, unroll=True)
    ro.first(proj_ref)
    spatial_out[...] = jnp.zeros_like(spatial_out)

    def spatial_back(h, carry):
        backward_head(flat_loader(spatial_ref, gatt_ref), adder(spatial_out), h, None)
        return carry

    lax.fori_loop(0, HEADS // 2, spatial_back, 0, unroll=2)
    rq.second()
    lax.fori_loop(HEADS // 2, HEADS, spatial_back, 0, unroll=2)
    rq.third()
    ro.second()
    ro.third()
    rq.last(w_qkv_out)
    ro.last(w_out_out)
    for c in sent:
        c.wait_send()
    rq.drain()
    ro.drain()


def whole_call(*args):
    any_space = pl.BlockSpec(memory_space=pl.ANY)
    vmem = pl.BlockSpec(memory_space=pltpu.VMEM)
    return pl.pallas_call(
        whole_kernel,
        out_shape=(
            pltpu.VMEM((256, D), BF),
            pltpu.VMEM((256, 3 * D), BF),
            pltpu.VMEM((ROWS, 36), F32),
            pltpu.VMEM((ROWS, 108), F32),
        ),
        in_specs=[any_space] * 7 + [vmem] * 2,
        out_specs=[vmem] * 4,
        scratch_shapes=reducer_scratch(3 * D, QX)
        + reducer_scratch(D, OX)
        + [
            pltpu.VMEM((DP, 18, 8, 4 * D), BF),
            pltpu.VMEM((SEQ, 8, 3 * D), BF),
            pltpu.VMEM((SEQ, 8, D), BF),
            pltpu.VMEM((256, 3 * D), BF),
            pltpu.VMEM((256, D), BF),
            pltpu.VMEM((256, D), BF),
            pltpu.VMEM((256, D), BF),
            pltpu.VMEM((256, 3 * D), BF),
            pltpu.VMEM((D, D), BF),
            pltpu.VMEM((256, D), F32),
            pltpu.VMEM((256, 128), F32),
            pltpu.VMEM((SEQ, 8, D), BF),
            pltpu.VMEM((SEQ, 8, D), BF),
            pltpu.VMEM((256, 256), F32),
            pltpu.VMEM((D, 256), F32),
            pltpu.VMEM((SEQ, 8, D), BF),
            pltpu.VMEM((SEQ, 8, D), BF),
            pltpu.VMEM((256, D), BF),
            pltpu.VMEM((256, D), BF),
            pltpu.VMEM((3, D), F32),
            pltpu.SemaphoreType.DMA((9,)),
            pltpu.SemaphoreType.DMA((4,)),
            pltpu.SemaphoreType.DMA((4,)),
            pltpu.SemaphoreType.DMA((76,)),
            pltpu.SemaphoreType.DMA((76,)),
        ],
        compiler_params=pltpu.CompilerParams(
            collective_id=0, has_side_effects=True, vmem_limit_bytes=VMEM_LIMIT
        ),
        name="whole",
    )(*args)


def per_device(
    hidden_in,
    qkv_spatial,
    qkv_temporal,
    grad_out,
    grad_temporal,
    gate_spatial,
    modulation,
    w_out_spatial,
    w_qkv_temporal,
):
    grad_hidden, grad_qkv_s, grad_w_out, grad_w_qkv = whole_call(
        w_out_spatial.reshape(18, 8, D),
        w_qkv_temporal.reshape(18, 8, 3 * D),
        qkv_temporal.reshape(SEQ, 8, 3 * D),
        grad_temporal.reshape(SEQ, 8, D),
        qkv_spatial.reshape(256, 3 * D),
        hidden_in.reshape(256, D),
        grad_out.reshape(256, D),
        gate_spatial,
        modulation.reshape(2, D),
    )
    return (
        grad_hidden.reshape(hidden_in.shape),
        grad_qkv_s.reshape(qkv_spatial.shape),
        grad_w_out,
        grad_w_qkv,
    )


def solution(mesh):
    in_specs = (
        P("dp", "seq", None, None),
        P("dp", "seq", None, None),
        P("dp", "seq", None, None),
        P("dp", "seq", None, None),
        P("dp", "seq", None, None),
        P("dp", None),
        P("dp", None, None),
        P("dp", None),
        P("dp", None),
    )
    out_specs = (
        P("dp", "seq", None, None),
        P("dp", "seq", None, None),
        P("dp", "seq"),
        P("dp", "seq"),
    )
    return jax.shard_map(
        per_device, mesh=mesh, in_specs=in_specs, out_specs=out_specs, check_vma=False
    )
```
